32 devices in a mesh: dp: 4 (over z), expert: 8 (over y, x, core).
Axes of the slice: x: 2, y: 2, z: 4, core: 2. Of those that a mesh axis runs over, the one named last changes fastest.
Arguments:
- tokens: bfloat16 [4096, 2048], P(('dp', 'expert')), may hold values from -6 to 6
- grad_out: bfloat16 [4096, 2048], P(('dp', 'expert')), may hold values from -0.59765625 to 0.59765625
- expert_ids: int32 [4096, 2], P(('dp', 'expert')), may hold values from 0 to 7, all different within a row; in each aligned block of 128 rows (0 to 127, 128 to 255, ...) at most 48 rows name the same one
- gates: float32 [4096, 2], P(('dp', 'expert')), may hold values from 0.05 to 1
- gate_weight: bfloat16 [8, 2048, 768], P('expert'), may hold values from -0.125 to 0.125
- up_weight: bfloat16 [8, 2048, 768], P('expert'), may hold values from -0.125 to 0.125
- down_weight: bfloat16 [8, 768, 2048], P('expert'), may hold values from -0.21875 to 0.21875
Outputs:
- grad_tokens: bfloat16 [4096, 2048], P(('dp', 'expert'))
- grad_gates: bfloat16 [4096, 2], P(('dp', 'expert'))
- grad_gate_weight: float32 [8, 2048, 768], P('expert', 'dp')
- grad_up_weight: float32 [8, 2048, 768], P('expert', 'dp')
- grad_down_weight: float32 [8, 768, 2048], P('expert', 'dp')
The draws below stay inside these ranges and needn't reach their ends.
Inputs may be any that keep to these rules, and one draw needn't show every extreme that they name: `expert_ids`: each row names 2 different experts. Within an aligned block of 128 rows (the rows of one device) no expert is named more than 48 times; in some such blocks one expert is named exactly 48 times.
All inputs are finite; a program needn't handle non-finite values.
Results may differ from the reference program's by a relative error of at most 0.012.
Values may be sent and summed in bfloat16 or wider, within the bound.
No kernel may reach another device: no remote copies, remote signals or barrier semaphores. Data moves between devices by JAX's collectives and lax.ppermute only.
A program may use at most 128 MiB of HBM per device.

```python
import math
import jax
import jax.numpy as jnp
import numpy as np
from jax import lax

D = 2048
H = 768
TOK_DEV = 128
EXPERTS = 8
TOP = 2
CAP = 48
TOKENS = 4096
N_DP = 4
N_EXPERT = 8


def steps_of(key, dims, cuts, smallest, high):
    def one(position, shards_of):
        draws = jax.random.uniform(jax.random.fold_in(jax.random.fold_in(key, 6), position), (shards_of,), jnp.float32, smallest / len(cuts), high / len(cuts))
        return jnp.repeat(jnp.exp(draws), dims[position] // shards_of).reshape((-1,) + (1,) * (len(dims) - position - 1))

    loudness = one(*cuts[0])
    for cut in cuts[1:]:
        loudness = loudness * one(*cut)
    return loudness


def deal_out(stream_key, own, number, rows, count, top, limit, lean):
    order = jax.random.permutation(stream_key, count)
    crowded, common = portions_of(count, rows * top, limit, lean, True), portions_of(count, rows * top, limit, lean, False)
    places = jnp.arange(count)

    def named(tallies, rotation):
        used = int((tallies > 0).sum())
        fixed = max(1, used // 4)
        passed = fixed + (places - fixed + rotation * (used - fixed)) % max(1, count - fixed)
        return jnp.zeros((count,), jnp.int32).at[order[jnp.where(places < fixed, places, passed)]].set(jnp.asarray(tallies, jnp.int32))

    tallies = jnp.where(number % 4 == 0, named(crowded, number // 4), named(common, number - number // 4 - 1))
    mixed = jax.random.permutation(jax.random.fold_in(own, 3), count)
    source_of, receiver = mixed[0:count // 2 * 2:2], mixed[1:count // 2 * 2:2]
    room = jnp.minimum(tallies[source_of] - 1, limit - tallies[receiver]) // 2
    room = jnp.where((source_of == order[0]) | (receiver == order[0]) | (tallies[receiver] == 0), 0, jnp.maximum(room, 0))
    passed = jax.random.randint(jax.random.fold_in(own, 4), (count // 2,), 0, 1 << 20) % (room + 1)
    tallies = tallies.at[source_of].add(-passed).at[receiver].add(passed)
    labels = jnp.searchsorted(jnp.cumsum(tallies), jnp.arange(rows * top), side="right").astype(jnp.int32)
    table = labels.reshape(top, rows).T
    table = table[jax.random.permutation(jax.random.fold_in(own, 1), rows)]
    rotation = jax.random.randint(jax.random.fold_in(own, 2), (rows, 1), 0, top)
    return jnp.take_along_axis(table, (jnp.arange(top)[None, :] + rotation) % top, axis=1)


def portions_of(number_of, total, most, slope, full):
    weights = [(1 << 20) // math.isqrt(rank ** slope) + 1 for rank in range(1, number_of + 1)]
    largest = most if full else min(most, max(-(-total // number_of), total * weights[0] // sum(weights)))
    least = 1 if total - largest >= number_of - 1 else 0
    holding, rest = [largest] + [least] * (number_of - 1), total - largest - least * (number_of - 1)
    while rest > 0:
        candidates = [i for i in range(1, number_of) if holding[i] < largest] or [i for i in range(1, number_of) if holding[i] < most]
        mass, left = sum([weights[i] for i in candidates]), rest
        for i in candidates:
            extra = min(most - holding[i], max(1, left * weights[i] // mass), rest)
            holding[i] = holding[i] + extra
            rest = rest - extra
    return np.array(holding)


def noise(own_key, shape, spread, reach, cuts=(), held_as=jnp.bfloat16):
    drawn = spread * jax.random.normal(own_key, shape, jnp.float32)
    if cuts:
        drawn = drawn * steps_of(own_key, shape, cuts, -0.22, 0.18)
    return jnp.clip(drawn, -reach, reach).astype(held_as)


def setup_inputs(seed: int = 0) -> dict:
    keys = jax.random.split(jax.random.key(seed), 8)
    tokens = noise(keys[0], (TOKENS, D), 1.0, 6.0, ((0, 32),))
    grad_out = noise(keys[1], (TOKENS, D), 0.1, 0.59765625, ((0, 32),))
    expert_ids_keys = jax.random.split(jax.random.fold_in(keys[2], 1), TOKENS // TOK_DEV)
    expert_ids_turns = jax.random.permutation(jax.random.fold_in(keys[2], 3), TOKENS // TOK_DEV)
    expert_ids = jax.vmap(lambda own, number: deal_out(jax.random.fold_in(keys[2], 2), own, number, TOK_DEV, EXPERTS, TOP, CAP, 2))(expert_ids_keys, expert_ids_turns).reshape((TOKENS, TOP))
    gates = jnp.clip(jnp.exp(math.log(1.0) - 2.9957323 * jax.random.uniform(keys[3], (TOKENS, TOP), jnp.float32) ** steps_of(keys[3], (TOKENS, TOP), ((0, 32),), -0.2, 0.2)), 0.05, 1.0)
    gate_weight = noise(keys[4], (EXPERTS, D, H), D ** -0.5, 0.125, ((0, 8),))
    up_weight = noise(keys[5], (EXPERTS, D, H), D ** -0.5, 0.125, ((0, 8),))
    down_weight = noise(keys[6], (EXPERTS, H, D), H ** -0.5, 0.21875, ((0, 8),))
    return {"tokens": tokens, "grad_out": grad_out, "expert_ids": expert_ids, "gates": gates, "gate_weight": gate_weight, "up_weight": up_weight, "down_weight": down_weight}


def silu_parts(preact):
    sigmoid_v = jax.nn.sigmoid(preact)
    return preact * sigmoid_v, sigmoid_v * (1.0 + preact * (1.0 - sigmoid_v))


def contract_rows(left, right):
    return lax.dot_general(left, right, (((0,), (0,)), ((), ())), preferred_element_type=jnp.float32)


def contract_last(left, right):
    return lax.dot_general(left, right, (((1,), (1,)), ((), ())), preferred_element_type=jnp.float32)


def expert_rows(rows_x, rows_go, rows_gate, w_gate, w_up, w_down):
    pre_gate = jnp.dot(rows_x, w_gate, preferred_element_type=jnp.float32)
    pre_up = jnp.dot(rows_x, w_up, preferred_element_type=jnp.float32)
    activated, derivative = silu_parts(pre_gate)
    hidden = (activated * pre_up).astype(jnp.bfloat16)
    expert_out = jnp.dot(hidden, w_down, preferred_element_type=jnp.float32)
    upstream = rows_go.astype(jnp.float32)
    gate_grad = jnp.sum(expert_out * upstream, axis=1).astype(jnp.bfloat16)
    grad_expert = (rows_gate.astype(jnp.float32)[:, None] * upstream).astype(jnp.bfloat16)
    grad_hidden = contract_last(grad_expert, w_down)
    grad_pre_gate = (grad_hidden * pre_up * derivative).astype(jnp.bfloat16)
    grad_pre_up = (grad_hidden * activated).astype(jnp.bfloat16)
    grad_row = contract_last(grad_pre_gate, w_gate) + contract_last(grad_pre_up, w_up)
    return grad_row.astype(jnp.bfloat16), gate_grad, hidden, grad_expert, grad_pre_gate, grad_pre_up


def rounded(term):
    return lax.optimization_barrier(term.astype(jnp.bfloat16)).astype(jnp.float32)


def reference(tokens, grad_out, expert_ids, gates, gate_weight, up_weight, down_weight):
    group_len = TOK_DEV * N_EXPERT
    slot_rows = N_EXPERT * CAP
    model_width = tokens.shape[1]
    hidden_width = gate_weight.shape[2]
    zero_half = jnp.zeros((), jnp.bfloat16)

    def per_expert(totals, expert):
        w_gate = lax.dynamic_index_in_dim(gate_weight, expert, 0, keepdims=False)
        w_up = lax.dynamic_index_in_dim(up_weight, expert, 0, keepdims=False)
        w_down = lax.dynamic_index_in_dim(down_weight, expert, 0, keepdims=False)

        def per_group(running, group_index):
            grad_acc, gate_acc, sum_gate, sum_up, sum_down = running
            offset = (group_index * group_len).astype(jnp.int32)
            ids_group = lax.dynamic_slice_in_dim(expert_ids, offset, group_len, 0)
            gates_group = lax.dynamic_slice_in_dim(gates, offset, group_len, 0)
            tokens_group = lax.dynamic_slice_in_dim(tokens, offset, group_len, 0)
            upstream_group = lax.dynamic_slice_in_dim(grad_out, offset, group_len, 0)
            matches = ids_group == expert
            routed = jnp.any(matches, axis=1)
            picked = jnp.nonzero(routed, size=slot_rows, fill_value=0)[0].astype(jnp.int32)
            present = jnp.arange(slot_rows, dtype=jnp.int32) < jnp.sum(routed.astype(jnp.int32))
            gate_token = jnp.sum(jnp.where(matches, gates_group, 0.0), axis=1).astype(jnp.bfloat16)
            rows_x = jnp.where(present[:, None], tokens_group[picked], zero_half)
            rows_go = jnp.where(present[:, None], upstream_group[picked], zero_half)
            rows_gate = jnp.where(present, gate_token[picked], zero_half)
            grad_row, gate_grad, hidden, grad_expert, grad_pre_gate, grad_pre_up = expert_rows(
                rows_x, rows_go, rows_gate, w_gate, w_up, w_down)
            row_terms = jnp.zeros((group_len, model_width), jnp.float32).at[picked].add(grad_row.astype(jnp.float32))
            old_rows = lax.dynamic_slice_in_dim(grad_acc, offset, group_len, 0)
            grad_acc = lax.dynamic_update_slice_in_dim(grad_acc, old_rows + row_terms, offset, 0)
            token_grad = jnp.zeros((group_len,), jnp.float32).at[picked].add(gate_grad.astype(jnp.float32))
            old_gates = lax.dynamic_slice_in_dim(gate_acc, offset, group_len, 0)
            new_gates = old_gates + jnp.where(matches, token_grad[:, None], 0.0)
            gate_acc = lax.dynamic_update_slice_in_dim(gate_acc, new_gates, offset, 0)
            sum_gate = sum_gate + rounded(contract_rows(rows_x, grad_pre_gate))
            sum_up = sum_up + rounded(contract_rows(rows_x, grad_pre_up))
            sum_down = sum_down + rounded(contract_rows(hidden, grad_expert))
            return (grad_acc, gate_acc, sum_gate, sum_up, sum_down), None

        start_state = (totals[0], totals[1],
                       jnp.zeros((model_width, hidden_width), jnp.float32),
                       jnp.zeros((model_width, hidden_width), jnp.float32),
                       jnp.zeros((hidden_width, model_width), jnp.float32))
        final_state, unused = lax.scan(per_group, start_state, jnp.arange(N_DP, dtype=jnp.int32))
        return (final_state[0], final_state[1]), (final_state[2], final_state[3], final_state[4])

    start_totals = (jnp.zeros(tokens.shape, jnp.float32), jnp.zeros(gates.shape, jnp.float32))
    totals, stacked = lax.scan(per_expert, start_totals, jnp.arange(EXPERTS, dtype=jnp.int32))
    return (totals[0].astype(jnp.bfloat16), totals[1].astype(jnp.bfloat16),
            stacked[0], stacked[1], stacked[2])
```

```python
import functools

import jax
import jax.numpy as jnp
from jax import lax
from jax.experimental import pallas as pl
from jax.experimental.pallas import tpu as pltpu
from jax.sharding import PartitionSpec as P

LANES = 128


def contract_rows(left, right):
    return lax.dot_general(
        left, right, (((0,), (0,)), ((), ())), preferred_element_type=jnp.float32
    )


def contract_last(left, right):
    return lax.dot_general(
        left, right, (((1,), (1,)), ((), ())), preferred_element_type=jnp.float32
    )


def route_kernel(experts, capacity, ids_ref, gates_ref, x_ref, go_ref, sx_ref, sg_ref, place_ref):
    tok_count, model_width = x_ref.shape
    slots = experts * capacity
    ids = ids_ref[...]
    gates = gates_ref[...]
    expert_of = lax.broadcasted_iota(jnp.int32, (tok_count, LANES), 1)
    named = jnp.zeros((tok_count, LANES), jnp.float32)
    gate_of = jnp.zeros((tok_count, LANES), jnp.float32)
    for k in range(ids.shape[1]):
        match = ids[:, k : k + 1] == expert_of
        named = jnp.where(match, 1.0, named)
        gate_of = jnp.where(match, gates[:, k : k + 1], gate_of)
    row = lax.broadcasted_iota(jnp.int32, (tok_count, tok_count), 0)
    col = lax.broadcasted_iota(jnp.int32, (tok_count, tok_count), 1)
    before = jnp.where(row > col, 1.0, 0.0).astype(jnp.bfloat16)
    earlier = jnp.dot(before, named.astype(jnp.bfloat16), preferred_element_type=jnp.float32)
    key = jnp.where(named > 0.0, earlier, -1.0).astype(jnp.bfloat16)
    first = lax.broadcasted_iota(jnp.int32, (LANES, slots), 0) * capacity
    slot = lax.broadcasted_iota(jnp.int32, (LANES, slots), 1)
    spread = jnp.where((slot >= first) & (slot < first + capacity), 1.0, 0.0).astype(jnp.bfloat16)
    wanted = jnp.sum(
        jnp.where(spread > 0.0, (slot - first).astype(jnp.float32), 0.0), axis=0, keepdims=True
    )
    key_at = jnp.dot(key, spread, preferred_element_type=jnp.float32)
    gate_at = jnp.dot(gate_of.astype(jnp.bfloat16), spread, preferred_element_type=jnp.float32)
    chosen = key_at == wanted
    place = jnp.where(chosen, 1.0, 0.0).astype(jnp.bfloat16)
    weigh = jnp.where(chosen, gate_at, 0.0).astype(jnp.bfloat16)
    place_ref[...] = place
    width = 512
    for at in range(0, model_width, width):
        cols = slice(at, at + width)
        sx_ref[:, cols] = contract_rows(place, x_ref[:, cols]).astype(jnp.bfloat16)
        sg_ref[:, cols] = contract_rows(weigh, go_ref[:, cols]).astype(jnp.bfloat16)


def route(expert_ids, gates, tokens, grad_out, experts, capacity):
    tok_count, model_width = tokens.shape
    slots = experts * capacity
    return pl.pallas_call(
        functools.partial(route_kernel, experts, capacity),
        out_shape=(
            jax.ShapeDtypeStruct((slots, model_width), jnp.bfloat16),
            jax.ShapeDtypeStruct((slots, model_width), jnp.bfloat16),
            jax.ShapeDtypeStruct((tok_count, slots), jnp.bfloat16),
        ),
        compiler_params=pltpu.CompilerParams(vmem_limit_bytes=32 * 1024 * 1024),
    )(expert_ids, gates, tokens, grad_out)


def local(tokens, grad_out, expert_ids, gates, gate_weight, up_weight, down_weight):
    experts = lax.axis_size("expert")
    tok_count, top_k = expert_ids.shape
    model_width = tokens.shape[1]
    capacity = 3 * tok_count * top_k // (2 * experts)
    slots = experts * capacity
    w_gate = gate_weight[0]
    w_up = up_weight[0]
    w_down = down_weight[0]

    def exchange(rows):
        return lax.all_to_all(
            rows.reshape(experts, capacity, -1), "expert", split_axis=0, concat_axis=0, tiled=True
        ).reshape(rows.shape)

    send_x, send_ge, place = route(expert_ids, gates, tokens, grad_out, experts, capacity)
    rows_x = exchange(send_x)
    rows_ge = exchange(send_ge)
    slice_x = lax.all_to_all(rows_x, "dp", split_axis=1, concat_axis=0, tiled=True)

    pre_gate = jnp.dot(rows_x, w_gate, preferred_element_type=jnp.float32)
    pre_up = jnp.dot(rows_x, w_up, preferred_element_type=jnp.float32)
    sigmoid_v = jax.nn.sigmoid(pre_gate)
    activated = pre_gate * sigmoid_v
    derivative = sigmoid_v * (1.0 + pre_gate * (1.0 - sigmoid_v))
    hidden = (activated * pre_up).astype(jnp.bfloat16)
    grad_hidden = contract_last(rows_ge, w_down)
    grad_pre_gate = (grad_hidden * pre_up * derivative).astype(jnp.bfloat16)
    grad_pre_up = (grad_hidden * activated).astype(jnp.bfloat16)
    gate_grad = jnp.sum(hidden.astype(jnp.float32) * grad_hidden, axis=1, keepdims=True)

    all_gpg = lax.all_gather(grad_pre_gate, "dp", axis=0, tiled=True)
    all_gpu = lax.all_gather(grad_pre_up, "dp", axis=0, tiled=True)
    grad_down_w = lax.psum_scatter(
        contract_rows(hidden, rows_ge).astype(jnp.bfloat16), "dp", scatter_dimension=0, tiled=True
    ).astype(jnp.float32)

    grad_row = (contract_last(grad_pre_gate, w_gate) + contract_last(grad_pre_up, w_up)).astype(
        jnp.bfloat16
    )
    coarse = gate_grad.astype(jnp.bfloat16)
    fine = (gate_grad - coarse.astype(jnp.float32)).astype(jnp.bfloat16)
    tail = jnp.concatenate([coarse, fine, jnp.zeros((slots, LANES - 2), jnp.bfloat16)], axis=1)
    back = exchange(jnp.concatenate([grad_row, tail], axis=1))

    grad_tokens = jnp.dot(place, back[:, :model_width], preferred_element_type=jnp.float32).astype(
        jnp.bfloat16
    )
    scaled = back[:, model_width].astype(jnp.float32) + back[:, model_width + 1].astype(jnp.float32)
    expert_of_slot = jnp.arange(slots, dtype=jnp.int32) // capacity
    hit = (expert_ids[:, :, None] == expert_of_slot) & (place[:, None, :] > 0)
    gate_b = gates.astype(jnp.bfloat16).astype(jnp.float32)
    grad_gates = (jnp.sum(jnp.where(hit, scaled, 0.0), axis=2) / gate_b).astype(jnp.bfloat16)

    grad_gate_w = contract_rows(slice_x, all_gpg)
    grad_up_w = contract_rows(slice_x, all_gpu)
    return (grad_tokens, grad_gates, grad_gate_w[None], grad_up_w[None], grad_down_w[None])


def solution(mesh):
    placed = (
        P(("dp", "expert"), None),
        P(("dp", "expert"), None),
        P(("dp", "expert"), None),
        P(("dp", "expert"), None),
        P("expert", None, None),
        P("expert", None, None),
        P("expert", None, None),
    )
    return jax.shard_map(
        local,
        mesh=mesh,
        in_specs=placed,
        out_specs=(
            P(("dp", "expert"), None),
            P(("dp", "expert"), None),
            P("expert", "dp", None),
            P("expert", "dp", None),
            P("expert", "dp", None),
        ),
        check_vma=False,
    )
```

```python
import functools

import jax
import jax.numpy as jnp
import numpy as np
from jax import lax
from jax.experimental import pallas as pl
from jax.experimental.pallas import tpu as pltpu
from jax.sharding import PartitionSpec as P

LANES = 128
CHUNKS = 1


def contract_rows(left, right):
    return lax.dot_general(
        left, right, (((0,), (0,)), ((), ())), preferred_element_type=jnp.float32
    )


def contract_last(left, right):
    return lax.dot_general(
        left, right, (((1,), (1,)), ((), ())), preferred_element_type=jnp.float32
    )


def slot_tables(experts, capacity, chunks):
    part = capacity // chunks
    slot = np.arange(experts * capacity)
    expert_at = (slot // part) % experts
    rank_at = (slot // (part * experts)) * part + slot % part
    return expert_at.astype(np.int32), rank_at.astype(np.int32)


def place_rows(ids, expert_at, rank_at):
    tok_count = ids[0].shape[0]
    slots = expert_at.shape[1]
    expert_of = lax.broadcasted_iota(jnp.int32, (tok_count, LANES), 1)
    named = jnp.zeros((tok_count, LANES), jnp.float32)
    for each in ids:
        named = jnp.where(each == expert_of, 1.0, named)
    row = lax.broadcasted_iota(jnp.int32, (tok_count, tok_count), 0)
    col = lax.broadcasted_iota(jnp.int32, (tok_count, tok_count), 1)
    before = jnp.where(row > col, 1.0, 0.0).astype(jnp.bfloat16)
    earlier = jnp.dot(before, named.astype(jnp.bfloat16), preferred_element_type=jnp.float32)
    key = jnp.where(named > 0.0, earlier, -1.0).astype(jnp.bfloat16)
    spread = jnp.where(
        lax.broadcasted_iota(jnp.int32, (LANES, slots), 0) == expert_at, 1.0, 0.0
    ).astype(jnp.bfloat16)
    key_at = jnp.dot(key, spread, preferred_element_type=jnp.float32)
    return key_at == rank_at.astype(jnp.float32), spread


def route_kernel(ids_ref, gates_ref, expert_ref, rank_ref, x_ref, go_ref, sx_ref, sg_ref, place_ref):
    tok_count, model_width = x_ref.shape
    ids = [ids_ref[:, k : k + 1] for k in range(ids_ref.shape[1])]
    chosen, spread = place_rows(ids, expert_ref[...], rank_ref[...])
    expert_of = lax.broadcasted_iota(jnp.int32, (tok_count, LANES), 1)
    gate_of = jnp.zeros((tok_count, LANES), jnp.float32)
    for k, each in enumerate(ids):
        gate_of = jnp.where(each == expert_of, gates_ref[:, k : k + 1], gate_of)
    gate_at = jnp.dot(gate_of.astype(jnp.bfloat16), spread, preferred_element_type=jnp.float32)
    place = jnp.where(chosen, 1.0, 0.0).astype(jnp.bfloat16)
    weigh = jnp.where(chosen, gate_at, 0.0).astype(jnp.bfloat16)
    place_ref[...] = place
    width = 512
    for at in range(0, model_width, width):
        cols = slice(at, at + width)
        sx_ref[:, cols] = contract_rows(place, x_ref[:, cols]).astype(jnp.bfloat16)
        sg_ref[:, cols] = contract_rows(weigh, go_ref[:, cols]).astype(jnp.bfloat16)


def route(expert_ids, gates, tokens, grad_out, expert_at, rank_at):
    tok_count, model_width = tokens.shape
    slots = expert_at.shape[1]
    return pl.pallas_call(
        route_kernel,
        out_shape=(
            jax.ShapeDtypeStruct((slots, model_width), jnp.bfloat16),
            jax.ShapeDtypeStruct((slots, model_width), jnp.bfloat16),
            jax.ShapeDtypeStruct((tok_count, slots), jnp.bfloat16),
        ),
        compiler_params=pltpu.CompilerParams(vmem_limit_bytes=32 * 1024 * 1024),
    )(expert_ids, gates, expert_at, rank_at, tokens, grad_out)


def slices_kernel(top_k, expert_ref, rank_ref, x_ref, out_ref):
    width = x_ref.shape[2] - LANES
    ids = [x_ref[0, :, width + k : width + k + 1].astype(jnp.int32) for k in range(top_k)]
    chosen, _ = place_rows(ids, expert_ref[...], rank_ref[...])
    place = jnp.where(chosen, 1.0, 0.0).astype(jnp.bfloat16)
    out_ref[...] = contract_rows(place, x_ref[0, :, :width]).astype(jnp.bfloat16)


def place_slices(received, top_k, expert_at, rank_at):
    groups, tok_count, wide = received.shape
    slots = expert_at.shape[1]
    width = wide - LANES
    table = pl.BlockSpec((1, slots), lambda g: (0, 0))
    return pl.pallas_call(
        functools.partial(slices_kernel, top_k),
        grid=(groups,),
        in_specs=[table, table, pl.BlockSpec((1, tok_count, wide), lambda g: (g, 0, 0))],
        out_specs=pl.BlockSpec((slots, width), lambda g: (0, g)),
        out_shape=jax.ShapeDtypeStruct((slots, groups * width), jnp.bfloat16),
        compiler_params=pltpu.CompilerParams(vmem_limit_bytes=32 * 1024 * 1024),
    )(expert_at, rank_at, received)


def gather_chain(own, groups):
    up = [(z, z + 1) for z in range(groups - 1)]
    down = [(z + 1, z) for z in range(groups - 1)]
    from_below, from_above = [own], [own]
    for step in range(1, groups):
        from_below.append(lax.ppermute(from_below[-1], "dp", up[step - 1 :]))
        from_above.append(lax.ppermute(from_above[-1], "dp", down[: groups - step]))
    return [own] + [from_below[s] + from_above[groups - s] for s in range(1, groups)]


def scatter_chain(partial, groups):
    z = lax.axis_index("dp")
    depth = partial.shape[0] // groups

    def block(index):
        index = jnp.clip(index, 0, groups - 1)
        return lax.dynamic_slice_in_dim(partial, index * depth, depth, 0)

    def total(sent, index):
        return (sent.astype(jnp.float32) + block(index).astype(jnp.float32)).astype(jnp.bfloat16)

    rising = falling = None
    for step in range(1, groups):
        send_up = block(z + groups - step) if step == 1 else total(rising, z + groups - step)
        send_down = block(z - groups + step) if step == 1 else total(falling, z - groups + step)
        rising = lax.ppermute(send_up, "dp", [(i, i + 1) for i in range(step)])
        falling = lax.ppermute(
            send_down, "dp", [(i, i - 1) for i in range(groups - step, groups)]
        )
    return block(z).astype(jnp.float32) + rising.astype(jnp.float32) + falling.astype(jnp.float32)


def local(tokens, grad_out, expert_ids, gates, gate_weight, up_weight, down_weight):
    experts = lax.axis_size("expert")
    groups = lax.axis_size("dp")
    tok_count, top_k = expert_ids.shape
    model_width = tokens.shape[1]
    capacity = 3 * tok_count * top_k // (2 * experts)
    slots = experts * capacity
    part = slots // CHUNKS
    width = model_width // groups
    w_gate = gate_weight[0]
    w_up = up_weight[0]
    w_down = down_weight[0]
    expert_at, rank_at = slot_tables(experts, capacity, CHUNKS)
    tables = (jnp.asarray(expert_at)[None], jnp.asarray(rank_at)[None])

    def exchange(rows):
        return lax.all_to_all(
            rows.reshape(experts, -1, rows.shape[1]),
            "expert",
            split_axis=0,
            concat_axis=0,
            tiled=True,
        ).reshape(rows.shape)

    send_x, send_ge, place = route(expert_ids, gates, tokens, grad_out, *tables)

    ids_lanes = jnp.pad(expert_ids.astype(jnp.bfloat16), ((0, 0), (0, LANES - top_k)))
    slices = jnp.concatenate(
        [
            tokens.reshape(tok_count, groups, width).transpose(1, 0, 2),
            jnp.broadcast_to(ids_lanes[None], (groups, tok_count, LANES)),
        ],
        axis=2,
    )
    slices = lax.all_to_all(slices, "dp", split_axis=0, concat_axis=0, tiled=True)
    send_slices = place_slices(slices, top_k, *tables)

    rows_x, rows_ge, rows_slices, hiddens, gpgs, gpus, sums = [], [], [], [], [], [], []
    for c in range(CHUNKS):
        rows = slice(c * part, (c + 1) * part)
        x_part = exchange(send_x[rows])
        ge_part = exchange(send_ge[rows])
        pre_gate = jnp.dot(x_part, w_gate, preferred_element_type=jnp.float32)
        pre_up = jnp.dot(x_part, w_up, preferred_element_type=jnp.float32)
        sigmoid_v = jax.nn.sigmoid(pre_gate)
        activated = pre_gate * sigmoid_v
        derivative = sigmoid_v * (1.0 + pre_gate * (1.0 - sigmoid_v))
        hidden = (activated * pre_up).astype(jnp.bfloat16)
        grad_hidden = contract_last(ge_part, w_down)
        gpgs.append((grad_hidden * pre_up * derivative).astype(jnp.bfloat16))
        gpus.append((grad_hidden * activated).astype(jnp.bfloat16))
        sums.append(jnp.sum(hidden.astype(jnp.float32) * grad_hidden, axis=1, keepdims=True))
        rows_ge.append(ge_part)
        hiddens.append(hidden)
        rows_slices.append(exchange(send_slices[rows]))

    all_gpg = [gather_chain(each, groups) for each in gpgs]
    all_gpu = [gather_chain(each, groups) for each in gpus]

    down_partial = sum(contract_rows(h, ge) for h, ge in zip(hiddens, rows_ge)).astype(jnp.bfloat16)
    grad_down_w = scatter_chain(down_partial, groups)

    gpg, gpu = jnp.concatenate(gpgs), jnp.concatenate(gpus)
    gate_grad = jnp.concatenate(sums)
    grad_row = (contract_last(gpg, w_gate) + contract_last(gpu, w_up)).astype(jnp.bfloat16)
    coarse = gate_grad.astype(jnp.bfloat16)
    fine = (gate_grad - coarse.astype(jnp.float32)).astype(jnp.bfloat16)
    tail = jnp.concatenate([coarse, fine, jnp.zeros((slots, LANES - 2), jnp.bfloat16)], axis=1)
    back = jnp.concatenate([grad_row, tail], axis=1).reshape(CHUNKS, experts, -1, model_width + LANES)
    back = lax.all_to_all(back, "expert", split_axis=1, concat_axis=1, tiled=True)
    back = back.reshape(slots, -1)

    grad_tokens = jnp.dot(place, back[:, :model_width], preferred_element_type=jnp.float32).astype(
        jnp.bfloat16
    )
    scaled = back[:, model_width].astype(jnp.float32) + back[:, model_width + 1].astype(jnp.float32)
    hit = (expert_ids[:, :, None] == tables[0][0]) & (place[:, None, :] > 0)
    gate_b = gates.astype(jnp.bfloat16).astype(jnp.float32)
    grad_gates = (jnp.sum(jnp.where(hit, scaled, 0.0), axis=2) / gate_b).astype(jnp.bfloat16)

    z = lax.axis_index("dp")
    grad_gate_w = jnp.zeros((width, w_gate.shape[1]), jnp.float32)
    grad_up_w = jnp.zeros((width, w_up.shape[1]), jnp.float32)
    for s in range(groups):
        start = lax.rem(z - s + groups, groups) * width
        for c in range(CHUNKS):
            part_x = lax.dynamic_slice_in_dim(rows_slices[c], start, width, 1)
            grad_gate_w += contract_rows(part_x, all_gpg[c][s])
            grad_up_w += contract_rows(part_x, all_gpu[c][s])
    return (grad_tokens, grad_gates, grad_gate_w[None], grad_up_w[None], grad_down_w[None])


def solution(mesh):
    placed = (
        P(("dp", "expert"), None),
        P(("dp", "expert"), None),
        P(("dp", "expert"), None),
        P(("dp", "expert"), None),
        P("expert", None, None),
        P("expert", None, None),
        P("expert", None, None),
    )
    return jax.shard_map(
        local,
        mesh=mesh,
        in_specs=placed,
        out_specs=(
            P(("dp", "expert"), None),
            P(("dp", "expert"), None),
            P("expert", "dp", None),
            P("expert", "dp", None),
            P("expert", "dp", None),
        ),
        check_vma=False,
    )
```

```python
import functools

import jax
import jax.numpy as jnp
import numpy as np
from jax import lax
from jax.experimental import pallas as pl
from jax.experimental.pallas import tpu as pltpu
from jax.sharding import PartitionSpec as P

LANES = 128
CHUNKS = 1
VMEM = pltpu.CompilerParams(vmem_limit_bytes=40 * 1024 * 1024)


def contract_rows(left, right):
    return lax.dot_general(
        left, right, (((0,), (0,)), ((), ())), preferred_element_type=jnp.float32
    )


def contract_last(left, right):
    return lax.dot_general(
        left, right, (((1,), (1,)), ((), ())), preferred_element_type=jnp.float32
    )


def cost(flops, *arrays):
    moved = sum(a.size * a.dtype.itemsize for a in arrays)
    return pl.CostEstimate(flops=flops, bytes_accessed=moved, transcendentals=0)


def slot_tables(experts, capacity, chunks):
    part = capacity // chunks
    slot = np.arange(experts * capacity)
    expert_at = (slot // part) % experts
    rank_at = (slot // (part * experts)) * part + slot % part
    return expert_at.astype(np.int32), rank_at.astype(np.int32)


def place_rows(ids, expert_at, rank_at):
    tok_count = ids[0].shape[0]
    slots = expert_at.shape[1]
    expert_of = lax.broadcasted_iota(jnp.int32, (tok_count, LANES), 1)
    named = jnp.zeros((tok_count, LANES), jnp.float32)
    for each in ids:
        named = jnp.where(each == expert_of, 1.0, named)
    row = lax.broadcasted_iota(jnp.int32, (tok_count, tok_count), 0)
    col = lax.broadcasted_iota(jnp.int32, (tok_count, tok_count), 1)
    before = jnp.where(row > col, 1.0, 0.0).astype(jnp.bfloat16)
    earlier = jnp.dot(before, named.astype(jnp.bfloat16), preferred_element_type=jnp.float32)
    key = jnp.where(named > 0.0, earlier, -1.0).astype(jnp.bfloat16)
    spread = jnp.where(
        lax.broadcasted_iota(jnp.int32, (LANES, slots), 0) == expert_at, 1.0, 0.0
    ).astype(jnp.bfloat16)
    key_at = jnp.dot(key, spread, preferred_element_type=jnp.float32)
    return key_at == rank_at.astype(jnp.float32), spread


def route_kernel(
    ids_ref, gates_ref, expert_ref, rank_ref, x_ref, go_ref, send_ref, place_ref, slices_ref
):
    tok_count, model_width = x_ref.shape
    groups = slices_ref.shape[0]
    top_k = ids_ref.shape[1]
    ids = [ids_ref[:, k : k + 1] for k in range(top_k)]
    chosen, spread = place_rows(ids, expert_ref[...], rank_ref[...])
    lane = lax.broadcasted_iota(jnp.int32, (tok_count, LANES), 1)
    gate_of = jnp.zeros((tok_count, LANES), jnp.float32)
    tail = jnp.zeros((tok_count, LANES), jnp.float32)
    for k, each in enumerate(ids):
        gate_of = jnp.where(each == lane, gates_ref[:, k : k + 1], gate_of)
        tail = jnp.where(lane == k, each.astype(jnp.float32), tail)
    gate_at = jnp.dot(gate_of.astype(jnp.bfloat16), spread, preferred_element_type=jnp.float32)
    place = jnp.where(chosen, 1.0, 0.0).astype(jnp.bfloat16)
    weigh = jnp.where(chosen, gate_at, 0.0).astype(jnp.bfloat16)
    place_ref[...] = place
    width = 512
    for at in range(0, model_width, width):
        cols = slice(at, at + width)
        right = slice(model_width + at, model_width + at + width)
        send_ref[:, cols] = contract_rows(place, x_ref[:, cols]).astype(jnp.bfloat16)
        send_ref[:, right] = contract_rows(weigh, go_ref[:, cols]).astype(jnp.bfloat16)
    share = model_width // groups
    for g in range(groups):
        slices_ref[g, :, :share] = x_ref[:, g * share : (g + 1) * share]
        slices_ref[g, :, share:] = tail.astype(jnp.bfloat16)


def route(expert_ids, gates, tokens, grad_out, tables, groups):
    tok_count, model_width = tokens.shape
    slots = tables[0].shape[1]
    out_shape = (
        jax.ShapeDtypeStruct((slots, 2 * model_width), jnp.bfloat16),
        jax.ShapeDtypeStruct((tok_count, slots), jnp.bfloat16),
        jax.ShapeDtypeStruct((groups, tok_count, model_width // groups + LANES), jnp.bfloat16),
    )
    return pl.pallas_call(
        route_kernel,
        out_shape=out_shape,
        compiler_params=VMEM,
        cost_estimate=cost(4 * slots * tok_count * model_width, tokens, grad_out, *out_shape),
    )(expert_ids, gates, *tables, tokens, grad_out)


def slices_kernel(top_k, expert_ref, rank_ref, *refs):
    out_ref = refs[-1]
    for s, x_ref in enumerate(refs[:-1]):
        width = x_ref.shape[1] - LANES
        ids = [x_ref[:, width + k : width + k + 1].astype(jnp.int32) for k in range(top_k)]
        chosen, _ = place_rows(ids, expert_ref[...], rank_ref[...])
        place = jnp.where(chosen, 1.0, 0.0).astype(jnp.bfloat16)
        out_ref[:, s * width : (s + 1) * width] = contract_rows(
            place, x_ref[:, :width]
        ).astype(jnp.bfloat16)


def place_slices(received, top_k, tables):
    tok_count, wide = received[0].shape
    slots = tables[0].shape[1]
    out_shape = jax.ShapeDtypeStruct((slots, len(received) * (wide - LANES)), jnp.bfloat16)
    return pl.pallas_call(
        functools.partial(slices_kernel, top_k),
        out_shape=out_shape,
        compiler_params=VMEM,
        cost_estimate=cost(2 * slots * tok_count * out_shape.shape[1], out_shape),
    )(*tables, *received)


def expert_kernel(rows_ref, gate_ref, up_ref, down_ref, hidden_ref, grads_ref, tail_ref, sum_ref):
    model_width = rows_ref.shape[1] // 2
    step = pl.program_id(0)
    rows_x = rows_ref[:, :model_width]
    pre_gate = jnp.dot(rows_x, gate_ref[0], preferred_element_type=jnp.float32)
    pre_up = jnp.dot(rows_x, up_ref[0], preferred_element_type=jnp.float32)
    grad_hidden = contract_last(rows_ref[:, model_width:], down_ref[0])
    sigmoid_v = 1.0 / (1.0 + jnp.exp(-pre_gate))
    activated = pre_gate * sigmoid_v
    derivative = sigmoid_v * (1.0 + pre_gate * (1.0 - sigmoid_v))
    hidden = (activated * pre_up).astype(jnp.bfloat16)
    hidden_ref[...] = hidden
    grads_ref[0] = (grad_hidden * pre_up * derivative).astype(jnp.bfloat16)
    grads_ref[1] = (grad_hidden * activated).astype(jnp.bfloat16)
    gate_grad = jnp.sum(hidden.astype(jnp.float32) * grad_hidden, axis=1, keepdims=True)

    @pl.when(step == 0)
    def _():
        sum_ref[...] = jnp.zeros_like(sum_ref)

    sum_ref[...] += gate_grad

    @pl.when(step == pl.num_programs(0) - 1)
    def _():
        total = sum_ref[...]
        coarse = total.astype(jnp.bfloat16).astype(jnp.float32)
        lane = lax.broadcasted_iota(jnp.int32, total.shape, 1)
        tail = jnp.where(lane == 0, coarse, jnp.where(lane == 1, total - coarse, 0.0))
        tail_ref[...] = tail.astype(jnp.bfloat16)


def expert_rows(rows, gate_weight, up_weight, down_weight):
    count, wide = rows.shape
    _, model_width, hidden_width = gate_weight.shape
    tile = 256
    out_shape = (
        jax.ShapeDtypeStruct((count, hidden_width), jnp.bfloat16),
        jax.ShapeDtypeStruct((2, count, hidden_width), jnp.bfloat16),
        jax.ShapeDtypeStruct((count, LANES), jnp.bfloat16),
    )
    return pl.pallas_call(
        expert_kernel,
        grid=(hidden_width // tile,),
        in_specs=[
            pl.BlockSpec((count, wide), lambda i: (0, 0)),
            pl.BlockSpec((1, model_width, tile), lambda i: (0, 0, i)),
            pl.BlockSpec((1, model_width, tile), lambda i: (0, 0, i)),
            pl.BlockSpec((1, tile, model_width), lambda i: (0, i, 0)),
        ],
        out_specs=(
            pl.BlockSpec((count, tile), lambda i: (0, i)),
            pl.BlockSpec((2, count, tile), lambda i: (0, 0, i)),
            pl.BlockSpec((count, LANES), lambda i: (0, 0)),
        ),
        out_shape=out_shape,
        scratch_shapes=[pltpu.VMEM((count, LANES), jnp.float32)],
        compiler_params=VMEM,
        cost_estimate=cost(
            6 * count * model_width * hidden_width, rows, gate_weight, up_weight, down_weight
        ),
    )(rows, gate_weight, up_weight, down_weight)


def back_kernel(grads_ref, tail_ref, gate_ref, up_ref, out_ref):
    step = pl.program_id(0)
    tile = gate_ref.shape[1]
    model_width = out_ref.shape[1] - LANES
    row = contract_last(grads_ref[0], gate_ref[0]) + contract_last(grads_ref[1], up_ref[0])
    out_ref[:, pl.ds(pl.multiple_of(step * tile, tile), tile)] = row.astype(jnp.bfloat16)
    out_ref[:, model_width:] = tail_ref[...]


def back_rows(grads, tail, gate_weight, up_weight):
    _, count, hidden_width = grads.shape
    model_width = gate_weight.shape[1]
    tile = 512
    out_shape = jax.ShapeDtypeStruct((count, model_width + LANES), jnp.bfloat16)
    return pl.pallas_call(
        back_kernel,
        grid=(model_width // tile,),
        in_specs=[
            pl.BlockSpec((2, count, hidden_width), lambda i: (0, 0, 0)),
            pl.BlockSpec((count, LANES), lambda i: (0, 0)),
            pl.BlockSpec((1, tile, hidden_width), lambda i: (0, i, 0)),
            pl.BlockSpec((1, tile, hidden_width), lambda i: (0, i, 0)),
        ],
        out_specs=pl.BlockSpec((count, model_width + LANES), lambda i: (0, 0)),
        out_shape=out_shape,
        compiler_params=VMEM,
        cost_estimate=cost(
            4 * count * model_width * hidden_width, grads, gate_weight, up_weight, out_shape
        ),
    )(grads, tail, gate_weight, up_weight)


def gather_chain(own, groups):
    up = [(z, z + 1) for z in range(groups - 1)]
    down = [(z + 1, z) for z in range(groups - 1)]
    from_below, from_above = [own], [own]
    for step in range(1, groups):
        from_below.append(lax.ppermute(from_below[-1], "dp", up[step - 1 :]))
        from_above.append(lax.ppermute(from_above[-1], "dp", down[: groups - step]))
    return [own] + [from_below[s] + from_above[groups - s] for s in range(1, groups)]


def scatter_chain(partial, groups):
    z = lax.axis_index("dp")
    depth = partial.shape[0] // groups

    def block(index):
        index = jnp.clip(index, 0, groups - 1)
        return lax.dynamic_slice_in_dim(partial, index * depth, depth, 0)

    def total(sent, index):
        return (sent.astype(jnp.float32) + block(index).astype(jnp.float32)).astype(jnp.bfloat16)

    rising = falling = None
    for step in range(1, groups):
        send_up = block(z + groups - step) if step == 1 else total(rising, z + groups - step)
        send_down = block(z - groups + step) if step == 1 else total(falling, z - groups + step)
        rising = lax.ppermute(send_up, "dp", [(i, i + 1) for i in range(step)])
        falling = lax.ppermute(
            send_down, "dp", [(i, i - 1) for i in range(groups - step, groups)]
        )
    return block(z).astype(jnp.float32) + rising.astype(jnp.float32) + falling.astype(jnp.float32)


def local(tokens, grad_out, expert_ids, gates, gate_weight, up_weight, down_weight):
    experts = lax.axis_size("expert")
    groups = lax.axis_size("dp")
    tok_count, top_k = expert_ids.shape
    model_width = tokens.shape[1]
    hidden_width = gate_weight.shape[2]
    capacity = 3 * tok_count * top_k // (2 * experts)
    slots = experts * capacity
    part = slots // CHUNKS
    width = model_width // groups
    expert_at, rank_at = slot_tables(experts, capacity, CHUNKS)
    tables = (jnp.asarray(expert_at)[None], jnp.asarray(rank_at)[None])
    z = lax.axis_index("dp")

    def exchange(rows):
        return lax.all_to_all(
            rows.reshape(experts, -1, rows.shape[1]),
            "expert",
            split_axis=0,
            concat_axis=0,
            tiled=True,
        ).reshape(rows.shape)

    send, place, slices = route(expert_ids, gates, tokens, grad_out, tables, groups)

    received = [lax.dynamic_index_in_dim(slices, z, 0, keepdims=False)]
    for shift in range(1, groups):
        mine = lax.dynamic_index_in_dim(slices, lax.rem(z + shift, groups), 0, keepdims=False)
        ring = [(i, (i + shift) % groups) for i in range(groups)]
        received.append(lax.ppermute(mine, "dp", ring))
    send_slices = place_slices(received, top_k, tables)

    rows, slice_rows, hiddens, grads, tails, backs = [], [], [], [], [], []
    for c in range(CHUNKS):
        at = slice(c * part, (c + 1) * part)
        rows.append(exchange(send[at]))
        hidden, grad, tail = expert_rows(rows[c], gate_weight, up_weight, down_weight)
        hiddens.append(hidden)
        grads.append(grad)
        tails.append(tail)
    gathered = [gather_chain(each, groups) for each in grads]

    down_partial = sum(
        contract_rows(h, r[:, model_width:]) for h, r in zip(hiddens, rows)
    ).astype(jnp.bfloat16)
    grad_down_w = scatter_chain(down_partial, groups)

    for c in range(CHUNKS):
        at = slice(c * part, (c + 1) * part)
        backs.append(exchange(back_rows(grads[c], tails[c], gate_weight, up_weight)))
        slice_rows.append(exchange(send_slices[at]))

    grad_tokens, scaled = 0.0, []
    for c, back in enumerate(backs):
        at = slice(c * part, (c + 1) * part)
        grad_tokens += jnp.dot(
            place[:, at], back[:, :model_width], preferred_element_type=jnp.float32
        )
        pair = back[:, model_width : model_width + 2].astype(jnp.float32)
        scaled.append(pair[:, 0] + pair[:, 1])
    grad_tokens = grad_tokens.astype(jnp.bfloat16)
    hit = (expert_ids[:, :, None] == tables[0][0]) & (place[:, None, :] > 0)
    gate_b = gates.astype(jnp.bfloat16).astype(jnp.float32)
    scaled = jnp.concatenate(scaled)
    grad_gates = (jnp.sum(jnp.where(hit, scaled, 0.0), axis=2) / gate_b).astype(jnp.bfloat16)

    grad_gate_w = jnp.zeros((width, hidden_width), jnp.float32)
    grad_up_w = jnp.zeros((width, hidden_width), jnp.float32)
    for s in range(groups):
        for c in range(CHUNKS):
            part_x = slice_rows[c][:, s * width : (s + 1) * width]
            grad_gate_w += contract_rows(part_x, gathered[c][s][0])
            grad_up_w += contract_rows(part_x, gathered[c][s][1])
    return (grad_tokens, grad_gates, grad_gate_w[None], grad_up_w[None], grad_down_w[None])


def solution(mesh):
    placed = (
        P(("dp", "expert"), None),
        P(("dp", "expert"), None),
        P(("dp", "expert"), None),
        P(("dp", "expert"), None),
        P("expert", None, None),
        P("expert", None, None),
        P("expert", None, None),
    )
    return jax.shard_map(
        local,
        mesh=mesh,
        in_specs=placed,
        out_specs=(
            P(("dp", "expert"), None),
            P(("dp", "expert"), None),
            P("expert", "dp", None),
            P("expert", "dp", None),
            P("expert", "dp", None),
        ),
        check_vma=False,
    )
```

```python
import functools

import jax
import jax.numpy as jnp
import numpy as np
from jax import lax
from jax.experimental import pallas as pl
from jax.experimental.pallas import tpu as pltpu
from jax.sharding import PartitionSpec as P

LANES = 128
EXTRA = 16
CHUNKS = 1
VMEM = pltpu.CompilerParams(vmem_limit_bytes=62 * 1024 * 1024)


def contract_rows(left, right):
    return lax.dot_general(
        left, right, (((0,), (0,)), ((), ())), preferred_element_type=jnp.float32
    )


def contract_last(left, right):
    return lax.dot_general(
        left, right, (((1,), (1,)), ((), ())), preferred_element_type=jnp.float32
    )


def cost():
    return pl.CostEstimate(flops=1024, bytes_accessed=1024, transcendentals=0)


def slot_tables(experts, capacity, chunks):
    part = capacity // chunks
    slot = np.arange(experts * capacity)
    expert_at = (slot // part) % experts
    rank_at = (slot // (part * experts)) * part + slot % part
    spread = (expert_at[:, None] == np.arange(LANES)[None, :]).astype(np.float32)
    spread[:, -1] = -rank_at
    return expert_at.astype(np.int32), jnp.asarray(spread, jnp.bfloat16)


def match_rows(id_rows):
    expert_of = lax.broadcasted_iota(jnp.int32, (LANES, id_rows[0].shape[1]), 0)
    return [each == expert_of for each in id_rows]


def chosen_slots(matches, spread):
    tok_count = matches[0].shape[1]
    named = functools.reduce(jnp.logical_or, matches)
    row = lax.broadcasted_iota(jnp.int32, (tok_count, tok_count), 0)
    col = lax.broadcasted_iota(jnp.int32, (tok_count, tok_count), 1)
    after = jnp.where(row < col, 1.0, 0.0).astype(jnp.bfloat16)
    earlier = jnp.dot(
        jnp.where(named, 1.0, 0.0).astype(jnp.bfloat16), after, preferred_element_type=jnp.float32
    )
    last = lax.broadcasted_iota(jnp.int32, named.shape, 0) == LANES - 1
    key = jnp.where(last, 1.0, jnp.where(named, earlier, -1.0)).astype(jnp.bfloat16)
    return jnp.dot(spread, key, preferred_element_type=jnp.float32) == 0.0


def route_kernel(ids_ref, gates_ref, spread_ref, x_ref, go_ref, place_ref, slices_ref, *send_refs):
    tok_count, model_width = x_ref.shape
    groups = slices_ref.shape[0]
    id_rows = [ids_ref[k : k + 1, :] for k in range(ids_ref.shape[0])]
    spread = spread_ref[...]
    matches = match_rows(id_rows)
    chosen = chosen_slots(matches, spread)
    gate_of = jnp.zeros(matches[0].shape, jnp.float32)
    for k, match in enumerate(matches):
        gate_of = jnp.where(match, gates_ref[k : k + 1, :], gate_of)
    gate_at = jnp.dot(spread, gate_of.astype(jnp.bfloat16), preferred_element_type=jnp.float32)
    place = jnp.where(chosen, 1.0, 0.0).astype(jnp.bfloat16)
    weigh = jnp.where(chosen, gate_at, 0.0).astype(jnp.bfloat16)
    place_ref[...] = place
    width = 512
    part = send_refs[0].shape[0]
    for c, send_ref in enumerate(send_refs):
        rows = slice(c * part, (c + 1) * part)
        for at in range(0, model_width, width):
            cols = slice(at, at + width)
            right = slice(model_width + at, model_width + at + width)
            send_ref[:, cols] = jnp.dot(
                place[rows], x_ref[:, cols], preferred_element_type=jnp.float32
            ).astype(jnp.bfloat16)
            send_ref[:, right] = jnp.dot(
                weigh[rows], go_ref[:, cols], preferred_element_type=jnp.float32
            ).astype(jnp.bfloat16)
    share = model_width // groups
    line = lax.broadcasted_iota(jnp.int32, (EXTRA, tok_count), 0)
    tail = jnp.zeros((EXTRA, tok_count), jnp.float32)
    for k, each in enumerate(id_rows):
        tail = jnp.where(line == k, each.astype(jnp.float32), tail)
    for g in range(groups):
        slices_ref[g, :tok_count, :] = x_ref[:, g * share : (g + 1) * share]
        slices_ref[g, tok_count:, :] = jnp.zeros((EXTRA, share), jnp.bfloat16)
        slices_ref[g, tok_count:, :tok_count] = tail.astype(jnp.bfloat16)


def route(expert_ids, gates, tokens, grad_out, spread, groups):
    tok_count, model_width = tokens.shape
    slots = spread.shape[0]
    sent = jax.ShapeDtypeStruct((slots // CHUNKS, 2 * model_width), jnp.bfloat16)
    out_shape = (
        jax.ShapeDtypeStruct((slots, tok_count), jnp.bfloat16),
        jax.ShapeDtypeStruct((groups, tok_count + EXTRA, model_width // groups), jnp.bfloat16),
        *[sent] * CHUNKS,
    )
    return pl.pallas_call(
        route_kernel,
        out_shape=out_shape,
        compiler_params=VMEM,
        cost_estimate=cost(),
    )(expert_ids.T, gates.T, spread, tokens, grad_out)


def slices_kernel(top_k, spread_ref, *refs):
    out_refs, refs = refs[-CHUNKS:], refs[:-CHUNKS]
    part = out_refs[0].shape[0]
    for s, x_ref in enumerate(refs):
        tok_count, width = x_ref.shape[0] - EXTRA, x_ref.shape[1]
        tail = x_ref[tok_count:, :tok_count].astype(jnp.float32).astype(jnp.int32)
        matches = match_rows([tail[k : k + 1, :] for k in range(top_k)])
        chosen = chosen_slots(matches, spread_ref[...])
        place = jnp.where(chosen, 1.0, 0.0).astype(jnp.bfloat16)
        for c, out_ref in enumerate(out_refs):
            out_ref[:, s * width : (s + 1) * width] = jnp.dot(
                place[c * part : (c + 1) * part],
                x_ref[:tok_count, :],
                preferred_element_type=jnp.float32,
            ).astype(jnp.bfloat16)


def place_slices(received, top_k, spread):
    width = received[0].shape[1]
    sent = jax.ShapeDtypeStruct((spread.shape[0] // CHUNKS, len(received) * width), jnp.bfloat16)
    return pl.pallas_call(
        functools.partial(slices_kernel, top_k),
        out_shape=[sent] * CHUNKS,
        compiler_params=VMEM,
        cost_estimate=cost(),
    )(spread, *received)


def down_kernel(chunks, *refs):
    out_ref = refs[-1]
    total = 0.0
    for hidden_ref, ge_ref in zip(refs[:chunks], refs[chunks:-1]):
        total += contract_rows(hidden_ref[...], ge_ref[...])
    out_ref[...] = total.astype(jnp.bfloat16)


def down_rows(hiddens, rows):
    part, hidden_width = hiddens[0].shape
    model_width = rows[0].shape[1] // 2
    tile = 256
    return pl.pallas_call(
        functools.partial(down_kernel, len(rows)),
        grid=(hidden_width // tile,),
        in_specs=[pl.BlockSpec((part, tile), lambda i: (0, i)) for _ in hiddens]
        + [pl.BlockSpec((part, model_width), lambda i: (0, 1)) for _ in rows],
        out_specs=pl.BlockSpec((tile, model_width), lambda i: (i, 0)),
        out_shape=jax.ShapeDtypeStruct((hidden_width, model_width), jnp.bfloat16),
        compiler_params=VMEM,
        cost_estimate=cost(),
    )(*hiddens, *rows)


def weight_kernel(terms, carried, *refs):
    outs = refs[-2:]
    for which, out_ref in enumerate(outs):
        total = refs[2 * terms + which][0] if carried else 0.0
        for t in range(terms):
            total += contract_rows(refs[t][...], refs[terms + t][which])
        out_ref[0] = total


def weight_rows(carried, terms, model_width, groups):
    _, part, hidden_width = terms[0][2].shape
    width = model_width // groups
    tile = 256
    count = len(terms)
    whole = pl.BlockSpec((1, width, tile), lambda i: (0, 0, i))
    out_shape = jax.ShapeDtypeStruct((1, width, hidden_width), jnp.float32)
    return pl.pallas_call(
        functools.partial(weight_kernel, count, bool(carried)),
        grid=(hidden_width // tile,),
        in_specs=[
            pl.BlockSpec((part, width), lambda i, s=s: (0, groups + s)) for _, s, _ in terms
        ]
        + [pl.BlockSpec((2, part, tile), lambda i: (0, 0, i)) for _ in terms]
        + [whole] * len(carried),
        out_specs=(whole, whole),
        out_shape=(out_shape, out_shape),
        input_output_aliases={2 * count + i: i for i in range(len(carried))},
        compiler_params=VMEM,
        cost_estimate=cost(),
    )(*[rows for rows, _, _ in terms], *[both for _, _, both in terms], *carried)


def expert_kernel(rows_ref, gate_ref, up_ref, down_ref, hidden_ref, grads_ref, tail_ref, sum_ref):
    model_width = rows_ref.shape[1] // 2
    step = pl.program_id(0)
    rows_x = rows_ref[:, :model_width]
    pre_gate = jnp.dot(rows_x, gate_ref[0], preferred_element_type=jnp.float32)
    pre_up = jnp.dot(rows_x, up_ref[0], preferred_element_type=jnp.float32)
    grad_hidden = contract_last(rows_ref[:, model_width:], down_ref[0])
    sigmoid_v = 1.0 / (1.0 + jnp.exp(-pre_gate))
    activated = pre_gate * sigmoid_v
    derivative = sigmoid_v * (1.0 + pre_gate * (1.0 - sigmoid_v))
    hidden = (activated * pre_up).astype(jnp.bfloat16)
    hidden_ref[...] = hidden
    grads_ref[0] = (grad_hidden * pre_up * derivative).astype(jnp.bfloat16)
    grads_ref[1] = (grad_hidden * activated).astype(jnp.bfloat16)
    gate_grad = jnp.sum(hidden.astype(jnp.float32) * grad_hidden, axis=1, keepdims=True)

    @pl.when(step == 0)
    def _():
        sum_ref[...] = jnp.zeros_like(sum_ref)

    sum_ref[...] += gate_grad

    @pl.when(step == pl.num_programs(0) - 1)
    def _():
        total = sum_ref[...]
        coarse = total.astype(jnp.bfloat16).astype(jnp.float32)
        lane = lax.broadcasted_iota(jnp.int32, total.shape, 1)
        tail = jnp.where(lane == 0, coarse, jnp.where(lane == 1, total - coarse, 0.0))
        tail_ref[...] = tail.astype(jnp.bfloat16)


def expert_rows(rows, gate_weight, up_weight, down_weight):
    count, wide = rows.shape
    _, model_width, hidden_width = gate_weight.shape
    tile = 256
    out_shape = (
        jax.ShapeDtypeStruct((count, hidden_width), jnp.bfloat16),
        jax.ShapeDtypeStruct((2, count, hidden_width), jnp.bfloat16),
        jax.ShapeDtypeStruct((count, LANES), jnp.bfloat16),
    )
    return pl.pallas_call(
        expert_kernel,
        grid=(hidden_width // tile,),
        in_specs=[
            pl.BlockSpec((count, wide), lambda i: (0, 0)),
            pl.BlockSpec((1, model_width, tile), lambda i: (0, 0, i)),
            pl.BlockSpec((1, model_width, tile), lambda i: (0, 0, i)),
            pl.BlockSpec((1, tile, model_width), lambda i: (0, i, 0)),
        ],
        out_specs=(
            pl.BlockSpec((count, tile), lambda i: (0, i)),
            pl.BlockSpec((2, count, tile), lambda i: (0, 0, i)),
            pl.BlockSpec((count, LANES), lambda i: (0, 0)),
        ),
        out_shape=out_shape,
        scratch_shapes=[pltpu.VMEM((count, LANES), jnp.float32)],
        compiler_params=VMEM,
        cost_estimate=cost(),
    )(rows, gate_weight, up_weight, down_weight)


def back_kernel(grads_ref, tail_ref, slices_ref, gate_ref, up_ref, out_ref):
    step = pl.program_id(0)
    tile = gate_ref.shape[1]
    model_width = slices_ref.shape[1]
    row = contract_last(grads_ref[0], gate_ref[0]) + contract_last(grads_ref[1], up_ref[0])
    cols = pl.ds(pl.multiple_of(step * tile, tile), tile)
    right = pl.ds(pl.multiple_of(model_width + step * tile, tile), tile)
    out_ref[:, cols] = row.astype(jnp.bfloat16)
    out_ref[:, right] = slices_ref[:, cols]
    out_ref[:, 2 * model_width :] = tail_ref[...]


def back_rows(grads, tail, slices, gate_weight, up_weight):
    _, count, hidden_width = grads.shape
    model_width = gate_weight.shape[1]
    tile = 512
    wide = 2 * model_width + LANES
    out_shape = jax.ShapeDtypeStruct((count, wide), jnp.bfloat16)
    return pl.pallas_call(
        back_kernel,
        grid=(model_width // tile,),
        in_specs=[
            pl.BlockSpec((2, count, hidden_width), lambda i: (0, 0, 0)),
            pl.BlockSpec((count, LANES), lambda i: (0, 0)),
            pl.BlockSpec((count, model_width), lambda i: (0, 0)),
            pl.BlockSpec((1, tile, hidden_width), lambda i: (0, i, 0)),
            pl.BlockSpec((1, tile, hidden_width), lambda i: (0, i, 0)),
        ],
        out_specs=pl.BlockSpec((count, wide), lambda i: (0, 0)),
        out_shape=out_shape,
        compiler_params=VMEM,
        cost_estimate=cost(),
    )(grads, tail, slices, gate_weight, up_weight)


def exchange_groups(grads, partial, groups, send_back, exchange):
    z = lax.axis_index("dp")
    depth = partial.shape[0] // groups
    chunks = len(grads)
    last = chunks + groups - 2

    def block(index):
        index = jnp.clip(index, 0, groups - 1)
        return lax.dynamic_slice_in_dim(partial, index * depth, depth, 0)

    def total(sent, index):
        return (sent.astype(jnp.float32) + block(index).astype(jnp.float32)).astype(jnp.bfloat16)

    below = [[own] for own in grads]
    above = [[own] for own in grads]
    backs = [exchange(send_back(c)) for c in range(chunks)]
    rising = falling = None
    for slot in range(chunks + groups - 1):
        active = [c for c in range(chunks) if 1 <= slot - c + 1 < groups]
        sums = slot - chunks + 1
        pair = None
        if sums == 1:
            pair = (block(z + groups - sums), block(z - groups + sums))
        elif sums > 1:
            pair = (total(rising, z + groups - sums), total(falling, z - groups + sums))
        for c in active:
            step = slot - c + 1
            up, down = below[c][-1], above[c][-1]
            if c == chunks - 1 and pair:
                up, down, pair = lax.optimization_barrier((up, down, pair))
                below[c][-1], above[c][-1] = up, down
            lifts = [(i, i + 1) for i in range(step - 1, groups - 1)]
            drops = [(i + 1, i) for i in range(groups - step)]
            below[c].append(lax.ppermute(up, "dp", lifts))
            above[c].append(lax.ppermute(down, "dp", drops))
        if slot == last:
            pair, backs[-1] = lax.optimization_barrier((pair, backs[-1]))
        if pair:
            rising = lax.ppermute(pair[0], "dp", [(i, i + 1) for i in range(sums)])
            falling = lax.ppermute(pair[1], "dp", [(i, i - 1) for i in range(groups - sums, groups)])
    summed = block(z).astype(jnp.float32) + rising.astype(jnp.float32) + falling.astype(jnp.float32)
    return below, above, backs, summed


def local(tokens, grad_out, expert_ids, gates, gate_weight, up_weight, down_weight):
    experts = lax.axis_size("expert")
    groups = lax.axis_size("dp")
    tok_count, top_k = expert_ids.shape
    model_width = tokens.shape[1]
    capacity = 3 * tok_count * top_k // (2 * experts)
    slots = experts * capacity
    part = slots // CHUNKS
    expert_at, spread = slot_tables(experts, capacity, CHUNKS)
    z = lax.axis_index("dp")

    def exchange(rows):
        return lax.all_to_all(
            rows.reshape(experts, -1, rows.shape[1]),
            "expert",
            split_axis=0,
            concat_axis=0,
            tiled=True,
        ).reshape(rows.shape)

    place, slices, *send = route(expert_ids, gates, tokens, grad_out, spread, groups)

    received = [lax.dynamic_index_in_dim(slices, z, 0, keepdims=False)]
    for shift in range(1, groups):
        mine = lax.dynamic_index_in_dim(slices, lax.rem(z + shift, groups), 0, keepdims=False)
        ring = [(i, (i + shift) % groups) for i in range(groups)]
        received.append(lax.ppermute(mine, "dp", ring))
    send_slices = place_slices(received, top_k, spread)

    rows, hiddens, grads, tails = [], [], [], []
    for c in range(CHUNKS):
        rows.append(exchange(send[c]))
        if c == CHUNKS - 1:
            rows[c], send_slices = lax.optimization_barrier((rows[c], send_slices))
        hidden, grad, tail = expert_rows(rows[c], gate_weight, up_weight, down_weight)
        hiddens.append(hidden)
        grads.append(grad)
        tails.append(tail)
    down_partial = down_rows(hiddens, rows)

    def send_back(c):
        return back_rows(grads[c], tails[c], send_slices[c], gate_weight, up_weight)

    below, above, backs, grad_down_w = exchange_groups(
        grads, down_partial, groups, send_back, exchange
    )

    grad_tokens, scaled = 0.0, []
    for c, back in enumerate(backs):
        at = slice(c * part, (c + 1) * part)
        grad_tokens += contract_rows(place[at], back[:, :model_width])
        pair = back[:, 2 * model_width : 2 * model_width + 2].astype(jnp.float32)
        scaled.append(pair[:, 0] + pair[:, 1])
    grad_tokens = grad_tokens.astype(jnp.bfloat16)
    scaled = jnp.concatenate(scaled)[:, None]
    gate_b = gates.T.astype(jnp.bfloat16).astype(jnp.float32)
    grad_gates = []
    for k in range(top_k):
        hit = (expert_ids[:, k][None, :] == expert_at[:, None]) & (place > 0)
        grad_gates.append(jnp.sum(jnp.where(hit, scaled, 0.0), axis=0) / gate_b[k])
    grad_gates = jnp.stack(grad_gates).astype(jnp.bfloat16).T

    grad_w = ()
    for step in range(groups):
        terms = []
        for c in range(CHUNKS):
            terms.append((backs[c], step, below[c][step]))
            if step:
                terms.append((backs[c], groups - step, above[c][step]))
        grad_w = weight_rows(grad_w, terms, model_width, groups)
    return (grad_tokens, grad_gates, *grad_w, grad_down_w[None])


def solution(mesh):
    placed = (
        P(("dp", "expert"), None),
        P(("dp", "expert"), None),
        P(("dp", "expert"), None),
        P(("dp", "expert"), None),
        P("expert", None, None),
        P("expert", None, None),
        P("expert", None, None),
    )
    return jax.shard_map(
        local,
        mesh=mesh,
        in_specs=placed,
        out_specs=(
            P(("dp", "expert"), None),
            P(("dp", "expert"), None),
            P("expert", "dp", None),
            P("expert", "dp", None),
            P("expert", "dp", None),
        ),
        check_vma=False,
    )
```

```python
import functools

import jax
import jax.numpy as jnp
import numpy as np
from jax import lax
from jax.experimental import pallas as pl
from jax.experimental.pallas import tpu as pltpu
from jax.sharding import PartitionSpec as P

LANES = 128
EXTRA = 16
CHUNKS = 2
VMEM = pltpu.CompilerParams(vmem_limit_bytes=62 * 1024 * 1024)


def contract_rows(left, right):
    return lax.dot_general(
        left, right, (((0,), (0,)), ((), ())), preferred_element_type=jnp.float32
    )


def contract_last(left, right):
    return lax.dot_general(
        left, right, (((1,), (1,)), ((), ())), preferred_element_type=jnp.float32
    )


def cost(flops=1024):
    return pl.CostEstimate(flops=flops, bytes_accessed=1024, transcendentals=0)


def chunk_ranks(capacity):
    edges = [capacity * c // CHUNKS for c in range(CHUNKS + 1)]
    return [np.arange(first, last) for first, last in zip(edges, edges[1:])]


def slot_tables(experts, capacity):
    ranks = chunk_ranks(capacity)
    rank_at = np.concatenate([np.tile(own, experts) for own in ranks])
    expert_at = np.concatenate([np.repeat(np.arange(experts), len(own)) for own in ranks])
    spread = (expert_at[:, None] == np.arange(LANES)[None, :]).astype(np.float32)
    spread[:, -1] = -rank_at
    return expert_at.astype(np.int32), jnp.asarray(spread, jnp.bfloat16)


def match_rows(id_rows):
    expert_of = lax.broadcasted_iota(jnp.int32, (LANES, id_rows[0].shape[1]), 0)
    return [each == expert_of for each in id_rows]


def chosen_slots(matches, spread):
    tok_count = matches[0].shape[1]
    named = functools.reduce(jnp.logical_or, matches)
    row = lax.broadcasted_iota(jnp.int32, (tok_count, tok_count), 0)
    col = lax.broadcasted_iota(jnp.int32, (tok_count, tok_count), 1)
    after = jnp.where(row < col, 1.0, 0.0).astype(jnp.bfloat16)
    earlier = jnp.dot(
        jnp.where(named, 1.0, 0.0).astype(jnp.bfloat16), after, preferred_element_type=jnp.float32
    )
    last = lax.broadcasted_iota(jnp.int32, named.shape, 0) == LANES - 1
    key = jnp.where(last, 1.0, jnp.where(named, earlier, -1.0)).astype(jnp.bfloat16)
    return jnp.dot(spread, key, preferred_element_type=jnp.float32) == 0.0


def route_kernel(ids_ref, gates_ref, spread_ref, x_ref, go_ref, place_ref, slices_ref, *send_refs):
    tok_count, model_width = x_ref.shape
    groups = slices_ref.shape[0]
    id_rows = [ids_ref[k : k + 1, :] for k in range(ids_ref.shape[0])]
    spread = spread_ref[...]
    matches = match_rows(id_rows)
    chosen = chosen_slots(matches, spread)
    gate_of = jnp.zeros(matches[0].shape, jnp.float32)
    for k, match in enumerate(matches):
        gate_of = jnp.where(match, gates_ref[k : k + 1, :], gate_of)
    gate_at = jnp.dot(spread, gate_of.astype(jnp.bfloat16), preferred_element_type=jnp.float32)
    place = jnp.where(chosen, 1.0, 0.0).astype(jnp.bfloat16)
    weigh = jnp.where(chosen, gate_at, 0.0).astype(jnp.bfloat16)
    place_ref[...] = place
    width = 512
    done = 0
    for send_ref in send_refs:
        rows = slice(done, done + send_ref.shape[0])
        done = rows.stop
        for at in range(0, model_width, width):
            cols = slice(at, at + width)
            right = slice(model_width + at, model_width + at + width)
            send_ref[:, cols] = jnp.dot(
                place[rows], x_ref[:, cols], preferred_element_type=jnp.float32
            ).astype(jnp.bfloat16)
            send_ref[:, right] = jnp.dot(
                weigh[rows], go_ref[:, cols], preferred_element_type=jnp.float32
            ).astype(jnp.bfloat16)
    share = model_width // groups
    line = lax.broadcasted_iota(jnp.int32, (EXTRA, tok_count), 0)
    tail = jnp.zeros((EXTRA, tok_count), jnp.float32)
    for k, each in enumerate(id_rows):
        tail = jnp.where(line == k, each.astype(jnp.float32), tail)
    for g in range(groups):
        slices_ref[g, :tok_count, :] = x_ref[:, g * share : (g + 1) * share]
        slices_ref[g, tok_count:, :] = jnp.zeros((EXTRA, share), jnp.bfloat16)
        slices_ref[g, tok_count:, :tok_count] = tail.astype(jnp.bfloat16)


def route(expert_ids, gates, tokens, grad_out, spread, parts, groups):
    tok_count, model_width = tokens.shape
    slots = spread.shape[0]
    out_shape = (
        jax.ShapeDtypeStruct((slots, tok_count), jnp.bfloat16),
        jax.ShapeDtypeStruct((groups, tok_count + EXTRA, model_width // groups), jnp.bfloat16),
        *[jax.ShapeDtypeStruct((part, 2 * model_width), jnp.bfloat16) for part in parts],
    )
    return pl.pallas_call(
        route_kernel,
        out_shape=out_shape,
        compiler_params=VMEM,
        cost_estimate=cost(),
    )(expert_ids.T, gates.T, spread, tokens, grad_out)


def slices_kernel(top_k, spread_ref, *refs):
    out_refs, refs = refs[-CHUNKS:], refs[:-CHUNKS]
    for s, x_ref in enumerate(refs):
        tok_count, width = x_ref.shape[0] - EXTRA, x_ref.shape[1]
        tail = x_ref[tok_count:, :tok_count].astype(jnp.float32).astype(jnp.int32)
        matches = match_rows([tail[k : k + 1, :] for k in range(top_k)])
        chosen = chosen_slots(matches, spread_ref[...])
        place = jnp.where(chosen, 1.0, 0.0).astype(jnp.bfloat16)
        done = 0
        for out_ref in out_refs:
            rows = slice(done, done + out_ref.shape[0])
            done = rows.stop
            out_ref[:, s * width : (s + 1) * width] = jnp.dot(
                place[rows],
                x_ref[:tok_count, :],
                preferred_element_type=jnp.float32,
            ).astype(jnp.bfloat16)


def place_slices(received, top_k, spread, parts):
    wide = len(received) * received[0].shape[1]
    return pl.pallas_call(
        functools.partial(slices_kernel, top_k),
        out_shape=[jax.ShapeDtypeStruct((part, wide), jnp.bfloat16) for part in parts],
        compiler_params=VMEM,
        cost_estimate=cost(),
    )(spread, *received)


def down_kernel(chunks, *refs):
    out_ref = refs[-1]
    total = 0.0
    for hidden_ref, ge_ref in zip(refs[:chunks], refs[chunks:-1]):
        total += contract_rows(hidden_ref[...], ge_ref[...])
    out_ref[...] = total.astype(jnp.bfloat16)


def down_rows(hiddens, rows):
    hidden_width = hiddens[0].shape[1]
    model_width = rows[0].shape[1] // 2
    tile = 256
    return pl.pallas_call(
        functools.partial(down_kernel, len(rows)),
        grid=(hidden_width // tile,),
        in_specs=[pl.BlockSpec((each.shape[0], tile), lambda i: (0, i)) for each in hiddens]
        + [pl.BlockSpec((each.shape[0], model_width), lambda i: (0, 1)) for each in rows],
        out_specs=pl.BlockSpec((tile, model_width), lambda i: (i, 0)),
        out_shape=jax.ShapeDtypeStruct((hidden_width, model_width), jnp.bfloat16),
        compiler_params=VMEM,
        cost_estimate=cost(20_000_000_000),
    )(*hiddens, *rows)


def weight_kernel(terms, _, *refs):
    for which, out_ref in enumerate(refs[-2:]):
        total = 0.0
        for t in range(terms):
            grads = refs[terms + t]
            grad = grads[0, which] if len(grads.shape) == 4 else grads[which]
            total += contract_rows(refs[t][...], grad)
        out_ref[0] = total


def weight_rows(terms, model_width, groups):
    hidden_width = terms[0][3].shape[-1]
    width = model_width // groups
    tile = 256

    def grads_spec(s, grads):
        if grads.ndim == 3:
            return pl.BlockSpec((*grads.shape[:2], tile), lambda i, z: (0, 0, i))
        return pl.BlockSpec(
            (1, *grads.shape[1:3], tile),
            lambda i, z: (lax.rem(z[0] + groups - s, groups), 0, 0, i),
        )

    whole = pl.BlockSpec((1, width, tile), lambda i, z: (0, 0, i))
    out_shape = jax.ShapeDtypeStruct((1, width, hidden_width), jnp.float32)
    return pl.pallas_call(
        functools.partial(weight_kernel, len(terms)),
        grid_spec=pltpu.PrefetchScalarGridSpec(
            num_scalar_prefetch=1,
            grid=(hidden_width // tile,),
            in_specs=[
                pl.BlockSpec((rows.shape[0], width), lambda i, z, at=(2 * c + 1) * groups + s: (0, at))
                for rows, c, s, _ in terms
            ]
            + [grads_spec(s, grads) for _, _, s, grads in terms],
            out_specs=(whole, whole),
        ),
        out_shape=(out_shape, out_shape),
        compiler_params=VMEM,
        cost_estimate=cost(),
    )(
        lax.axis_index("dp").astype(jnp.int32)[None],
        *[rows for rows, _, _, _ in terms],
        *[grads for _, _, _, grads in terms],
    )


def expert_kernel(rows_ref, gate_ref, up_ref, down_ref, hidden_ref, grads_ref, tail_ref, sum_ref):
    model_width = rows_ref.shape[1] // 2
    step = pl.program_id(0)
    rows_x = rows_ref[:, :model_width]
    pre_gate = jnp.dot(rows_x, gate_ref[0], preferred_element_type=jnp.float32)
    pre_up = jnp.dot(rows_x, up_ref[0], preferred_element_type=jnp.float32)
    grad_hidden = contract_last(rows_ref[:, model_width:], down_ref[0])
    sigmoid_v = 1.0 / (1.0 + jnp.exp(-pre_gate))
    activated = pre_gate * sigmoid_v
    derivative = sigmoid_v * (1.0 + pre_gate * (1.0 - sigmoid_v))
    hidden = (activated * pre_up).astype(jnp.bfloat16)
    hidden_ref[...] = hidden
    grads_ref[0] = (grad_hidden * pre_up * derivative).astype(jnp.bfloat16)
    grads_ref[1] = (grad_hidden * activated).astype(jnp.bfloat16)
    gate_grad = jnp.sum(hidden.astype(jnp.float32) * grad_hidden, axis=1, keepdims=True)

    @pl.when(step == 0)
    def _():
        sum_ref[...] = jnp.zeros_like(sum_ref)

    sum_ref[...] += gate_grad

    @pl.when(step == pl.num_programs(0) - 1)
    def _():
        total = sum_ref[...]
        coarse = total.astype(jnp.bfloat16).astype(jnp.float32)
        lane = lax.broadcasted_iota(jnp.int32, total.shape, 1)
        tail = jnp.where(lane == 0, coarse, jnp.where(lane == 1, total - coarse, 0.0))
        tail_ref[...] = tail.astype(jnp.bfloat16)


def expert_rows(rows, gate_weight, up_weight, down_weight):
    count, wide = rows.shape
    _, model_width, hidden_width = gate_weight.shape
    tile = 256
    out_shape = (
        jax.ShapeDtypeStruct((count, hidden_width), jnp.bfloat16),
        jax.ShapeDtypeStruct((2, count, hidden_width), jnp.bfloat16),
        jax.ShapeDtypeStruct((count, LANES), jnp.bfloat16),
    )
    return pl.pallas_call(
        expert_kernel,
        grid=(hidden_width // tile,),
        in_specs=[
            pl.BlockSpec((count, wide), lambda i: (0, 0)),
            pl.BlockSpec((1, model_width, tile), lambda i: (0, 0, i)),
            pl.BlockSpec((1, model_width, tile), lambda i: (0, 0, i)),
            pl.BlockSpec((1, tile, model_width), lambda i: (0, i, 0)),
        ],
        out_specs=(
            pl.BlockSpec((count, tile), lambda i: (0, i)),
            pl.BlockSpec((2, count, tile), lambda i: (0, 0, i)),
            pl.BlockSpec((count, LANES), lambda i: (0, 0)),
        ),
        out_shape=out_shape,
        scratch_shapes=[pltpu.VMEM((count, LANES), jnp.float32)],
        compiler_params=VMEM,
        cost_estimate=cost(),
    )(rows, gate_weight, up_weight, down_weight)


def back_kernel(chunk, tiles, grads_ref, slices_ref, *refs):
    step = pl.program_id(0)
    tails, (gate_ref, up_ref), out_ref = refs[: chunk + 1], refs[chunk + 1 : chunk + 3], refs[-1]

    @pl.when(step < tiles)
    def _():
        row = contract_last(grads_ref[0], gate_ref[0]) + contract_last(grads_ref[1], up_ref[0])
        out_ref[...] = row.astype(jnp.bfloat16)

    @pl.when((step >= tiles) & (step < 2 * tiles))
    def _():
        out_ref[...] = slices_ref[...]

    @pl.when(step == 2 * tiles)
    def _():
        out_ref[...] = jnp.zeros_like(out_ref)
        for c, tail_ref in enumerate(tails):
            out_ref[:, c * LANES : (c + 1) * LANES] = tail_ref[...]


def back_rows(grads, tails, slices, gate_weight, up_weight, before):
    chunk = len(before)
    _, count, hidden_width = grads.shape
    model_width = gate_weight.shape[1]
    tile = 512
    tiles = model_width // tile
    last = chunk == CHUNKS - 1
    weight = pl.BlockSpec((1, tile, hidden_width), lambda i: (0, jnp.minimum(i, tiles - 1), 0))
    return pl.pallas_call(
        functools.partial(back_kernel, chunk, tiles),
        grid=(2 * tiles + last,),
        in_specs=[
            pl.BlockSpec((2, count, hidden_width), lambda i: (0, 0, 0)),
            pl.BlockSpec((count, tile), lambda i: (0, jnp.clip(i - tiles, 0, tiles - 1))),
            *[pl.BlockSpec((count, LANES), lambda i: (0, 0)) for _ in tails],
            weight,
            weight,
            *[pl.BlockSpec(memory_space=pl.ANY) for _ in before[-1:]],
        ],
        out_specs=pl.BlockSpec(
            (count, tile), lambda i: (0, jnp.where(i < 2 * tiles, 2 * tiles * chunk + i, 2 * tiles * CHUNKS))
        ),
        out_shape=jax.ShapeDtypeStruct((count, 2 * CHUNKS * model_width + tile), jnp.bfloat16),
        input_output_aliases={4 + len(tails): 0} if before else {},
        compiler_params=VMEM,
        cost_estimate=cost(),
    )(grads, slices, *tails, gate_weight, up_weight, *before[-1:])


def exchange_groups(grads, partial, groups, early, back):
    z = lax.axis_index("dp")
    depth = partial.shape[0] // groups

    def block(index):
        index = jnp.clip(index, 0, groups - 1)
        return lax.dynamic_slice_in_dim(partial, index * depth, depth, 0)

    def total(sent, index):
        return (sent.astype(jnp.float32) + block(index).astype(jnp.float32)).astype(jnp.bfloat16)

    below, above = [grads], [grads]
    rising = falling = None
    for step in range(1, groups + 1):
        sums = step - 1
        pair = None
        if sums == 1:
            pair = (partial[-depth:], partial[:depth])
        elif sums > 1:
            pair = (total(rising, z + groups - sums), total(falling, z - groups + sums))
        if step < groups:
            if pair:
                tied = (below[-1], above[-1], pair, early)
                below[-1], above[-1], pair, early = lax.optimization_barrier(tied)
            lifts = [(i, i + 1) for i in range(step - 1, groups - 1)]
            drops = [(i + 1, i) for i in range(groups - step)]
            below.append(lax.ppermute(below[-1], "dp", lifts))
            above.append(lax.ppermute(above[-1], "dp", drops))
        else:
            tied = (below[-1], above[-1], pair, back)
            below[-1], above[-1], pair, back = lax.optimization_barrier(tied)
        if pair:
            rising = lax.ppermute(pair[0], "dp", [(i, i + 1) for i in range(sums)])
            falling = lax.ppermute(pair[1], "dp", [(i, i - 1) for i in range(groups - sums, groups)])
    summed = block(z).astype(jnp.float32) + rising.astype(jnp.float32) + falling.astype(jnp.float32)
    return early, back, below, above, summed


def local(tokens, grad_out, expert_ids, gates, gate_weight, up_weight, down_weight):
    experts = lax.axis_size("expert")
    groups = lax.axis_size("dp")
    tok_count, top_k = expert_ids.shape
    model_width = tokens.shape[1]
    capacity = 3 * tok_count * top_k // (2 * experts)
    parts = [experts * len(own) for own in chunk_ranks(capacity)]
    expert_at, spread = slot_tables(experts, capacity)
    z = lax.axis_index("dp")

    def exchange(rows):
        return lax.all_to_all(
            rows.reshape(experts, -1, rows.shape[1]),
            "expert",
            split_axis=0,
            concat_axis=0,
            tiled=True,
        ).reshape(rows.shape)

    place, slices, *send = route(expert_ids, gates, tokens, grad_out, spread, parts, groups)

    received = [lax.dynamic_index_in_dim(slices, z, 0, keepdims=False)]
    for shift in range(1, groups):
        mine = lax.dynamic_index_in_dim(slices, lax.rem(z + shift, groups), 0, keepdims=False)
        ring = [(i, (i + shift) % groups) for i in range(groups)]
        received.append(lax.ppermute(mine, "dp", ring))

    rows, hiddens, grads, tails, gathered, backs = [], [], [], [], [], []
    for c in range(CHUNKS):
        if c == 1:
            send[c], received = lax.optimization_barrier((send[c], received))
        rows.append(exchange(send[c]))
        if c == 0:
            send_slices = place_slices(received, top_k, spread, parts)
        else:
            rows[c], backs[-1] = lax.optimization_barrier((rows[c], backs[-1]))
        hidden, grad, tail = expert_rows(rows[c], gate_weight, up_weight, down_weight)
        hiddens.append(hidden)
        grads.append(grad)
        tails.append(tail)
        if c < CHUNKS - 1:
            gathered.append(lax.all_gather(grad, "dp"))
        backs.append(back_rows(grad, tails, send_slices[c], gate_weight, up_weight, backs))
    down_partial = down_rows(hiddens, rows)
    back = exchange(backs[-1])

    gathered, back, below, above, grad_down_w = exchange_groups(
        grads[-1], down_partial, groups, gathered, back
    )
    terms = [(back, c, s, each) for c, each in enumerate(gathered) for s in range(groups)]
    for s in range(groups):
        terms.append((back, CHUNKS - 1, s, below[s]))
        if s:
            terms.append((back, CHUNKS - 1, s, above[groups - s]))
    grad_w = weight_rows(terms, model_width, groups)

    grad_tokens, scaled, done = 0.0, [], 0
    for c, part in enumerate(parts):
        at = slice(done, done + part)
        done = at.stop
        first = 2 * c * model_width
        grad_tokens += contract_rows(place[at], back[:, first : first + model_width])
        first = 2 * CHUNKS * model_width + c * LANES
        pair = back[:, first : first + 2].astype(jnp.float32)
        scaled.append(pair[:, 0] + pair[:, 1])
    grad_tokens = grad_tokens.astype(jnp.bfloat16)
    scaled = jnp.concatenate(scaled)[:, None]
    gate_b = gates.T.astype(jnp.bfloat16).astype(jnp.float32)
    grad_gates = []
    for k in range(top_k):
        hit = (expert_ids[:, k][None, :] == expert_at[:, None]) & (place > 0)
        grad_gates.append(jnp.sum(jnp.where(hit, scaled, 0.0), axis=0) / gate_b[k])
    grad_gates = jnp.stack(grad_gates).astype(jnp.bfloat16).T

    return (grad_tokens, grad_gates, *grad_w, grad_down_w[None])


def solution(mesh):
    placed = (
        P(("dp", "expert"), None),
        P(("dp", "expert"), None),
        P(("dp", "expert"), None),
        P(("dp", "expert"), None),
        P("expert", None, None),
        P("expert", None, None),
        P("expert", None, None),
    )
    return jax.shard_map(
        local,
        mesh=mesh,
        in_specs=placed,
        out_specs=(
            P(("dp", "expert"), None),
            P(("dp", "expert"), None),
            P("expert", "dp", None),
            P("expert", "dp", None),
            P("expert", "dp", None),
        ),
        check_vma=False,
    )
```

```python
import functools

import jax
import jax.numpy as jnp
import numpy as np
from jax import lax
from jax.experimental import pallas as pl
from jax.experimental.pallas import tpu as pltpu
from jax.sharding import PartitionSpec as P

LANES = 128
EXTRA = 16
CHUNKS = 1
VMEM = pltpu.CompilerParams(vmem_limit_bytes=62 * 1024 * 1024)


def contract_rows(left, right):
    return lax.dot_general(
        left, right, (((0,), (0,)), ((), ())), preferred_element_type=jnp.float32
    )


def contract_last(left, right):
    return lax.dot_general(
        left, right, (((1,), (1,)), ((), ())), preferred_element_type=jnp.float32
    )


def cost(flops=1024):
    return pl.CostEstimate(flops=flops, bytes_accessed=1024, transcendentals=0)


def chunk_ranks(capacity):
    edges = [capacity * c // CHUNKS for c in range(CHUNKS + 1)]
    return [np.arange(first, last) for first, last in zip(edges, edges[1:])]


def slot_tables(experts, capacity):
    ranks = chunk_ranks(capacity)
    rank_at = np.concatenate([np.tile(own, experts) for own in ranks])
    expert_at = np.concatenate([np.repeat(np.arange(experts), len(own)) for own in ranks])
    spread = (expert_at[:, None] == np.arange(LANES)[None, :]).astype(np.float32)
    spread[:, -1] = -rank_at
    return expert_at.astype(np.int32), jnp.asarray(spread, jnp.bfloat16)


def match_rows(id_rows):
    expert_of = lax.broadcasted_iota(jnp.int32, (LANES, id_rows[0].shape[1]), 0)
    return [each == expert_of for each in id_rows]


def chosen_slots(matches, spread):
    tok_count = matches[0].shape[1]
    named = functools.reduce(jnp.logical_or, matches)
    row = lax.broadcasted_iota(jnp.int32, (tok_count, tok_count), 0)
    col = lax.broadcasted_iota(jnp.int32, (tok_count, tok_count), 1)
    after = jnp.where(row < col, 1.0, 0.0).astype(jnp.bfloat16)
    earlier = jnp.dot(
        jnp.where(named, 1.0, 0.0).astype(jnp.bfloat16), after, preferred_element_type=jnp.float32
    )
    last = lax.broadcasted_iota(jnp.int32, named.shape, 0) == LANES - 1
    key = jnp.where(last, 1.0, jnp.where(named, earlier, -1.0)).astype(jnp.bfloat16)
    return jnp.dot(spread, key, preferred_element_type=jnp.float32) == 0.0


def route_kernel(ids_ref, gates_ref, spread_ref, x_ref, go_ref, place_ref, slices_ref, *send_refs):
    tok_count, model_width = x_ref.shape
    groups = slices_ref.shape[0]
    id_rows = [ids_ref[k : k + 1, :] for k in range(ids_ref.shape[0])]
    spread = spread_ref[...]
    matches = match_rows(id_rows)
    chosen = chosen_slots(matches, spread)
    gate_of = jnp.zeros(matches[0].shape, jnp.float32)
    for k, match in enumerate(matches):
        gate_of = jnp.where(match, gates_ref[k : k + 1, :], gate_of)
    gate_at = jnp.dot(spread, gate_of.astype(jnp.bfloat16), preferred_element_type=jnp.float32)
    place = jnp.where(chosen, 1.0, 0.0).astype(jnp.bfloat16)
    weigh = jnp.where(chosen, gate_at, 0.0).astype(jnp.bfloat16)
    place_ref[...] = place
    width = 512
    done = 0
    for send_ref in send_refs:
        rows = slice(done, done + send_ref.shape[0])
        done = rows.stop
        for at in range(0, model_width, width):
            cols = slice(at, at + width)
            right = slice(model_width + at, model_width + at + width)
            send_ref[:, cols] = jnp.dot(
                place[rows], x_ref[:, cols], preferred_element_type=jnp.float32
            ).astype(jnp.bfloat16)
            send_ref[:, right] = jnp.dot(
                weigh[rows], go_ref[:, cols], preferred_element_type=jnp.float32
            ).astype(jnp.bfloat16)
    share = model_width // groups
    line = lax.broadcasted_iota(jnp.int32, (EXTRA, tok_count), 0)
    tail = jnp.zeros((EXTRA, tok_count), jnp.float32)
    for k, each in enumerate(id_rows):
        tail = jnp.where(line == k, each.astype(jnp.float32), tail)
    for g in range(groups):
        slices_ref[g, :tok_count, :] = x_ref[:, g * share : (g + 1) * share]
        slices_ref[g, tok_count:, :] = jnp.zeros((EXTRA, share), jnp.bfloat16)
        slices_ref[g, tok_count:, :tok_count] = tail.astype(jnp.bfloat16)


def route(expert_ids, gates, tokens, grad_out, spread, parts, groups):
    tok_count, model_width = tokens.shape
    slots = spread.shape[0]
    out_shape = (
        jax.ShapeDtypeStruct((slots, tok_count), jnp.bfloat16),
        jax.ShapeDtypeStruct((groups, tok_count + EXTRA, model_width // groups), jnp.bfloat16),
        *[jax.ShapeDtypeStruct((part, 2 * model_width), jnp.bfloat16) for part in parts],
    )
    return pl.pallas_call(
        route_kernel,
        out_shape=out_shape,
        compiler_params=VMEM,
        cost_estimate=cost(),
    )(expert_ids.T, gates.T, spread, tokens, grad_out)


def slices_kernel(top_k, spread_ref, *refs):
    out_refs, refs = refs[-CHUNKS:], refs[:-CHUNKS]
    for s, x_ref in enumerate(refs):
        tok_count, width = x_ref.shape[0] - EXTRA, x_ref.shape[1]
        tail = x_ref[tok_count:, :tok_count].astype(jnp.float32).astype(jnp.int32)
        matches = match_rows([tail[k : k + 1, :] for k in range(top_k)])
        chosen = chosen_slots(matches, spread_ref[...])
        place = jnp.where(chosen, 1.0, 0.0).astype(jnp.bfloat16)
        done = 0
        for out_ref in out_refs:
            rows = slice(done, done + out_ref.shape[0])
            done = rows.stop
            out_ref[:, s * width : (s + 1) * width] = jnp.dot(
                place[rows],
                x_ref[:tok_count, :],
                preferred_element_type=jnp.float32,
            ).astype(jnp.bfloat16)


def place_slices(received, top_k, spread, parts):
    wide = len(received) * received[0].shape[1]
    return pl.pallas_call(
        functools.partial(slices_kernel, top_k),
        out_shape=[jax.ShapeDtypeStruct((part, wide), jnp.bfloat16) for part in parts],
        compiler_params=VMEM,
        cost_estimate=cost(),
    )(spread, *received)


def down_kernel(chunks, *refs):
    out_ref = refs[-1]
    total = 0.0
    for hidden_ref, ge_ref in zip(refs[:chunks], refs[chunks:-1]):
        total += contract_rows(hidden_ref[...], ge_ref[...])
    out_ref[...] = total.astype(jnp.bfloat16)


def down_rows(hiddens, rows):
    hidden_width = hiddens[0].shape[1]
    model_width = rows[0].shape[1] // 2
    tile = 256
    return pl.pallas_call(
        functools.partial(down_kernel, len(rows)),
        grid=(hidden_width // tile,),
        in_specs=[pl.BlockSpec((each.shape[0], tile), lambda i: (0, i)) for each in hiddens]
        + [pl.BlockSpec((each.shape[0], model_width), lambda i: (0, 1)) for each in rows],
        out_specs=pl.BlockSpec((tile, model_width), lambda i: (i, 0)),
        out_shape=jax.ShapeDtypeStruct((hidden_width, model_width), jnp.bfloat16),
        compiler_params=VMEM,
        cost_estimate=cost(),
    )(*hiddens, *rows)


def weight_kernel(terms, _, *refs):
    for which, out_ref in enumerate(refs[-2:]):
        total = 0.0
        for t in range(terms):
            grads = refs[terms + t]
            grad = grads[0, which] if len(grads.shape) == 4 else grads[which]
            total += contract_rows(refs[t][...], grad)
        out_ref[0] = total


def weight_rows(terms, model_width, groups):
    hidden_width = terms[0][3].shape[-1]
    width = model_width // groups
    tile = 256

    def grads_spec(s, grads):
        if grads.ndim == 3:
            return pl.BlockSpec((*grads.shape[:2], tile), lambda i, z: (0, 0, i))
        return pl.BlockSpec(
            (1, *grads.shape[1:3], tile),
            lambda i, z: (lax.rem(z[0] + groups - s, groups), 0, 0, i),
        )

    whole = pl.BlockSpec((1, width, tile), lambda i, z: (0, 0, i))
    out_shape = jax.ShapeDtypeStruct((1, width, hidden_width), jnp.float32)
    return pl.pallas_call(
        functools.partial(weight_kernel, len(terms)),
        grid_spec=pltpu.PrefetchScalarGridSpec(
            num_scalar_prefetch=1,
            grid=(hidden_width // tile,),
            in_specs=[
                pl.BlockSpec((rows.shape[0], width), lambda i, z, at=(2 * c + 1) * groups + s: (0, at))
                for rows, c, s, _ in terms
            ]
            + [grads_spec(s, grads) for _, _, s, grads in terms],
            out_specs=(whole, whole),
        ),
        out_shape=(out_shape, out_shape),
        compiler_params=VMEM,
        cost_estimate=cost(),
    )(
        lax.axis_index("dp").astype(jnp.int32)[None],
        *[rows for rows, _, _, _ in terms],
        *[grads for _, _, _, grads in terms],
    )


def expert_kernel(rows_ref, gate_ref, up_ref, down_ref, hidden_ref, grads_ref, tail_ref, sum_ref):
    model_width = rows_ref.shape[1] // 2
    step = pl.program_id(0)
    rows_x = rows_ref[:, :model_width]
    pre_gate = jnp.dot(rows_x, gate_ref[0], preferred_element_type=jnp.float32)
    pre_up = jnp.dot(rows_x, up_ref[0], preferred_element_type=jnp.float32)
    grad_hidden = contract_last(rows_ref[:, model_width:], down_ref[0])
    sigmoid_v = 1.0 / (1.0 + jnp.exp(-pre_gate))
    activated = pre_gate * sigmoid_v
    derivative = sigmoid_v * (1.0 + pre_gate * (1.0 - sigmoid_v))
    hidden = (activated * pre_up).astype(jnp.bfloat16)
    hidden_ref[...] = hidden
    grads_ref[0] = (grad_hidden * pre_up * derivative).astype(jnp.bfloat16)
    grads_ref[1] = (grad_hidden * activated).astype(jnp.bfloat16)
    gate_grad = jnp.sum(hidden.astype(jnp.float32) * grad_hidden, axis=1, keepdims=True)

    @pl.when(step == 0)
    def _():
        sum_ref[...] = jnp.zeros_like(sum_ref)

    sum_ref[...] += gate_grad

    @pl.when(step == pl.num_programs(0) - 1)
    def _():
        total = sum_ref[...]
        coarse = total.astype(jnp.bfloat16).astype(jnp.float32)
        lane = lax.broadcasted_iota(jnp.int32, total.shape, 1)
        tail = jnp.where(lane == 0, coarse, jnp.where(lane == 1, total - coarse, 0.0))
        tail_ref[...] = tail.astype(jnp.bfloat16)


def expert_rows(rows, gate_weight, up_weight, down_weight):
    count, wide = rows.shape
    _, model_width, hidden_width = gate_weight.shape
    tile = 256
    out_shape = (
        jax.ShapeDtypeStruct((count, hidden_width), jnp.bfloat16),
        jax.ShapeDtypeStruct((2, count, hidden_width), jnp.bfloat16),
        jax.ShapeDtypeStruct((count, LANES), jnp.bfloat16),
    )
    return pl.pallas_call(
        expert_kernel,
        grid=(hidden_width // tile,),
        in_specs=[
            pl.BlockSpec((count, wide), lambda i: (0, 0)),
            pl.BlockSpec((1, model_width, tile), lambda i: (0, 0, i)),
            pl.BlockSpec((1, model_width, tile), lambda i: (0, 0, i)),
            pl.BlockSpec((1, tile, model_width), lambda i: (0, i, 0)),
        ],
        out_specs=(
            pl.BlockSpec((count, tile), lambda i: (0, i)),
            pl.BlockSpec((2, count, tile), lambda i: (0, 0, i)),
            pl.BlockSpec((count, LANES), lambda i: (0, 0)),
        ),
        out_shape=out_shape,
        scratch_shapes=[pltpu.VMEM((count, LANES), jnp.float32)],
        compiler_params=VMEM,
        cost_estimate=cost(),
    )(rows, gate_weight, up_weight, down_weight)


def back_kernel(chunk, tiles, grads_ref, slices_ref, *refs):
    step = pl.program_id(0)
    tails, (gate_ref, up_ref), out_ref = refs[: chunk + 1], refs[chunk + 1 : chunk + 3], refs[-1]

    @pl.when(step < tiles)
    def _():
        row = contract_last(grads_ref[0], gate_ref[0]) + contract_last(grads_ref[1], up_ref[0])
        out_ref[...] = row.astype(jnp.bfloat16)

    @pl.when((step >= tiles) & (step < 2 * tiles))
    def _():
        out_ref[...] = slices_ref[...]

    @pl.when(step == 2 * tiles)
    def _():
        out_ref[...] = jnp.zeros_like(out_ref)
        for c, tail_ref in enumerate(tails):
            out_ref[:, c * LANES : (c + 1) * LANES] = tail_ref[...]


def back_rows(grads, tails, slices, gate_weight, up_weight, before):
    chunk = len(before)
    _, count, hidden_width = grads.shape
    model_width = gate_weight.shape[1]
    tile = 512
    tiles = model_width // tile
    last = chunk == CHUNKS - 1
    weight = pl.BlockSpec((1, tile, hidden_width), lambda i: (0, jnp.minimum(i, tiles - 1), 0))
    return pl.pallas_call(
        functools.partial(back_kernel, chunk, tiles),
        grid=(2 * tiles + last,),
        in_specs=[
            pl.BlockSpec((2, count, hidden_width), lambda i: (0, 0, 0)),
            pl.BlockSpec((count, tile), lambda i: (0, jnp.clip(i - tiles, 0, tiles - 1))),
            *[pl.BlockSpec((count, LANES), lambda i: (0, 0)) for _ in tails],
            weight,
            weight,
            *[pl.BlockSpec(memory_space=pl.ANY) for _ in before[-1:]],
        ],
        out_specs=pl.BlockSpec(
            (count, tile), lambda i: (0, jnp.where(i < 2 * tiles, 2 * tiles * chunk + i, 2 * tiles * CHUNKS))
        ),
        out_shape=jax.ShapeDtypeStruct((count, 2 * CHUNKS * model_width + tile), jnp.bfloat16),
        input_output_aliases={4 + len(tails): 0} if before else {},
        compiler_params=VMEM,
        cost_estimate=cost(),
    )(grads, slices, *tails, gate_weight, up_weight, *before[-1:])


def exchange_groups(grads, partial, groups, early, back):
    z = lax.axis_index("dp")
    depth = partial.shape[0] // groups

    def block(index):
        index = jnp.clip(index, 0, groups - 1)
        return lax.dynamic_slice_in_dim(partial, index * depth, depth, 0)

    def total(sent, index):
        return (sent.astype(jnp.float32) + block(index).astype(jnp.float32)).astype(jnp.bfloat16)

    below, above = [grads], [grads]
    rising = falling = None
    for step in range(1, groups + 1):
        sums = step - 1
        pair = None
        if sums == 1:
            pair = (partial[-depth:], partial[:depth])
        elif sums > 1:
            pair = (total(rising, z + groups - sums), total(falling, z - groups + sums))
        if step < groups:
            if pair:
                tied = (below[-1], above[-1], pair, early)
                below[-1], above[-1], pair, early = lax.optimization_barrier(tied)
            lifts = [(i, i + 1) for i in range(step - 1, groups - 1)]
            drops = [(i + 1, i) for i in range(groups - step)]
            below.append(lax.ppermute(below[-1], "dp", lifts))
            above.append(lax.ppermute(above[-1], "dp", drops))
        else:
            tied = (below[-1], above[-1], pair, back)
            below[-1], above[-1], pair, back = lax.optimization_barrier(tied)
        if pair:
            rising = lax.ppermute(pair[0], "dp", [(i, i + 1) for i in range(sums)])
            falling = lax.ppermute(pair[1], "dp", [(i, i - 1) for i in range(groups - sums, groups)])
    summed = block(z).astype(jnp.float32) + rising.astype(jnp.float32) + falling.astype(jnp.float32)
    return early, back, below, above, summed


def local(tokens, grad_out, expert_ids, gates, gate_weight, up_weight, down_weight):
    experts = lax.axis_size("expert")
    groups = lax.axis_size("dp")
    tok_count, top_k = expert_ids.shape
    model_width = tokens.shape[1]
    capacity = 3 * tok_count * top_k // (2 * experts)
    parts = [experts * len(own) for own in chunk_ranks(capacity)]
    expert_at, spread = slot_tables(experts, capacity)
    z = lax.axis_index("dp")

    def exchange(rows):
        return lax.all_to_all(
            rows.reshape(experts, -1, rows.shape[1]),
            "expert",
            split_axis=0,
            concat_axis=0,
            tiled=True,
        ).reshape(rows.shape)

    place, slices, *send = route(expert_ids, gates, tokens, grad_out, spread, parts, groups)

    received = [lax.dynamic_index_in_dim(slices, z, 0, keepdims=False)]
    for shift in range(1, groups):
        mine = lax.dynamic_index_in_dim(slices, lax.rem(z + shift, groups), 0, keepdims=False)
        ring = [(i, (i + shift) % groups) for i in range(groups)]
        received.append(lax.ppermute(mine, "dp", ring))

    rows, hiddens, grads, tails, gathered, backs = [], [], [], [], [], []
    for c in range(CHUNKS):
        if c == 1:
            send[c], received = lax.optimization_barrier((send[c], received))
        rows.append(exchange(send[c]))
        if c == 0:
            send_slices = place_slices(received, top_k, spread, parts)
        if CHUNKS == 1:
            rows[c], send_slices = lax.optimization_barrier((rows[c], send_slices))
        else:
            rows[c], backs[-1] = lax.optimization_barrier((rows[c], backs[-1]))
        hidden, grad, tail = expert_rows(rows[c], gate_weight, up_weight, down_weight)
        hiddens.append(hidden)
        grads.append(grad)
        tails.append(tail)
        if c < CHUNKS - 1:
            gathered.append(lax.all_gather(grad, "dp"))
        backs.append(back_rows(grad, tails, send_slices[c], gate_weight, up_weight, backs))
    down_partial = down_rows(hiddens, rows)
    back = exchange(backs[-1])

    gathered, back, below, above, grad_down_w = exchange_groups(
        grads[-1], down_partial, groups, gathered, back
    )
    terms = [(back, c, s, each) for c, each in enumerate(gathered) for s in range(groups)]
    for s in range(groups):
        terms.append((back, CHUNKS - 1, s, below[s]))
        if s:
            terms.append((back, CHUNKS - 1, s, above[groups - s]))
    grad_w = weight_rows(terms, model_width, groups)

    grad_tokens, scaled, done = 0.0, [], 0
    for c, part in enumerate(parts):
        at = slice(done, done + part)
        done = at.stop
        first = 2 * c * model_width
        grad_tokens += contract_rows(place[at], back[:, first : first + model_width])
        first = 2 * CHUNKS * model_width + c * LANES
        pair = back[:, first : first + 2].astype(jnp.float32)
        scaled.append(pair[:, 0] + pair[:, 1])
    grad_tokens = grad_tokens.astype(jnp.bfloat16)
    scaled = jnp.concatenate(scaled)[:, None]
    gate_b = gates.T.astype(jnp.bfloat16).astype(jnp.float32)
    grad_gates = []
    for k in range(top_k):
        hit = (expert_ids[:, k][None, :] == expert_at[:, None]) & (place > 0)
        grad_gates.append(jnp.sum(jnp.where(hit, scaled, 0.0), axis=0) / gate_b[k])
    grad_gates = jnp.stack(grad_gates).astype(jnp.bfloat16).T

    return (grad_tokens, grad_gates, *grad_w, grad_down_w[None])


def solution(mesh):
    placed = (
        P(("dp", "expert"), None),
        P(("dp", "expert"), None),
        P(("dp", "expert"), None),
        P(("dp", "expert"), None),
        P("expert", None, None),
        P("expert", None, None),
        P("expert", None, None),
    )
    return jax.shard_map(
        local,
        mesh=mesh,
        in_specs=placed,
        out_specs=(
            P(("dp", "expert"), None),
            P(("dp", "expert"), None),
            P("expert", "dp", None),
            P("expert", "dp", None),
            P("expert", "dp", None),
        ),
        check_vma=False,
    )
```

```python
import functools

import jax
import jax.numpy as jnp
import numpy as np
from jax import lax
from jax.experimental import pallas as pl
from jax.experimental.pallas import tpu as pltpu
from jax.sharding import PartitionSpec as P

LANES = 128
EXTRA = 16
CHUNKS = 1
VMEM = pltpu.CompilerParams(vmem_limit_bytes=62 * 1024 * 1024)


def contract_rows(left, right):
    return lax.dot_general(
        left, right, (((0,), (0,)), ((), ())), preferred_element_type=jnp.float32
    )


def contract_last(left, right):
    return lax.dot_general(
        left, right, (((1,), (1,)), ((), ())), preferred_element_type=jnp.float32
    )


def cost(flops=1024):
    return pl.CostEstimate(flops=flops, bytes_accessed=1024, transcendentals=0)


def chunk_ranks(capacity):
    edges = [capacity * c // CHUNKS for c in range(CHUNKS + 1)]
    return [np.arange(first, last) for first, last in zip(edges, edges[1:])]


def slot_tables(experts, capacity):
    ranks = chunk_ranks(capacity)
    rank_at = np.concatenate([np.tile(own, experts) for own in ranks])
    expert_at = np.concatenate([np.repeat(np.arange(experts), len(own)) for own in ranks])
    spread = (expert_at[:, None] == np.arange(LANES)[None, :]).astype(np.float32)
    spread[:, -1] = -rank_at
    return expert_at.astype(np.int32), jnp.asarray(spread, jnp.bfloat16)


def match_rows(id_rows):
    expert_of = lax.broadcasted_iota(jnp.int32, (LANES, id_rows[0].shape[1]), 0)
    return [each == expert_of for each in id_rows]


def chosen_slots(matches, spread):
    tok_count = matches[0].shape[1]
    named = functools.reduce(jnp.logical_or, matches)
    row = lax.broadcasted_iota(jnp.int32, (tok_count, tok_count), 0)
    col = lax.broadcasted_iota(jnp.int32, (tok_count, tok_count), 1)
    after = jnp.where(row < col, 1.0, 0.0).astype(jnp.bfloat16)
    earlier = jnp.dot(
        jnp.where(named, 1.0, 0.0).astype(jnp.bfloat16), after, preferred_element_type=jnp.float32
    )
    last = lax.broadcasted_iota(jnp.int32, named.shape, 0) == LANES - 1
    key = jnp.where(last, 1.0, jnp.where(named, earlier, -1.0)).astype(jnp.bfloat16)
    return jnp.dot(spread, key, preferred_element_type=jnp.float32) == 0.0


def route_kernel(ids_ref, gates_ref, spread_ref, x_ref, go_ref, place_ref, slices_ref, *send_refs):
    tok_count, model_width = x_ref.shape
    groups = slices_ref.shape[0]
    id_rows = [ids_ref[k : k + 1, :] for k in range(ids_ref.shape[0])]
    spread = spread_ref[...]
    matches = match_rows(id_rows)
    chosen = chosen_slots(matches, spread)
    gate_of = jnp.zeros(matches[0].shape, jnp.float32)
    for k, match in enumerate(matches):
        gate_of = jnp.where(match, gates_ref[k : k + 1, :], gate_of)
    gate_at = jnp.dot(spread, gate_of.astype(jnp.bfloat16), preferred_element_type=jnp.float32)
    place = jnp.where(chosen, 1.0, 0.0).astype(jnp.bfloat16)
    weigh = jnp.where(chosen, gate_at, 0.0).astype(jnp.bfloat16)
    place_ref[...] = place
    width = 512
    done = 0
    for send_ref in send_refs:
        rows = slice(done, done + send_ref.shape[0])
        done = rows.stop
        for at in range(0, model_width, width):
            cols = slice(at, at + width)
            right = slice(model_width + at, model_width + at + width)
            send_ref[:, cols] = jnp.dot(
                place[rows], x_ref[:, cols], preferred_element_type=jnp.float32
            ).astype(jnp.bfloat16)
            send_ref[:, right] = jnp.dot(
                weigh[rows], go_ref[:, cols], preferred_element_type=jnp.float32
            ).astype(jnp.bfloat16)
    share = model_width // groups
    line = lax.broadcasted_iota(jnp.int32, (EXTRA, tok_count), 0)
    tail = jnp.zeros((EXTRA, tok_count), jnp.float32)
    for k, each in enumerate(id_rows):
        tail = jnp.where(line == k, each.astype(jnp.float32), tail)
    for g in range(groups):
        slices_ref[g, :tok_count, :] = x_ref[:, g * share : (g + 1) * share]
        slices_ref[g, tok_count:, :] = jnp.zeros((EXTRA, share), jnp.bfloat16)
        slices_ref[g, tok_count:, :tok_count] = tail.astype(jnp.bfloat16)


def route(expert_ids, gates, tokens, grad_out, spread, parts, groups):
    tok_count, model_width = tokens.shape
    slots = spread.shape[0]
    out_shape = (
        jax.ShapeDtypeStruct((slots, tok_count), jnp.bfloat16),
        jax.ShapeDtypeStruct((groups, tok_count + EXTRA, model_width // groups), jnp.bfloat16),
        *[jax.ShapeDtypeStruct((part, 2 * model_width), jnp.bfloat16) for part in parts],
    )
    return pl.pallas_call(
        route_kernel,
        out_shape=out_shape,
        compiler_params=VMEM,
        cost_estimate=cost(),
    )(expert_ids.T, gates.T, spread, tokens, grad_out)


def slices_kernel(top_k, spread_ref, *refs):
    out_refs, refs = refs[-CHUNKS:], refs[:-CHUNKS]
    for s, x_ref in enumerate(refs):
        tok_count, width = x_ref.shape[0] - EXTRA, x_ref.shape[1]
        tail = x_ref[tok_count:, :tok_count].astype(jnp.float32).astype(jnp.int32)
        matches = match_rows([tail[k : k + 1, :] for k in range(top_k)])
        chosen = chosen_slots(matches, spread_ref[...])
        place = jnp.where(chosen, 1.0, 0.0).astype(jnp.bfloat16)
        done = 0
        for out_ref in out_refs:
            rows = slice(done, done + out_ref.shape[0])
            done = rows.stop
            out_ref[:, s * width : (s + 1) * width] = jnp.dot(
                place[rows],
                x_ref[:tok_count, :],
                preferred_element_type=jnp.float32,
            ).astype(jnp.bfloat16)


def place_slices(received, top_k, spread, parts):
    wide = len(received) * received[0].shape[1]
    return pl.pallas_call(
        functools.partial(slices_kernel, top_k),
        out_shape=[jax.ShapeDtypeStruct((part, wide), jnp.bfloat16) for part in parts],
        compiler_params=VMEM,
        cost_estimate=cost(),
    )(spread, *received)


def down_kernel(chunks, *refs):
    out_ref = refs[-1]
    total = 0.0
    for hidden_ref, ge_ref in zip(refs[:chunks], refs[chunks:-1]):
        total += contract_rows(hidden_ref[...], ge_ref[...])
    out_ref[...] = total.astype(jnp.bfloat16)


def down_rows(hiddens, rows):
    hidden_width = hiddens[0].shape[1]
    model_width = rows[0].shape[1] // 2
    tile = 256
    return pl.pallas_call(
        functools.partial(down_kernel, len(rows)),
        grid=(hidden_width // tile,),
        in_specs=[pl.BlockSpec((each.shape[0], tile), lambda i: (0, i)) for each in hiddens]
        + [pl.BlockSpec((each.shape[0], model_width), lambda i: (0, 1)) for each in rows],
        out_specs=pl.BlockSpec((tile, model_width), lambda i: (i, 0)),
        out_shape=jax.ShapeDtypeStruct((hidden_width, model_width), jnp.bfloat16),
        compiler_params=VMEM,
        cost_estimate=cost(),
    )(*hiddens, *rows)


def weight_kernel(terms, _, *refs):
    for which, out_ref in enumerate(refs[-2:]):
        total = 0.0
        for t in range(terms):
            grads = refs[terms + t]
            grad = grads[0, which] if len(grads.shape) == 4 else grads[which]
            total += contract_rows(refs[t][...], grad)
        out_ref[0] = total


def weight_rows(terms, model_width, groups):
    hidden_width = terms[0][3].shape[-1]
    width = model_width // groups
    tile = 256

    def grads_spec(s, grads):
        if grads.ndim == 3:
            return pl.BlockSpec((*grads.shape[:2], tile), lambda i, z: (0, 0, i))
        return pl.BlockSpec(
            (1, *grads.shape[1:3], tile),
            lambda i, z: (lax.rem(z[0] + groups - s, groups), 0, 0, i),
        )

    whole = pl.BlockSpec((1, width, tile), lambda i, z: (0, 0, i))
    out_shape = jax.ShapeDtypeStruct((1, width, hidden_width), jnp.float32)
    return pl.pallas_call(
        functools.partial(weight_kernel, len(terms)),
        grid_spec=pltpu.PrefetchScalarGridSpec(
            num_scalar_prefetch=1,
            grid=(hidden_width // tile,),
            in_specs=[
                pl.BlockSpec((rows.shape[0], width), lambda i, z, at=(2 * c + 1) * groups + s: (0, at))
                for rows, c, s, _ in terms
            ]
            + [grads_spec(s, grads) for _, _, s, grads in terms],
            out_specs=(whole, whole),
        ),
        out_shape=(out_shape, out_shape),
        compiler_params=VMEM,
        cost_estimate=cost(),
    )(
        lax.axis_index("dp").astype(jnp.int32)[None],
        *[rows for rows, _, _, _ in terms],
        *[grads for _, _, _, grads in terms],
    )


def expert_kernel(rows_ref, gate_ref, up_ref, down_ref, hidden_ref, grads_ref, tail_ref, sum_ref):
    model_width = rows_ref.shape[1] // 2
    step = pl.program_id(0)
    rows_x = rows_ref[:, :model_width]
    pre_gate = jnp.dot(rows_x, gate_ref[0], preferred_element_type=jnp.float32)
    pre_up = jnp.dot(rows_x, up_ref[0], preferred_element_type=jnp.float32)
    grad_hidden = contract_last(rows_ref[:, model_width:], down_ref[0])
    sigmoid_v = 1.0 / (1.0 + jnp.exp(-pre_gate))
    activated = pre_gate * sigmoid_v
    derivative = sigmoid_v * (1.0 + pre_gate * (1.0 - sigmoid_v))
    hidden = (activated * pre_up).astype(jnp.bfloat16)
    hidden_ref[...] = hidden
    grads_ref[0] = (grad_hidden * pre_up * derivative).astype(jnp.bfloat16)
    grads_ref[1] = (grad_hidden * activated).astype(jnp.bfloat16)
    gate_grad = jnp.sum(hidden.astype(jnp.float32) * grad_hidden, axis=1, keepdims=True)

    @pl.when(step == 0)
    def _():
        sum_ref[...] = jnp.zeros_like(sum_ref)

    sum_ref[...] += gate_grad

    @pl.when(step == pl.num_programs(0) - 1)
    def _():
        total = sum_ref[...]
        coarse = total.astype(jnp.bfloat16).astype(jnp.float32)
        lane = lax.broadcasted_iota(jnp.int32, total.shape, 1)
        tail = jnp.where(lane == 0, coarse, jnp.where(lane == 1, total - coarse, 0.0))
        tail_ref[...] = tail.astype(jnp.bfloat16)


def expert_rows(rows, gate_weight, up_weight, down_weight):
    count, wide = rows.shape
    _, model_width, hidden_width = gate_weight.shape
    tile = 256
    out_shape = (
        jax.ShapeDtypeStruct((count, hidden_width), jnp.bfloat16),
        jax.ShapeDtypeStruct((2, count, hidden_width), jnp.bfloat16),
        jax.ShapeDtypeStruct((count, LANES), jnp.bfloat16),
    )
    return pl.pallas_call(
        expert_kernel,
        grid=(hidden_width // tile,),
        in_specs=[
            pl.BlockSpec((count, wide), lambda i: (0, 0)),
            pl.BlockSpec((1, model_width, tile), lambda i: (0, 0, i)),
            pl.BlockSpec((1, model_width, tile), lambda i: (0, 0, i)),
            pl.BlockSpec((1, tile, model_width), lambda i: (0, i, 0)),
        ],
        out_specs=(
            pl.BlockSpec((count, tile), lambda i: (0, i)),
            pl.BlockSpec((2, count, tile), lambda i: (0, 0, i)),
            pl.BlockSpec((count, LANES), lambda i: (0, 0)),
        ),
        out_shape=out_shape,
        scratch_shapes=[pltpu.VMEM((count, LANES), jnp.float32)],
        compiler_params=VMEM,
        cost_estimate=cost(),
    )(rows, gate_weight, up_weight, down_weight)


def back_kernel(chunk, tiles, grads_ref, slices_ref, *refs):
    step = pl.program_id(0)
    tails, (gate_ref, up_ref), out_ref = refs[: chunk + 1], refs[chunk + 1 : chunk + 3], refs[-1]

    @pl.when(step < tiles)
    def _():
        row = contract_last(grads_ref[0], gate_ref[0]) + contract_last(grads_ref[1], up_ref[0])
        out_ref[...] = row.astype(jnp.bfloat16)

    @pl.when((step >= tiles) & (step < 2 * tiles))
    def _():
        out_ref[...] = slices_ref[...]

    @pl.when(step == 2 * tiles)
    def _():
        out_ref[...] = jnp.zeros_like(out_ref)
        for c, tail_ref in enumerate(tails):
            out_ref[:, c * LANES : (c + 1) * LANES] = tail_ref[...]


def back_rows(grads, tails, slices, gate_weight, up_weight, before):
    chunk = len(before)
    _, count, hidden_width = grads.shape
    model_width = gate_weight.shape[1]
    tile = 512
    tiles = model_width // tile
    last = chunk == CHUNKS - 1
    weight = pl.BlockSpec((1, tile, hidden_width), lambda i: (0, jnp.minimum(i, tiles - 1), 0))
    return pl.pallas_call(
        functools.partial(back_kernel, chunk, tiles),
        grid=(2 * tiles + last,),
        in_specs=[
            pl.BlockSpec((2, count, hidden_width), lambda i: (0, 0, 0)),
            pl.BlockSpec((count, tile), lambda i: (0, jnp.clip(i - tiles, 0, tiles - 1))),
            *[pl.BlockSpec((count, LANES), lambda i: (0, 0)) for _ in tails],
            weight,
            weight,
            *[pl.BlockSpec(memory_space=pl.ANY) for _ in before[-1:]],
        ],
        out_specs=pl.BlockSpec(
            (count, tile), lambda i: (0, jnp.where(i < 2 * tiles, 2 * tiles * chunk + i, 2 * tiles * CHUNKS))
        ),
        out_shape=jax.ShapeDtypeStruct((count, 2 * CHUNKS * model_width + tile), jnp.bfloat16),
        input_output_aliases={4 + len(tails): 0} if before else {},
        compiler_params=VMEM,
        cost_estimate=cost(),
    )(grads, slices, *tails, gate_weight, up_weight, *before[-1:])


def exchange_groups(grads, groups, back):
    below, above = [grads], [grads]
    for step in range(1, groups):
        lifts = [(i, i + 1) for i in range(step - 1, groups - 1)]
        drops = [(i + 1, i) for i in range(groups - step)]
        below.append(lax.ppermute(below[-1], "dp", lifts))
        above.append(lax.ppermute(above[-1], "dp", drops))
    below[-1], above[-1], back = lax.optimization_barrier((below[-1], above[-1], back))
    return back, below, above


def local(tokens, grad_out, expert_ids, gates, gate_weight, up_weight, down_weight):
    experts = lax.axis_size("expert")
    groups = lax.axis_size("dp")
    tok_count, top_k = expert_ids.shape
    model_width = tokens.shape[1]
    capacity = 3 * tok_count * top_k // (2 * experts)
    parts = [experts * len(own) for own in chunk_ranks(capacity)]
    expert_at, spread = slot_tables(experts, capacity)
    z = lax.axis_index("dp")

    def exchange(rows):
        return lax.all_to_all(
            rows.reshape(experts, -1, rows.shape[1]),
            "expert",
            split_axis=0,
            concat_axis=0,
            tiled=True,
        ).reshape(rows.shape)

    place, slices, *send = route(expert_ids, gates, tokens, grad_out, spread, parts, groups)

    received = [lax.dynamic_index_in_dim(slices, z, 0, keepdims=False)]
    for shift in range(1, groups):
        mine = lax.dynamic_index_in_dim(slices, lax.rem(z + shift, groups), 0, keepdims=False)
        ring = [(i, (i + shift) % groups) for i in range(groups)]
        received.append(lax.ppermute(mine, "dp", ring))

    rows, hiddens, grads, tails, gathered, backs = [], [], [], [], [], []
    for c in range(CHUNKS):
        if c == 1:
            send[c], received = lax.optimization_barrier((send[c], received))
        rows.append(exchange(send[c]))
        if c == 0:
            send_slices = place_slices(received, top_k, spread, parts)
        if CHUNKS == 1:
            rows[c], send_slices = lax.optimization_barrier((rows[c], send_slices))
        else:
            rows[c], backs[-1] = lax.optimization_barrier((rows[c], backs[-1]))
        hidden, grad, tail = expert_rows(rows[c], gate_weight, up_weight, down_weight)
        hiddens.append(hidden)
        grads.append(grad)
        tails.append(tail)
        if c < CHUNKS - 1:
            gathered.append(lax.all_gather(grad, "dp"))
        backs.append(back_rows(grad, tails, send_slices[c], gate_weight, up_weight, backs))
    grad_down_w = lax.psum_scatter(
        down_rows(hiddens, rows), "dp", scatter_dimension=0, tiled=True
    ).astype(jnp.float32)
    back = exchange(backs[-1])

    back, below, above = exchange_groups(grads[-1], groups, back)
    terms = [(back, c, s, each) for c, each in enumerate(gathered) for s in range(groups)]
    for s in range(groups):
        terms.append((back, CHUNKS - 1, s, below[s]))
        if s:
            terms.append((back, CHUNKS - 1, s, above[groups - s]))
    grad_w = weight_rows(terms, model_width, groups)

    grad_tokens, scaled, done = 0.0, [], 0
    for c, part in enumerate(parts):
        at = slice(done, done + part)
        done = at.stop
        first = 2 * c * model_width
        grad_tokens += contract_rows(place[at], back[:, first : first + model_width])
        first = 2 * CHUNKS * model_width + c * LANES
        pair = back[:, first : first + 2].astype(jnp.float32)
        scaled.append(pair[:, 0] + pair[:, 1])
    grad_tokens = grad_tokens.astype(jnp.bfloat16)
    scaled = jnp.concatenate(scaled)[:, None]
    gate_b = gates.T.astype(jnp.bfloat16).astype(jnp.float32)
    grad_gates = []
    for k in range(top_k):
        hit = (expert_ids[:, k][None, :] == expert_at[:, None]) & (place > 0)
        grad_gates.append(jnp.sum(jnp.where(hit, scaled, 0.0), axis=0) / gate_b[k])
    grad_gates = jnp.stack(grad_gates).astype(jnp.bfloat16).T

    return (grad_tokens, grad_gates, *grad_w, grad_down_w[None])


def solution(mesh):
    placed = (
        P(("dp", "expert"), None),
        P(("dp", "expert"), None),
        P(("dp", "expert"), None),
        P(("dp", "expert"), None),
        P("expert", None, None),
        P("expert", None, None),
        P("expert", None, None),
    )
    return jax.shard_map(
        local,
        mesh=mesh,
        in_specs=placed,
        out_specs=(
            P(("dp", "expert"), None),
            P(("dp", "expert"), None),
            P("expert", "dp", None),
            P("expert", "dp", None),
            P("expert", "dp", None),
        ),
        check_vma=False,
    )
```

```python
import functools

import jax
import jax.numpy as jnp
import numpy as np
from jax import lax
from jax.experimental import pallas as pl
from jax.experimental.pallas import tpu as pltpu
from jax.sharding import PartitionSpec as P

LANES = 128
EXTRA = 16
VMEM = pltpu.CompilerParams(vmem_limit_bytes=62 * 1024 * 1024)


def contract_rows(left, right):
    return lax.dot_general(
        left, right, (((0,), (0,)), ((), ())), preferred_element_type=jnp.float32
    )


def contract_last(left, right):
    return lax.dot_general(
        left, right, (((1,), (1,)), ((), ())), preferred_element_type=jnp.float32
    )


def cost(flops=1024):
    return pl.CostEstimate(flops=flops, bytes_accessed=1024, transcendentals=0)


def slot_table(experts, capacity):
    slot = np.arange(experts * capacity)
    spread = (slot[:, None] // capacity == np.arange(LANES)[None, :]).astype(np.float32)
    spread[:, -1] = -(slot % capacity)
    return jnp.asarray(spread, jnp.bfloat16)


def match_rows(id_rows):
    expert_of = lax.broadcasted_iota(jnp.int32, (LANES, id_rows[0].shape[1]), 0)
    return [each == expert_of for each in id_rows]


def chosen_slots(matches, spread):
    tok_count = matches[0].shape[1]
    named = functools.reduce(jnp.logical_or, matches)
    row = lax.broadcasted_iota(jnp.int32, (tok_count, tok_count), 0)
    col = lax.broadcasted_iota(jnp.int32, (tok_count, tok_count), 1)
    after = jnp.where(row < col, 1.0, 0.0).astype(jnp.bfloat16)
    earlier = jnp.dot(
        jnp.where(named, 1.0, 0.0).astype(jnp.bfloat16), after, preferred_element_type=jnp.float32
    )
    last = lax.broadcasted_iota(jnp.int32, named.shape, 0) == LANES - 1
    key = jnp.where(last, 1.0, jnp.where(named, earlier, -1.0)).astype(jnp.bfloat16)
    return jnp.dot(spread, key, preferred_element_type=jnp.float32) == 0.0


def route_kernel(ids_ref, gates_ref, spread_ref, x_ref, go_ref, send_ref, place_ref, tokens_ref):
    tok_count, model_width = x_ref.shape
    id_rows = [ids_ref[k : k + 1, :] for k in range(ids_ref.shape[0])]
    spread = spread_ref[...]
    matches = match_rows(id_rows)
    chosen = chosen_slots(matches, spread)
    gate_of = jnp.zeros(matches[0].shape, jnp.float32)
    for k, match in enumerate(matches):
        gate_of = jnp.where(match, gates_ref[k : k + 1, :], gate_of)
    gate_at = jnp.dot(spread, gate_of.astype(jnp.bfloat16), preferred_element_type=jnp.float32)
    place = jnp.where(chosen, 1.0, 0.0).astype(jnp.bfloat16)
    weigh = jnp.where(chosen, gate_at, 0.0).astype(jnp.bfloat16)
    place_ref[...] = place
    width = 512
    for at in range(0, model_width, width):
        cols = slice(at, at + width)
        right = slice(model_width + at, model_width + at + width)
        send_ref[:, cols] = jnp.dot(
            place, x_ref[:, cols], preferred_element_type=jnp.float32
        ).astype(jnp.bfloat16)
        send_ref[:, right] = jnp.dot(
            weigh, go_ref[:, cols], preferred_element_type=jnp.float32
        ).astype(jnp.bfloat16)
    line = lax.broadcasted_iota(jnp.int32, (EXTRA, tok_count), 0)
    tail = jnp.zeros((EXTRA, tok_count), jnp.float32)
    for k, each in enumerate(id_rows):
        tail = jnp.where(line == k, each.astype(jnp.float32), tail)
    tokens_ref[:tok_count, :] = x_ref[...]
    tokens_ref[tok_count:, :] = jnp.zeros((EXTRA, model_width), jnp.bfloat16)
    tokens_ref[tok_count:, :tok_count] = tail.astype(jnp.bfloat16)


def route(expert_ids, gates, tokens, grad_out, spread):
    tok_count, model_width = tokens.shape
    slots = spread.shape[0]
    return pl.pallas_call(
        route_kernel,
        out_shape=(
            jax.ShapeDtypeStruct((slots, 2 * model_width), jnp.bfloat16),
            jax.ShapeDtypeStruct((slots, tok_count), jnp.bfloat16),
            jax.ShapeDtypeStruct((tok_count + EXTRA, model_width), jnp.bfloat16),
        ),
        compiler_params=VMEM,
        cost_estimate=cost(),
    )(expert_ids.T, gates.T, spread, tokens, grad_out)


def others_kernel(top_k, spread_ref, *refs):
    out_ref = refs[-1]
    for s, (low_ref, high_ref) in enumerate(zip(refs[:-1:2], refs[1:-1:2])):
        tok_count, model_width = low_ref.shape[0] - EXTRA, low_ref.shape[1]
        tail = low_ref[tok_count:, :tok_count].astype(jnp.float32)
        tail = (tail + high_ref[tok_count:, :tok_count].astype(jnp.float32)).astype(jnp.int32)
        matches = match_rows([tail[k : k + 1, :] for k in range(top_k)])
        chosen = chosen_slots(matches, spread_ref[...])
        place = jnp.where(chosen, 1.0, 0.0).astype(jnp.bfloat16)
        width = 512
        for at in range(0, model_width, width):
            cols = slice(s * model_width + at, s * model_width + at + width)
            out_ref[:, cols] = jnp.dot(
                place,
                low_ref[:tok_count, at : at + width] + high_ref[:tok_count, at : at + width],
                preferred_element_type=jnp.float32,
            ).astype(jnp.bfloat16)


def place_others(received, top_k, spread):
    wide = len(received) // 2 * received[0].shape[1]
    return pl.pallas_call(
        functools.partial(others_kernel, top_k),
        out_shape=jax.ShapeDtypeStruct((spread.shape[0], wide), jnp.bfloat16),
        compiler_params=VMEM,
        cost_estimate=cost(),
    )(spread, *received)


def silu_parts(pre_gate):
    sigmoid_v = 1.0 / (1.0 + jnp.exp(-pre_gate))
    return pre_gate * sigmoid_v, sigmoid_v * (1.0 + pre_gate * (1.0 - sigmoid_v))


def expert_kernel(rows_ref, gate_ref, up_ref, down_ref, hidden_ref, back_ref, grads_ref, tail_ref, sum_ref):
    model_width = rows_ref.shape[1] // 2
    step = pl.program_id(0)
    rows_x = rows_ref[:, :model_width]
    pre_gate = jnp.dot(rows_x, gate_ref[0], preferred_element_type=jnp.float32)
    pre_up = jnp.dot(rows_x, up_ref[0], preferred_element_type=jnp.float32)
    grad_hidden = contract_last(rows_ref[:, model_width:], down_ref[0])
    activated, derivative = silu_parts(pre_gate)
    hidden = (activated * pre_up).astype(jnp.bfloat16)
    hidden_ref[...] = hidden
    back_ref[...] = grad_hidden.astype(jnp.bfloat16)
    grads_ref[0] = (grad_hidden * pre_up * derivative).astype(jnp.bfloat16)
    grads_ref[1] = (grad_hidden * activated).astype(jnp.bfloat16)
    gate_grad = jnp.sum(hidden.astype(jnp.float32) * grad_hidden, axis=1, keepdims=True)

    @pl.when(step == 0)
    def _():
        sum_ref[...] = jnp.zeros_like(sum_ref)

    sum_ref[...] += gate_grad

    @pl.when(step == pl.num_programs(0) - 1)
    def _():
        total = sum_ref[...]
        coarse = total.astype(jnp.bfloat16).astype(jnp.float32)
        lane = lax.broadcasted_iota(jnp.int32, total.shape, 1)
        tail = jnp.where(lane == 0, coarse, jnp.where(lane == 1, total - coarse, 0.0))
        tail_ref[...] = tail.astype(jnp.bfloat16)


def expert_rows(rows, gate_weight, up_weight, down_weight):
    count, wide = rows.shape
    _, model_width, hidden_width = gate_weight.shape
    tile = 256
    flat = pl.BlockSpec((count, tile), lambda i: (0, i))
    weight = pl.BlockSpec((1, model_width, tile), lambda i: (0, 0, i))
    return pl.pallas_call(
        expert_kernel,
        grid=(hidden_width // tile,),
        in_specs=[
            pl.BlockSpec((count, wide), lambda i: (0, 0)),
            weight,
            weight,
            pl.BlockSpec((1, tile, model_width), lambda i: (0, i, 0)),
        ],
        out_specs=(
            flat,
            flat,
            pl.BlockSpec((2, count, tile), lambda i: (0, 0, i)),
            pl.BlockSpec((count, LANES), lambda i: (0, 0)),
        ),
        out_shape=(
            jax.ShapeDtypeStruct((count, hidden_width), jnp.bfloat16),
            jax.ShapeDtypeStruct((count, hidden_width), jnp.bfloat16),
            jax.ShapeDtypeStruct((2, count, hidden_width), jnp.bfloat16),
            jax.ShapeDtypeStruct((count, LANES), jnp.bfloat16),
        ),
        scratch_shapes=[pltpu.VMEM((count, LANES), jnp.float32)],
        compiler_params=VMEM,
        cost_estimate=cost(),
    )(rows, gate_weight, up_weight, down_weight)


def down_kernel(hidden_ref, ge_ref, out_ref):
    out_ref[...] = contract_rows(hidden_ref[...], ge_ref[...]).astype(jnp.bfloat16)


def down_rows(hidden, rows):
    count, hidden_width = hidden.shape
    model_width = rows.shape[1] // 2
    tile = 256
    return pl.pallas_call(
        down_kernel,
        grid=(hidden_width // tile,),
        in_specs=[
            pl.BlockSpec((count, tile), lambda i: (0, i)),
            pl.BlockSpec((count, model_width), lambda i: (0, 1)),
        ],
        out_specs=pl.BlockSpec((tile, model_width), lambda i: (i, 0)),
        out_shape=jax.ShapeDtypeStruct((hidden_width, model_width), jnp.bfloat16),
        compiler_params=VMEM,
        cost_estimate=cost(),
    )(hidden, rows)


def back_kernel(tiles, grads_ref, tail_ref, gate_ref, up_ref, out_ref):
    step = pl.program_id(0)

    @pl.when(step < tiles)
    def _():
        row = contract_last(grads_ref[0], gate_ref[0]) + contract_last(grads_ref[1], up_ref[0])
        out_ref[...] = row.astype(jnp.bfloat16)

    @pl.when(step == tiles)
    def _():
        out_ref[:, :LANES] = tail_ref[...]


def back_rows(grads, tail, gate_weight, up_weight):
    _, count, hidden_width = grads.shape
    model_width = gate_weight.shape[1]
    tile = 512
    tiles = model_width // tile
    weight = pl.BlockSpec((1, tile, hidden_width), lambda i: (0, jnp.minimum(i, tiles - 1), 0))
    return pl.pallas_call(
        functools.partial(back_kernel, tiles),
        grid=(tiles + 1,),
        in_specs=[
            pl.BlockSpec((2, count, hidden_width), lambda i: (0, 0, 0)),
            pl.BlockSpec((count, LANES), lambda i: (0, 0)),
            weight,
            weight,
        ],
        out_specs=pl.BlockSpec((count, tile), lambda i: (0, i)),
        out_shape=jax.ShapeDtypeStruct((count, model_width + LANES), jnp.bfloat16),
        compiler_params=VMEM,
        cost_estimate=cost(),
    )(grads, tail, gate_weight, up_weight)


def weight_kernel(shifts, own, carried, z_ref, *refs):
    count = len(shifts)
    xs, lows, highs = refs[:count], refs[count : 2 * count], refs[2 * count : 3 * count]
    gate_ref, up_ref, *more = refs[3 * count : -2]
    outs = refs[-2:]
    width = outs[0].shape[1]
    columns = pl.ds(pl.multiple_of(z_ref[0] * width, LANES), width)
    totals = [0.0, 0.0]
    if own:
        rows_ref, grads_ref = more[:2]
        totals = [contract_rows(rows_ref[...], grads_ref[k]) for k in range(2)]
    if carried:
        totals = [total + ref[0] for total, ref in zip(totals, more[-2:])]
    for shift, x_ref, low_ref, high_ref in zip(shifts, xs, lows, highs):
        pre_gate = jnp.dot(x_ref[...], gate_ref[0], preferred_element_type=jnp.float32)
        pre_up = jnp.dot(x_ref[...], up_ref[0], preferred_element_type=jnp.float32)
        activated, derivative = silu_parts(pre_gate)
        low, high = low_ref[...].astype(jnp.float32), high_ref[...].astype(jnp.float32)
        grad_hidden = jnp.where(z_ref[0] >= shift, low, high)
        own_x = x_ref[:, columns]
        grads = (grad_hidden * pre_up * derivative, grad_hidden * activated)
        for k, grad in enumerate(grads):
            totals[k] = totals[k] + contract_rows(own_x, grad.astype(jnp.bfloat16))
    for out_ref, total in zip(outs, totals):
        out_ref[0] = total


def weight_rows(terms, own, carried, gate_weight, up_weight, groups):
    _, model_width, hidden_width = gate_weight.shape
    width = model_width // groups
    slots = terms[0][0].shape[0]
    shifts = tuple(shift for _, _, shift, _, _ in terms)
    tile = 256
    whole = pl.BlockSpec((1, width, tile), lambda i, z: (0, 0, i))
    weight = pl.BlockSpec((1, model_width, tile), lambda i, z: (0, 0, i))
    flat = pl.BlockSpec((slots, tile), lambda i, z: (0, i))
    out_shape = jax.ShapeDtypeStruct((1, width, hidden_width), jnp.float32)
    in_specs = [
        pl.BlockSpec((slots, model_width), lambda i, z, at=at: (0, at)) for _, at, *_ in terms
    ]
    in_specs += [flat] * (2 * len(terms)) + [weight, weight]
    if own:
        in_specs.append(pl.BlockSpec((slots, width), lambda i, z: (0, z[0])))
        in_specs.append(pl.BlockSpec((2, slots, tile), lambda i, z: (0, 0, i)))
    first = 1 + len(in_specs)
    return pl.pallas_call(
        functools.partial(weight_kernel, shifts, bool(own), bool(carried)),
        grid_spec=pltpu.PrefetchScalarGridSpec(
            num_scalar_prefetch=1,
            grid=(hidden_width // tile,),
            in_specs=in_specs + [whole] * len(carried),
            out_specs=(whole, whole),
        ),
        out_shape=(out_shape, out_shape),
        input_output_aliases={first + k: k for k in range(len(carried))},
        compiler_params=VMEM,
        cost_estimate=cost(),
    )(
        lax.axis_index("dp").astype(jnp.int32)[None],
        *[rows for rows, *_ in terms],
        *[low for *_, low, _ in terms],
        *[high for *_, high in terms],
        gate_weight,
        up_weight,
        *own,
        *carried,
    )


def pieces(payload_rows, block):
    depth, wide = block
    count = payload_rows // depth
    share = wide // count
    return [
        (slice(j * depth, (j + 1) * depth), slice(0, share), slice(j * share, (j + 1) * share))
        for j in range(count)
    ]


def hop_kernel(step, groups, z_ref, *refs):
    z = z_ref[0]
    for way in range(2):
        got_ref, block_ref, out_ref = refs[way], refs[2 + way], refs[4 + way]
        passed = z if way == 0 else groups - 1 - z

        @pl.when(passed < step)
        def _():
            for rows, left, right in pieces(out_ref.shape[0], block_ref.shape[1:]):
                part = block_ref[0, :, right]
                if step > 1:
                    total = part.astype(jnp.float32) + got_ref[rows, left].astype(jnp.float32)
                    part = total.astype(jnp.bfloat16)
                out_ref[rows, left] = part

        @pl.when(passed >= step)
        def _():
            width = min(got_ref.shape[1], out_ref.shape[1])
            out_ref[:, :width] = got_ref[:, :width]


def hop(step, got, partial, width):
    groups, depth, wide = partial.shape
    rows = got[0].shape[0]
    whole = pl.BlockSpec((rows, width), lambda i, z: (0, 0))
    sums = [
        pl.BlockSpec((1, depth, wide), lambda i, z: (jnp.minimum(z[0] + groups - step, groups - 1), 0, 0)),
        pl.BlockSpec((1, depth, wide), lambda i, z: (jnp.maximum(z[0] - groups + step, 0), 0, 0)),
    ]
    return pl.pallas_call(
        functools.partial(hop_kernel, step, groups),
        grid_spec=pltpu.PrefetchScalarGridSpec(
            num_scalar_prefetch=1,
            grid=(1,),
            in_specs=[pl.BlockSpec(each.shape, lambda i, z: (0, 0)) for each in got] + sums,
            out_specs=(whole, whole),
        ),
        out_shape=[jax.ShapeDtypeStruct((rows, width), jnp.bfloat16)] * 2,
        compiler_params=VMEM,
        cost_estimate=cost(),
    )(lax.axis_index("dp").astype(jnp.int32)[None], *got, partial, partial)


def last_kernel(z_ref, up_ref, down_ref, block_ref, out_ref):
    for rows, left, right in pieces(up_ref.shape[0], block_ref.shape[1:]):
        total = up_ref[rows, left].astype(jnp.float32) + down_ref[rows, left].astype(jnp.float32)
        out_ref[0, :, right] = total + block_ref[0, :, right].astype(jnp.float32)


def last_sum(got, partial):
    groups, depth, wide = partial.shape
    return pl.pallas_call(
        last_kernel,
        grid_spec=pltpu.PrefetchScalarGridSpec(
            num_scalar_prefetch=1,
            grid=(1,),
            in_specs=[pl.BlockSpec(each.shape, lambda i, z: (0, 0)) for each in got]
            + [pl.BlockSpec((1, depth, wide), lambda i, z: (z[0], 0, 0))],
            out_specs=pl.BlockSpec((1, depth, wide), lambda i, z: (0, 0, 0)),
        ),
        out_shape=jax.ShapeDtypeStruct((1, depth, wide), jnp.float32),
        compiler_params=VMEM,
        cost_estimate=cost(),
    )(lax.axis_index("dp").astype(jnp.int32)[None], *got, partial)


def shift_both(sent, groups):
    up = [(i, i + 1) for i in range(groups - 1)]
    down = [(i + 1, i) for i in range(groups - 1)]
    return lax.ppermute(sent[0], "dp", up), lax.ppermute(sent[1], "dp", down)


def local(tokens, grad_out, expert_ids, gates, gate_weight, up_weight, down_weight):
    experts = lax.axis_size("expert")
    groups = lax.axis_size("dp")
    tok_count, top_k = expert_ids.shape
    model_width = tokens.shape[1]
    capacity = 3 * tok_count * top_k // (2 * experts)
    spread = slot_table(experts, capacity)

    def exchange(rows):
        return lax.all_to_all(
            rows.reshape(experts, capacity, -1), "expert", split_axis=0, concat_axis=0, tiled=True
        ).reshape(rows.shape)

    send, place, own_tokens = route(expert_ids, gates, tokens, grad_out, spread)
    batches = [(groups // 2,)] if groups % 2 == 0 else []
    batches += [(s, groups - s) for s in range((groups - 1) // 2, 0, -1)]
    below, above = [own_tokens], [own_tokens]
    for step in range(1, groups):
        lifts = [(i, i + 1) for i in range(step - 1, groups - 1)]
        drops = [(i + 1, i) for i in range(groups - step)]
        below.append(lax.ppermute(below[-1], "dp", lifts))
        above.append(lax.ppermute(above[-1], "dp", drops))

    def tokens_of(batch):
        return [side for s in batch for side in (below[s], above[groups - s])]

    placed = [place_others(tokens_of(batches[0]), top_k, spread)]
    rows = exchange(send)
    rows, placed[0] = lax.optimization_barrier((rows, placed[0]))
    hidden, grad_hidden, grads, tail = expert_rows(rows, gate_weight, up_weight, down_weight)
    for batch in batches[1:]:
        grads, *received = lax.optimization_barrier((grads, *tokens_of(batch)))
        placed.append(place_others(received, top_k, spread))
    partial = down_rows(hidden, rows).reshape(groups, -1, model_width)
    back = back_rows(grads, tail, gate_weight, up_weight)
    wide = max(hidden.shape[1], partial[0].size // rows.shape[0])

    got = [shift_both((grad_hidden, grad_hidden), groups)]
    got[0], partial, placed[1:] = lax.optimization_barrier((got[0], partial, placed[1:]))
    others, own, grad_w = exchange(placed[0]), (rows, grads), ()
    for step in range(1, groups):
        got.append(shift_both(hop(step, got[-1], partial, wide), groups))
        if step == 1:
            got[step], back = lax.optimization_barrier((got[step], back))
        i = step - groups + len(batches)
        if i < 0:
            continue
        batch = batches[i]
        if i + 1 < len(batches):
            others, placed[i + 1] = lax.optimization_barrier((others, placed[i + 1]))
            later = exchange(placed[i + 1])
        else:
            others, back = lax.optimization_barrier((others, back))
            back = exchange(back)
        terms = [
            (others, at, s, got[s - 1][0], got[groups - s - 1][1]) for at, s in enumerate(batch)
        ]
        grad_w = weight_rows(terms, own, grad_w, gate_weight, up_weight, groups)
        own, others = (), later
        got[step], grad_w = lax.optimization_barrier((got[step], grad_w))
    grad_down_w = last_sum(got[-1], partial)

    grad_tokens = contract_rows(place, back[:, :model_width]).astype(jnp.bfloat16)
    scaled = back[:, model_width : model_width + 2].astype(jnp.float32)
    scaled = scaled[:, :1] + scaled[:, 1:]
    expert_at = np.arange(experts * capacity, dtype=np.int32)[:, None] // capacity
    gate_b = gates.T.astype(jnp.bfloat16).astype(jnp.float32)
    grad_gates = []
    for k in range(top_k):
        hit = (expert_ids[:, k][None, :] == expert_at) & (place > 0)
        grad_gates.append(jnp.sum(jnp.where(hit, scaled, 0.0), axis=0) / gate_b[k])
    grad_gates = jnp.stack(grad_gates).astype(jnp.bfloat16).T
    return (grad_tokens, grad_gates, *grad_w, grad_down_w)


def solution(mesh):
    placed = (
        P(("dp", "expert"), None),
        P(("dp", "expert"), None),
        P(("dp", "expert"), None),
        P(("dp", "expert"), None),
        P("expert", None, None),
        P("expert", None, None),
        P("expert", None, None),
    )
    return jax.shard_map(
        local,
        mesh=mesh,
        in_specs=placed,
        out_specs=(
            P(("dp", "expert"), None),
            P(("dp", "expert"), None),
            P("expert", "dp", None),
            P("expert", "dp", None),
            P("expert", "dp", None),
        ),
        check_vma=False,
    )
```

```python
import functools

import jax
import jax.numpy as jnp
import numpy as np
from jax import lax
from jax.experimental import pallas as pl
from jax.experimental.pallas import tpu as pltpu
from jax.sharding import PartitionSpec as P

LANES = 128
EXTRA = 16
VMEM = pltpu.CompilerParams(vmem_limit_bytes=62 * 1024 * 1024)


def contract_rows(left, right):
    return lax.dot_general(
        left, right, (((0,), (0,)), ((), ())), preferred_element_type=jnp.float32
    )


def contract_last(left, right):
    return lax.dot_general(
        left, right, (((1,), (1,)), ((), ())), preferred_element_type=jnp.float32
    )


def cost(flops=1024):
    return pl.CostEstimate(flops=flops, bytes_accessed=1024, transcendentals=0)


def slot_table(experts, capacity):
    slot = np.arange(experts * capacity)
    spread = (slot[:, None] // capacity == np.arange(LANES)[None, :]).astype(np.float32)
    spread[:, -1] = -(slot % capacity)
    return jnp.asarray(spread, jnp.bfloat16)


def match_rows(id_rows):
    expert_of = lax.broadcasted_iota(jnp.int32, (LANES, id_rows[0].shape[1]), 0)
    return [each == expert_of for each in id_rows]


def chosen_slots(matches, spread):
    tok_count = matches[0].shape[1]
    named = functools.reduce(jnp.logical_or, matches)
    row = lax.broadcasted_iota(jnp.int32, (tok_count, tok_count), 0)
    col = lax.broadcasted_iota(jnp.int32, (tok_count, tok_count), 1)
    after = jnp.where(row < col, 1.0, 0.0).astype(jnp.bfloat16)
    earlier = jnp.dot(
        jnp.where(named, 1.0, 0.0).astype(jnp.bfloat16), after, preferred_element_type=jnp.float32
    )
    last = lax.broadcasted_iota(jnp.int32, named.shape, 0) == LANES - 1
    key = jnp.where(last, 1.0, jnp.where(named, earlier, -1.0)).astype(jnp.bfloat16)
    return jnp.dot(spread, key, preferred_element_type=jnp.float32) == 0.0


def route_kernel(ids_ref, gates_ref, spread_ref, x_ref, go_ref, sx_ref, sg_ref, place_ref, tokens_ref):
    tok_count, model_width = x_ref.shape
    id_rows = [ids_ref[k : k + 1, :] for k in range(ids_ref.shape[0])]
    spread = spread_ref[...]
    matches = match_rows(id_rows)
    chosen = chosen_slots(matches, spread)
    gate_of = jnp.zeros(matches[0].shape, jnp.float32)
    for k, match in enumerate(matches):
        gate_of = jnp.where(match, gates_ref[k : k + 1, :], gate_of)
    gate_at = jnp.dot(spread, gate_of.astype(jnp.bfloat16), preferred_element_type=jnp.float32)
    place = jnp.where(chosen, 1.0, 0.0).astype(jnp.bfloat16)
    weigh = jnp.where(chosen, gate_at, 0.0).astype(jnp.bfloat16)
    place_ref[...] = place
    width = 512
    for at in range(0, model_width, width):
        cols = slice(at, at + width)
        sx_ref[:, cols] = jnp.dot(
            place, x_ref[:, cols], preferred_element_type=jnp.float32
        ).astype(jnp.bfloat16)
        sg_ref[:, cols] = jnp.dot(
            weigh, go_ref[:, cols], preferred_element_type=jnp.float32
        ).astype(jnp.bfloat16)
    line = lax.broadcasted_iota(jnp.int32, (EXTRA, tok_count), 0)
    tail = jnp.zeros((EXTRA, tok_count), jnp.float32)
    for k, each in enumerate(id_rows):
        tail = jnp.where(line == k, each.astype(jnp.float32), tail)
    tokens_ref[:tok_count, :] = x_ref[...]
    tokens_ref[tok_count:, :] = jnp.zeros((EXTRA, model_width), jnp.bfloat16)
    tokens_ref[tok_count:, :tok_count] = tail.astype(jnp.bfloat16)


def route(expert_ids, gates, tokens, grad_out, spread):
    tok_count, model_width = tokens.shape
    slots = spread.shape[0]
    return pl.pallas_call(
        route_kernel,
        out_shape=(
            jax.ShapeDtypeStruct((slots, model_width), jnp.bfloat16),
            jax.ShapeDtypeStruct((slots, model_width), jnp.bfloat16),
            jax.ShapeDtypeStruct((slots, tok_count), jnp.bfloat16),
            jax.ShapeDtypeStruct((tok_count + EXTRA, model_width), jnp.bfloat16),
        ),
        compiler_params=VMEM,
        cost_estimate=cost(),
    )(expert_ids.T, gates.T, spread, tokens, grad_out)


def others_kernel(top_k, spread_ref, *refs):
    out_ref = refs[-1]
    for s, (low_ref, high_ref) in enumerate(zip(refs[:-1:2], refs[1:-1:2])):
        tok_count, model_width = low_ref.shape[0] - EXTRA, low_ref.shape[1]
        tail = low_ref[tok_count:, :tok_count].astype(jnp.float32)
        tail = (tail + high_ref[tok_count:, :tok_count].astype(jnp.float32)).astype(jnp.int32)
        matches = match_rows([tail[k : k + 1, :] for k in range(top_k)])
        chosen = chosen_slots(matches, spread_ref[...])
        place = jnp.where(chosen, 1.0, 0.0).astype(jnp.bfloat16)
        width = 512
        for at in range(0, model_width, width):
            cols = slice(s * model_width + at, s * model_width + at + width)
            out_ref[:, cols] = jnp.dot(
                place,
                low_ref[:tok_count, at : at + width] + high_ref[:tok_count, at : at + width],
                preferred_element_type=jnp.float32,
            ).astype(jnp.bfloat16)


def place_others(received, top_k, spread):
    wide = len(received) // 2 * received[0].shape[1]
    return pl.pallas_call(
        functools.partial(others_kernel, top_k),
        out_shape=jax.ShapeDtypeStruct((spread.shape[0], wide), jnp.bfloat16),
        compiler_params=VMEM,
        cost_estimate=cost(),
    )(spread, *received)


def silu_parts(pre_gate):
    sigmoid_v = 1.0 / (1.0 + jnp.exp(-pre_gate))
    return pre_gate * sigmoid_v, sigmoid_v * (1.0 + pre_gate * (1.0 - sigmoid_v))


def cotangent_kernel(ge_ref, down_ref, out_ref):
    out_ref[...] = contract_last(ge_ref[...], down_ref[0]).astype(jnp.bfloat16)


def cotangent_rows(rows_ge, down_weight):
    count, model_width = rows_ge.shape
    hidden_width = down_weight.shape[1]
    tile = 256
    return pl.pallas_call(
        cotangent_kernel,
        grid=(hidden_width // tile,),
        in_specs=[
            pl.BlockSpec((count, model_width), lambda i: (0, 0)),
            pl.BlockSpec((1, tile, model_width), lambda i: (0, i, 0)),
        ],
        out_specs=pl.BlockSpec((count, tile), lambda i: (0, i)),
        out_shape=jax.ShapeDtypeStruct((count, hidden_width), jnp.bfloat16),
        compiler_params=VMEM,
        cost_estimate=cost(),
    )(rows_ge, down_weight)


def expert_kernel(x_ref, ge_ref, gh_ref, gate_ref, up_ref, grads_ref, down_ref, tail_ref, sum_ref):
    step = pl.program_id(0)
    pre_gate = jnp.dot(x_ref[...], gate_ref[0], preferred_element_type=jnp.float32)
    pre_up = jnp.dot(x_ref[...], up_ref[0], preferred_element_type=jnp.float32)
    grad_hidden = gh_ref[...].astype(jnp.float32)
    activated, derivative = silu_parts(pre_gate)
    hidden = (activated * pre_up).astype(jnp.bfloat16)
    grads_ref[0] = (grad_hidden * pre_up * derivative).astype(jnp.bfloat16)
    grads_ref[1] = (grad_hidden * activated).astype(jnp.bfloat16)
    down_ref[...] = contract_rows(hidden, ge_ref[...]).astype(jnp.bfloat16)
    gate_grad = jnp.sum(hidden.astype(jnp.float32) * grad_hidden, axis=1, keepdims=True)

    @pl.when(step == 0)
    def _():
        sum_ref[...] = jnp.zeros_like(sum_ref)

    sum_ref[...] += gate_grad

    @pl.when(step == pl.num_programs(0) - 1)
    def _():
        total = sum_ref[...]
        coarse = total.astype(jnp.bfloat16).astype(jnp.float32)
        lane = lax.broadcasted_iota(jnp.int32, total.shape, 1)
        tail = jnp.where(lane == 0, coarse, jnp.where(lane == 1, total - coarse, 0.0))
        tail_ref[...] = tail.astype(jnp.bfloat16)


def expert_rows(rows_x, rows_ge, grad_hidden, gate_weight, up_weight):
    count, model_width = rows_x.shape
    hidden_width = gate_weight.shape[2]
    tile = 256
    weight = pl.BlockSpec((1, model_width, tile), lambda i: (0, 0, i))
    return pl.pallas_call(
        expert_kernel,
        grid=(hidden_width // tile,),
        in_specs=[
            pl.BlockSpec((count, model_width), lambda i: (0, 0)),
            pl.BlockSpec((count, model_width), lambda i: (0, 0)),
            pl.BlockSpec((count, tile), lambda i: (0, i)),
            weight,
            weight,
        ],
        out_specs=(
            pl.BlockSpec((2, count, tile), lambda i: (0, 0, i)),
            pl.BlockSpec((tile, model_width), lambda i: (i, 0)),
            pl.BlockSpec((count, LANES), lambda i: (0, 0)),
        ),
        out_shape=(
            jax.ShapeDtypeStruct((2, count, hidden_width), jnp.bfloat16),
            jax.ShapeDtypeStruct((hidden_width, model_width), jnp.bfloat16),
            jax.ShapeDtypeStruct((count, LANES), jnp.bfloat16),
        ),
        scratch_shapes=[pltpu.VMEM((count, LANES), jnp.float32)],
        compiler_params=VMEM,
        cost_estimate=cost(),
    )(rows_x, rows_ge, grad_hidden, gate_weight, up_weight)


def back_kernel(tiles, grads_ref, tail_ref, gate_ref, up_ref, out_ref):
    step = pl.program_id(0)

    @pl.when(step < tiles)
    def _():
        row = contract_last(grads_ref[0], gate_ref[0]) + contract_last(grads_ref[1], up_ref[0])
        out_ref[...] = row.astype(jnp.bfloat16)

    @pl.when(step == tiles)
    def _():
        out_ref[:, :LANES] = tail_ref[...]


def back_rows(grads, tail, gate_weight, up_weight):
    _, count, hidden_width = grads.shape
    model_width = gate_weight.shape[1]
    tile = 512
    tiles = model_width // tile
    weight = pl.BlockSpec((1, tile, hidden_width), lambda i: (0, jnp.minimum(i, tiles - 1), 0))
    return pl.pallas_call(
        functools.partial(back_kernel, tiles),
        grid=(tiles + 1,),
        in_specs=[
            pl.BlockSpec((2, count, hidden_width), lambda i: (0, 0, 0)),
            pl.BlockSpec((count, LANES), lambda i: (0, 0)),
            weight,
            weight,
        ],
        out_specs=pl.BlockSpec((count, tile), lambda i: (0, i)),
        out_shape=jax.ShapeDtypeStruct((count, model_width + LANES), jnp.bfloat16),
        compiler_params=VMEM,
        cost_estimate=cost(),
    )(grads, tail, gate_weight, up_weight)


def weight_kernel(shifts, own, carried, z_ref, *refs):
    count = len(shifts)
    xs, lows, highs = refs[:count], refs[count : 2 * count], refs[2 * count : 3 * count]
    gate_ref, up_ref, *more = refs[3 * count : -2]
    outs = refs[-2:]
    width = outs[0].shape[1]
    columns = pl.ds(pl.multiple_of(z_ref[0] * width, LANES), width)
    totals = [0.0, 0.0]
    if own:
        rows_ref, grads_ref = more[:2]
        totals = [contract_rows(rows_ref[...], grads_ref[k]) for k in range(2)]
    if carried:
        totals = [total + ref[0] for total, ref in zip(totals, more[-2:])]
    for shift, x_ref, low_ref, high_ref in zip(shifts, xs, lows, highs):
        pre_gate = jnp.dot(x_ref[...], gate_ref[0], preferred_element_type=jnp.float32)
        pre_up = jnp.dot(x_ref[...], up_ref[0], preferred_element_type=jnp.float32)
        activated, derivative = silu_parts(pre_gate)
        low, high = low_ref[...].astype(jnp.float32), high_ref[...].astype(jnp.float32)
        grad_hidden = jnp.where(z_ref[0] >= shift, low, high)
        own_x = x_ref[:, columns]
        grads = (grad_hidden * pre_up * derivative, grad_hidden * activated)
        for k, grad in enumerate(grads):
            totals[k] = totals[k] + contract_rows(own_x, grad.astype(jnp.bfloat16))
    for out_ref, total in zip(outs, totals):
        out_ref[0] = total


def weight_rows(terms, own, carried, gate_weight, up_weight, groups):
    _, model_width, hidden_width = gate_weight.shape
    width = model_width // groups
    slots = terms[0][0].shape[0]
    shifts = tuple(shift for _, _, shift, _, _ in terms)
    tile = 256
    whole = pl.BlockSpec((1, width, tile), lambda i, z: (0, 0, i))
    weight = pl.BlockSpec((1, model_width, tile), lambda i, z: (0, 0, i))
    flat = pl.BlockSpec((slots, tile), lambda i, z: (0, i))
    out_shape = jax.ShapeDtypeStruct((1, width, hidden_width), jnp.float32)
    in_specs = [
        pl.BlockSpec((slots, model_width), lambda i, z, at=at: (0, at)) for _, at, *_ in terms
    ]
    in_specs += [flat] * (2 * len(terms)) + [weight, weight]
    if own:
        in_specs.append(pl.BlockSpec((slots, width), lambda i, z: (0, z[0])))
        in_specs.append(pl.BlockSpec((2, slots, tile), lambda i, z: (0, 0, i)))
    first = 1 + len(in_specs)
    return pl.pallas_call(
        functools.partial(weight_kernel, shifts, bool(own), bool(carried)),
        grid_spec=pltpu.PrefetchScalarGridSpec(
            num_scalar_prefetch=1,
            grid=(hidden_width // tile,),
            in_specs=in_specs + [whole] * len(carried),
            out_specs=(whole, whole),
        ),
        out_shape=(out_shape, out_shape),
        input_output_aliases={first + k: k for k in range(len(carried))},
        compiler_params=VMEM,
        cost_estimate=cost(),
    )(
        lax.axis_index("dp").astype(jnp.int32)[None],
        *[rows for rows, *_ in terms],
        *[low for *_, low, _ in terms],
        *[high for *_, high in terms],
        gate_weight,
        up_weight,
        *own,
        *carried,
    )


def pieces(payload_rows, block):
    depth, wide = block
    count = payload_rows // depth
    share = wide // count
    return [
        (slice(j * depth, (j + 1) * depth), slice(0, share), slice(j * share, (j + 1) * share))
        for j in range(count)
    ]


def hop_kernel(step, groups, z_ref, *refs):
    z = z_ref[0]
    for way in range(2):
        got_ref, block_ref, out_ref = refs[way], refs[2 + way], refs[4 + way]
        passed = z if way == 0 else groups - 1 - z

        @pl.when(passed < step)
        def _():
            for rows, left, right in pieces(out_ref.shape[0], block_ref.shape[1:]):
                part = block_ref[0, :, right]
                if step > 1:
                    total = part.astype(jnp.float32) + got_ref[rows, left].astype(jnp.float32)
                    part = total.astype(jnp.bfloat16)
                out_ref[rows, left] = part

        @pl.when(passed >= step)
        def _():
            width = min(got_ref.shape[1], out_ref.shape[1])
            out_ref[:, :width] = got_ref[:, :width]


def hop(step, got, partial, width):
    groups, depth, wide = partial.shape
    rows = got[0].shape[0]
    whole = pl.BlockSpec((rows, width), lambda i, z: (0, 0))
    sums = [
        pl.BlockSpec((1, depth, wide), lambda i, z: (jnp.minimum(z[0] + groups - step, groups - 1), 0, 0)),
        pl.BlockSpec((1, depth, wide), lambda i, z: (jnp.maximum(z[0] - groups + step, 0), 0, 0)),
    ]
    return pl.pallas_call(
        functools.partial(hop_kernel, step, groups),
        grid_spec=pltpu.PrefetchScalarGridSpec(
            num_scalar_prefetch=1,
            grid=(1,),
            in_specs=[pl.BlockSpec(each.shape, lambda i, z: (0, 0)) for each in got] + sums,
            out_specs=(whole, whole),
        ),
        out_shape=[jax.ShapeDtypeStruct((rows, width), jnp.bfloat16)] * 2,
        compiler_params=VMEM,
        cost_estimate=cost(),
    )(lax.axis_index("dp").astype(jnp.int32)[None], *got, partial, partial)


def last_kernel(z_ref, up_ref, down_ref, block_ref, out_ref):
    for rows, left, right in pieces(up_ref.shape[0], block_ref.shape[1:]):
        total = up_ref[rows, left].astype(jnp.float32) + down_ref[rows, left].astype(jnp.float32)
        out_ref[0, :, right] = total + block_ref[0, :, right].astype(jnp.float32)


def last_sum(got, partial):
    groups, depth, wide = partial.shape
    return pl.pallas_call(
        last_kernel,
        grid_spec=pltpu.PrefetchScalarGridSpec(
            num_scalar_prefetch=1,
            grid=(1,),
            in_specs=[pl.BlockSpec(each.shape, lambda i, z: (0, 0)) for each in got]
            + [pl.BlockSpec((1, depth, wide), lambda i, z: (z[0], 0, 0))],
            out_specs=pl.BlockSpec((1, depth, wide), lambda i, z: (0, 0, 0)),
        ),
        out_shape=jax.ShapeDtypeStruct((1, depth, wide), jnp.float32),
        compiler_params=VMEM,
        cost_estimate=cost(),
    )(lax.axis_index("dp").astype(jnp.int32)[None], *got, partial)


def shift_both(sent, groups):
    up = [(i, i + 1) for i in range(groups - 1)]
    down = [(i + 1, i) for i in range(groups - 1)]
    return lax.ppermute(sent[0], "dp", up), lax.ppermute(sent[1], "dp", down)


def local(tokens, grad_out, expert_ids, gates, gate_weight, up_weight, down_weight):
    experts = lax.axis_size("expert")
    groups = lax.axis_size("dp")
    tok_count, top_k = expert_ids.shape
    model_width = tokens.shape[1]
    capacity = 3 * tok_count * top_k // (2 * experts)
    spread = slot_table(experts, capacity)

    def exchange(rows):
        return lax.all_to_all(
            rows.reshape(experts, capacity, -1), "expert", split_axis=0, concat_axis=0, tiled=True
        ).reshape(rows.shape)

    send_x, send_ge, place, own_tokens = route(expert_ids, gates, tokens, grad_out, spread)
    batches = [(groups // 2,)] if groups % 2 == 0 else []
    batches += [(s, groups - s) for s in range((groups - 1) // 2, 0, -1)]
    below, above = [own_tokens], [own_tokens]
    for step in range(1, groups):
        lifts = [(i, i + 1) for i in range(step - 1, groups - 1)]
        drops = [(i + 1, i) for i in range(groups - step)]
        below.append(lax.ppermute(below[-1], "dp", lifts))
        above.append(lax.ppermute(above[-1], "dp", drops))

    def tokens_of(batch):
        return [side for s in batch for side in (below[s], above[groups - s])]

    placed = [place_others(tokens_of(batches[0]), top_k, spread)]
    rows_ge = exchange(send_ge)
    tied = (rows_ge, send_x, below[1], above[1])
    rows_ge, send_x, below[1], above[1] = lax.optimization_barrier(tied)
    grad_hidden = cotangent_rows(rows_ge, down_weight)
    got = [shift_both((grad_hidden, grad_hidden), groups)]

    rows_x = exchange(send_x)
    rows_x, placed[0], got[0] = lax.optimization_barrier((rows_x, placed[0], got[0]))
    grads, partial, tail = expert_rows(rows_x, rows_ge, grad_hidden, gate_weight, up_weight)
    partial = partial.reshape(groups, -1, model_width)
    back = back_rows(grads, tail, gate_weight, up_weight)
    wide = max(grad_hidden.shape[1], partial[0].size // rows_x.shape[0])

    others, own, grad_w = exchange(placed[0]), (rows_x, grads), ()
    for step in range(1, groups):
        sent = hop(step, got[-1], partial, wide)
        if step == 1:
            for batch in batches[1:]:
                sent, received = lax.optimization_barrier((sent, tokens_of(batch)))
                placed.append(place_others(received, top_k, spread))
        got.append(shift_both(sent, groups))
        if step == 1:
            got[step], back = lax.optimization_barrier((got[step], back))
        i = step - groups + len(batches)
        if i < 0:
            continue
        batch = batches[i]
        if i + 1 < len(batches):
            others, placed[i + 1] = lax.optimization_barrier((others, placed[i + 1]))
            later = exchange(placed[i + 1])
        else:
            others, back = lax.optimization_barrier((others, back))
            back = exchange(back)
        terms = [
            (others, at, s, got[s - 1][0], got[groups - s - 1][1]) for at, s in enumerate(batch)
        ]
        grad_w = weight_rows(terms, own, grad_w, gate_weight, up_weight, groups)
        own, others = (), later
        got[step], grad_w = lax.optimization_barrier((got[step], grad_w))
    grad_down_w = last_sum(got[-1], partial)

    grad_tokens = contract_rows(place, back[:, :model_width]).astype(jnp.bfloat16)
    scaled = back[:, model_width : model_width + 2].astype(jnp.float32)
    scaled = scaled[:, :1] + scaled[:, 1:]
    expert_at = np.arange(experts * capacity, dtype=np.int32)[:, None] // capacity
    gate_b = gates.T.astype(jnp.bfloat16).astype(jnp.float32)
    grad_gates = []
    for k in range(top_k):
        hit = (expert_ids[:, k][None, :] == expert_at) & (place > 0)
        grad_gates.append(jnp.sum(jnp.where(hit, scaled, 0.0), axis=0) / gate_b[k])
    grad_gates = jnp.stack(grad_gates).astype(jnp.bfloat16).T
    return (grad_tokens, grad_gates, *grad_w, grad_down_w)


def solution(mesh):
    placed = (
        P(("dp", "expert"), None),
        P(("dp", "expert"), None),
        P(("dp", "expert"), None),
        P(("dp", "expert"), None),
        P("expert", None, None),
        P("expert", None, None),
        P("expert", None, None),
    )
    return jax.shard_map(
        local,
        mesh=mesh,
        in_specs=placed,
        out_specs=(
            P(("dp", "expert"), None),
            P(("dp", "expert"), None),
            P("expert", "dp", None),
            P("expert", "dp", None),
            P("expert", "dp", None),
        ),
        check_vma=False,
    )
```

```python
import functools

import jax
import jax.numpy as jnp
import numpy as np
from jax import lax
from jax.experimental import pallas as pl
from jax.experimental.pallas import tpu as pltpu
from jax.sharding import PartitionSpec as P

LANES = 128
EXTRA = 16
CHUNKS = 1
VMEM = pltpu.CompilerParams(vmem_limit_bytes=62 * 1024 * 1024)


def contract_rows(left, right):
    return lax.dot_general(
        left, right, (((0,), (0,)), ((), ())), preferred_element_type=jnp.float32
    )


def contract_last(left, right):
    return lax.dot_general(
        left, right, (((1,), (1,)), ((), ())), preferred_element_type=jnp.float32
    )


def cost(flops=1024):
    return pl.CostEstimate(flops=flops, bytes_accessed=1024, transcendentals=0)


def chunk_ranks(capacity):
    edges = [capacity * c // CHUNKS for c in range(CHUNKS + 1)]
    return [np.arange(first, last) for first, last in zip(edges, edges[1:])]


def slot_tables(experts, capacity):
    ranks = chunk_ranks(capacity)
    rank_at = np.concatenate([np.tile(own, experts) for own in ranks])
    expert_at = np.concatenate([np.repeat(np.arange(experts), len(own)) for own in ranks])
    spread = (expert_at[:, None] == np.arange(LANES)[None, :]).astype(np.float32)
    spread[:, -1] = -rank_at
    return expert_at.astype(np.int32), jnp.asarray(spread, jnp.bfloat16)


def match_rows(id_rows):
    expert_of = lax.broadcasted_iota(jnp.int32, (LANES, id_rows[0].shape[1]), 0)
    return [each == expert_of for each in id_rows]


def chosen_slots(matches, spread):
    tok_count = matches[0].shape[1]
    named = functools.reduce(jnp.logical_or, matches)
    row = lax.broadcasted_iota(jnp.int32, (tok_count, tok_count), 0)
    col = lax.broadcasted_iota(jnp.int32, (tok_count, tok_count), 1)
    after = jnp.where(row < col, 1.0, 0.0).astype(jnp.bfloat16)
    earlier = jnp.dot(
        jnp.where(named, 1.0, 0.0).astype(jnp.bfloat16), after, preferred_element_type=jnp.float32
    )
    last = lax.broadcasted_iota(jnp.int32, named.shape, 0) == LANES - 1
    key = jnp.where(last, 1.0, jnp.where(named, earlier, -1.0)).astype(jnp.bfloat16)
    return jnp.dot(spread, key, preferred_element_type=jnp.float32) == 0.0


def route_kernel(
    tiles, ids_ref, gates_ref, spread_ref, x_ref, go_ref, place_ref, slices_ref, send_ref, weigh_ref
):
    tok_count, width = x_ref.shape
    step = pl.program_id(0)

    @pl.when(step == 0)
    def _():
        id_rows = [ids_ref[k : k + 1, :] for k in range(ids_ref.shape[0])]
        spread = spread_ref[...]
        matches = match_rows(id_rows)
        chosen = chosen_slots(matches, spread)
        gate_of = jnp.zeros(matches[0].shape, jnp.float32)
        for k, match in enumerate(matches):
            gate_of = jnp.where(match, gates_ref[k : k + 1, :], gate_of)
        gate_at = jnp.dot(spread, gate_of.astype(jnp.bfloat16), preferred_element_type=jnp.float32)
        place_ref[...] = jnp.where(chosen, 1.0, 0.0).astype(jnp.bfloat16)
        weigh_ref[...] = jnp.where(chosen, gate_at, 0.0).astype(jnp.bfloat16)

    @pl.when(step < tiles)
    def _():
        row = jnp.dot(place_ref[...], x_ref[...], preferred_element_type=jnp.float32)
        send_ref[...] = row.astype(jnp.bfloat16)
        line = lax.broadcasted_iota(jnp.int32, (EXTRA, tok_count), 0)
        tail = jnp.zeros((EXTRA, tok_count), jnp.float32)
        for k in range(ids_ref.shape[0]):
            tail = jnp.where(line == k, ids_ref[k : k + 1, :].astype(jnp.float32), tail)
        slices_ref[0, :tok_count, :] = x_ref[...]
        slices_ref[0, tok_count:, :] = jnp.zeros((EXTRA, width), jnp.bfloat16)
        slices_ref[0, tok_count:, :tok_count] = tail.astype(jnp.bfloat16)

    @pl.when(step >= tiles)
    def _():
        row = jnp.dot(weigh_ref[...], go_ref[...], preferred_element_type=jnp.float32)
        send_ref[...] = row.astype(jnp.bfloat16)


def route(expert_ids, gates, tokens, grad_out, spread, groups):
    tok_count, model_width = tokens.shape
    slots = spread.shape[0]
    width = model_width // groups
    top_k = expert_ids.shape[1]
    return pl.pallas_call(
        functools.partial(route_kernel, groups),
        grid=(2 * groups,),
        in_specs=[
            pl.BlockSpec((top_k, tok_count), lambda i: (0, 0)),
            pl.BlockSpec((top_k, tok_count), lambda i: (0, 0)),
            pl.BlockSpec((slots, LANES), lambda i: (0, 0)),
            pl.BlockSpec((tok_count, width), lambda i: (0, jnp.minimum(i, groups - 1))),
            pl.BlockSpec((tok_count, width), lambda i: (0, jnp.maximum(i - groups, 0))),
        ],
        out_specs=(
            pl.BlockSpec((slots, tok_count), lambda i: (0, 0)),
            pl.BlockSpec((1, tok_count + EXTRA, width), lambda i: (jnp.minimum(i, groups - 1), 0, 0)),
            pl.BlockSpec((slots, width), lambda i: (0, i)),
        ),
        out_shape=(
            jax.ShapeDtypeStruct((slots, tok_count), jnp.bfloat16),
            jax.ShapeDtypeStruct((groups, tok_count + EXTRA, width), jnp.bfloat16),
            jax.ShapeDtypeStruct((slots, 2 * model_width), jnp.bfloat16),
        ),
        scratch_shapes=[pltpu.VMEM((slots, tok_count), jnp.bfloat16)],
        compiler_params=VMEM,
        cost_estimate=cost(),
    )(expert_ids.T, gates.T, spread, tokens, grad_out)


def slices_kernel(top_k, spread_ref, *refs):
    out_refs, refs = refs[-CHUNKS:], refs[:-CHUNKS]
    for s, x_ref in enumerate(refs):
        tok_count, width = x_ref.shape[0] - EXTRA, x_ref.shape[1]
        tail = x_ref[tok_count:, :tok_count].astype(jnp.float32).astype(jnp.int32)
        matches = match_rows([tail[k : k + 1, :] for k in range(top_k)])
        chosen = chosen_slots(matches, spread_ref[...])
        place = jnp.where(chosen, 1.0, 0.0).astype(jnp.bfloat16)
        done = 0
        for out_ref in out_refs:
            rows = slice(done, done + out_ref.shape[0])
            done = rows.stop
            out_ref[:, s * width : (s + 1) * width] = jnp.dot(
                place[rows],
                x_ref[:tok_count, :],
                preferred_element_type=jnp.float32,
            ).astype(jnp.bfloat16)


def place_slices(received, top_k, spread, parts):
    wide = len(received) * received[0].shape[1]
    return pl.pallas_call(
        functools.partial(slices_kernel, top_k),
        out_shape=[jax.ShapeDtypeStruct((part, wide), jnp.bfloat16) for part in parts],
        compiler_params=VMEM,
        cost_estimate=cost(),
    )(spread, *received)


def down_kernel(chunks, *refs):
    out_ref = refs[-1]
    total = 0.0
    for hidden_ref, ge_ref in zip(refs[:chunks], refs[chunks:-1]):
        total += contract_rows(hidden_ref[...], ge_ref[...])
    out_ref[...] = total.astype(jnp.bfloat16)


def down_rows(hiddens, rows):
    hidden_width = hiddens[0].shape[1]
    model_width = rows[0].shape[1] // 2
    tile = 256
    return pl.pallas_call(
        functools.partial(down_kernel, len(rows)),
        grid=(hidden_width // tile,),
        in_specs=[pl.BlockSpec((each.shape[0], tile), lambda i: (0, i)) for each in hiddens]
        + [pl.BlockSpec((each.shape[0], model_width), lambda i: (0, 1)) for each in rows],
        out_specs=pl.BlockSpec((tile, model_width), lambda i: (i, 0)),
        out_shape=jax.ShapeDtypeStruct((hidden_width, model_width), jnp.bfloat16),
        compiler_params=VMEM,
        cost_estimate=cost(),
    )(*hiddens, *rows)


def weight_kernel(terms, _, *refs):
    for which, out_ref in enumerate(refs[-2:]):
        total = 0.0
        for t in range(terms):
            grads = refs[terms + t]
            grad = grads[0, which] if len(grads.shape) == 4 else grads[which]
            total += contract_rows(refs[t][...], grad)
        out_ref[0] = total


def weight_rows(terms, model_width, groups):
    hidden_width = terms[0][3].shape[-1]
    width = model_width // groups
    tile = 256

    def grads_spec(s, grads):
        if grads.ndim == 3:
            return pl.BlockSpec((*grads.shape[:2], tile), lambda i, z: (0, 0, i))
        return pl.BlockSpec(
            (1, *grads.shape[1:3], tile),
            lambda i, z: (lax.rem(z[0] + groups - s, groups), 0, 0, i),
        )

    whole = pl.BlockSpec((1, width, tile), lambda i, z: (0, 0, i))
    out_shape = jax.ShapeDtypeStruct((1, width, hidden_width), jnp.float32)
    return pl.pallas_call(
        functools.partial(weight_kernel, len(terms)),
        grid_spec=pltpu.PrefetchScalarGridSpec(
            num_scalar_prefetch=1,
            grid=(hidden_width // tile,),
            in_specs=[
                pl.BlockSpec((rows.shape[0], width), lambda i, z, at=(2 * c + 1) * groups + s: (0, at))
                for rows, c, s, _ in terms
            ]
            + [grads_spec(s, grads) for _, _, s, grads in terms],
            out_specs=(whole, whole),
        ),
        out_shape=(out_shape, out_shape),
        compiler_params=VMEM,
        cost_estimate=cost(),
    )(
        lax.axis_index("dp").astype(jnp.int32)[None],
        *[rows for rows, _, _, _ in terms],
        *[grads for _, _, _, grads in terms],
    )


def expert_kernel(
    rows_hbm, gate_hbm, up_hbm, down_hbm, hidden_hbm, grads_hbm, tail_ref, x, ge, gate, up, down, hidden, grads, sems
):
    tiles, model_width, tile = gate.shape
    asked = []

    def ask(source, target):
        copy = pltpu.make_async_copy(source, target, sems.at[len(asked)])
        copy.start()
        asked.append(copy)
        return copy

    wanted = []
    for t in range(tiles):
        cols = pl.ds(t * tile, tile)
        first = [ask(rows_hbm.at[:, pl.ds(0, model_width)], x)] if t == 0 else []
        first.append(ask(gate_hbm.at[0, :, cols], gate.at[t]))
        second = [ask(up_hbm.at[0, :, cols], up.at[t])]
        third = [ask(rows_hbm.at[:, pl.ds(model_width, model_width)], ge)] if t == 0 else []
        third.append(ask(down_hbm.at[0, cols, :], down.at[t]))
        wanted.append((first, second, third))

    total = jnp.zeros((x.shape[0], 1), jnp.float32)
    leaving = []
    for t, (first, second, third) in enumerate(wanted):
        cols = pl.ds(t * tile, tile)
        for copy in first:
            copy.wait()
        pre_gate = jnp.dot(x[...], gate[t], preferred_element_type=jnp.float32)
        for copy in second:
            copy.wait()
        pre_up = jnp.dot(x[...], up[t], preferred_element_type=jnp.float32)
        for copy in third:
            copy.wait()
        grad_hidden = contract_last(ge[...], down[t])
        sigmoid_v = 1.0 / (1.0 + jnp.exp(-pre_gate))
        activated = pre_gate * sigmoid_v
        derivative = sigmoid_v * (1.0 + pre_gate * (1.0 - sigmoid_v))
        made = (activated * pre_up).astype(jnp.bfloat16)
        hidden[t] = made
        grads[t, 0] = (grad_hidden * pre_up * derivative).astype(jnp.bfloat16)
        grads[t, 1] = (grad_hidden * activated).astype(jnp.bfloat16)
        leaving.append(ask(hidden.at[t], hidden_hbm.at[:, cols]))
        leaving.append(ask(grads.at[t], grads_hbm.at[:, :, cols]))
        total += jnp.sum(made.astype(jnp.float32) * grad_hidden, axis=1, keepdims=True)
    coarse = total.astype(jnp.bfloat16).astype(jnp.float32)
    lane = lax.broadcasted_iota(jnp.int32, tail_ref.shape, 1)
    tail = jnp.where(lane == 0, coarse, jnp.where(lane == 1, total - coarse, 0.0))
    tail_ref[...] = tail.astype(jnp.bfloat16)
    for copy in leaving:
        copy.wait()


def expert_rows(rows, gate_weight, up_weight, down_weight):
    count = rows.shape[0]
    _, model_width, hidden_width = gate_weight.shape
    tile = 256
    tiles = hidden_width // tile
    anywhere = pl.BlockSpec(memory_space=pl.ANY)
    return pl.pallas_call(
        expert_kernel,
        in_specs=[anywhere] * 4,
        out_specs=(anywhere, anywhere, pl.BlockSpec(memory_space=pltpu.VMEM)),
        out_shape=(
            jax.ShapeDtypeStruct((count, hidden_width), jnp.bfloat16),
            jax.ShapeDtypeStruct((2, count, hidden_width), jnp.bfloat16),
            jax.ShapeDtypeStruct((count, LANES), jnp.bfloat16),
        ),
        scratch_shapes=[
            pltpu.VMEM((count, model_width), jnp.bfloat16),
            pltpu.VMEM((count, model_width), jnp.bfloat16),
            pltpu.VMEM((tiles, model_width, tile), jnp.bfloat16),
            pltpu.VMEM((tiles, model_width, tile), jnp.bfloat16),
            pltpu.VMEM((tiles, tile, model_width), jnp.bfloat16),
            pltpu.VMEM((tiles, count, tile), jnp.bfloat16),
            pltpu.VMEM((tiles, 2, count, tile), jnp.bfloat16),
            pltpu.SemaphoreType.DMA((5 * tiles + 2,)),
        ],
        compiler_params=VMEM,
        cost_estimate=cost(),
    )(rows, gate_weight, up_weight, down_weight)


def back_kernel(chunk, tiles, grads_ref, slices_ref, *refs):
    step = pl.program_id(0)
    tails, (gate_ref, up_ref), out_ref = refs[: chunk + 1], refs[chunk + 1 : chunk + 3], refs[-1]

    @pl.when(step < tiles)
    def _():
        row = contract_last(grads_ref[0], gate_ref[0]) + contract_last(grads_ref[1], up_ref[0])
        out_ref[...] = row.astype(jnp.bfloat16)

    @pl.when((step >= tiles) & (step < 2 * tiles))
    def _():
        out_ref[...] = slices_ref[...]

    @pl.when(step == 2 * tiles)
    def _():
        out_ref[...] = jnp.zeros_like(out_ref)
        for c, tail_ref in enumerate(tails):
            out_ref[:, c * LANES : (c + 1) * LANES] = tail_ref[...]


def back_rows(grads, tails, slices, gate_weight, up_weight, before):
    chunk = len(before)
    _, count, hidden_width = grads.shape
    model_width = gate_weight.shape[1]
    tile = 512
    tiles = model_width // tile
    last = chunk == CHUNKS - 1
    weight = pl.BlockSpec((1, tile, hidden_width), lambda i: (0, jnp.minimum(i, tiles - 1), 0))
    return pl.pallas_call(
        functools.partial(back_kernel, chunk, tiles),
        grid=(2 * tiles + last,),
        in_specs=[
            pl.BlockSpec((2, count, hidden_width), lambda i: (0, 0, 0)),
            pl.BlockSpec((count, tile), lambda i: (0, jnp.clip(i - tiles, 0, tiles - 1))),
            *[pl.BlockSpec((count, LANES), lambda i: (0, 0)) for _ in tails],
            weight,
            weight,
            *[pl.BlockSpec(memory_space=pl.ANY) for _ in before[-1:]],
        ],
        out_specs=pl.BlockSpec(
            (count, tile), lambda i: (0, jnp.where(i < 2 * tiles, 2 * tiles * chunk + i, 2 * tiles * CHUNKS))
        ),
        out_shape=jax.ShapeDtypeStruct((count, 2 * CHUNKS * model_width + tile), jnp.bfloat16),
        input_output_aliases={4 + len(tails): 0} if before else {},
        compiler_params=VMEM,
        cost_estimate=cost(),
    )(grads, slices, *tails, gate_weight, up_weight, *before[-1:])


def exchange_groups(grads, partial, groups, early, back):
    z = lax.axis_index("dp")
    depth = partial.shape[0] // groups

    def block(index):
        index = jnp.clip(index, 0, groups - 1)
        return lax.dynamic_slice_in_dim(partial, index * depth, depth, 0)

    def total(sent, index):
        return (sent.astype(jnp.float32) + block(index).astype(jnp.float32)).astype(jnp.bfloat16)

    below, above = [grads], [grads]
    rising = falling = None
    for step in range(1, groups + 1):
        sums = step - 1
        pair = None
        if sums == 1:
            pair = (partial[-depth:], partial[:depth])
        elif sums > 1:
            pair = (total(rising, z + groups - sums), total(falling, z - groups + sums))
        if step < groups:
            low, high = below[-1], above[-1]
            if pair:
                tied = (below[-1], above[-1], pair, early)
                below[-1], above[-1], pair, early = lax.optimization_barrier(tied)
            lifts = [(i, i + 1) for i in range(step - 1, groups - 1)]
            drops = [(i + 1, i) for i in range(groups - step)]
            below.append(lax.ppermute(low, "dp", lifts))
            above.append(lax.ppermute(high, "dp", drops))
        else:
            pair, back = lax.optimization_barrier((pair, back))
        if pair:
            rising = lax.ppermute(pair[0], "dp", [(i, i + 1) for i in range(sums)])
            falling = lax.ppermute(pair[1], "dp", [(i, i - 1) for i in range(groups - sums, groups)])
    summed = block(z).astype(jnp.float32) + rising.astype(jnp.float32) + falling.astype(jnp.float32)
    return early, back, below, above, summed


def local(tokens, grad_out, expert_ids, gates, gate_weight, up_weight, down_weight):
    experts = lax.axis_size("expert")
    groups = lax.axis_size("dp")
    tok_count, top_k = expert_ids.shape
    model_width = tokens.shape[1]
    capacity = 3 * tok_count * top_k // (2 * experts)
    parts = [experts * len(own) for own in chunk_ranks(capacity)]
    expert_at, spread = slot_tables(experts, capacity)
    z = lax.axis_index("dp")

    def exchange(rows):
        return lax.all_to_all(
            rows.reshape(experts, -1, rows.shape[1]),
            "expert",
            split_axis=0,
            concat_axis=0,
            tiled=True,
        ).reshape(rows.shape)

    place, slices, *send = route(expert_ids, gates, tokens, grad_out, spread, groups)

    received = [lax.dynamic_index_in_dim(slices, z, 0, keepdims=False)]
    for shift in range(1, groups):
        mine = lax.dynamic_index_in_dim(slices, lax.rem(z + shift, groups), 0, keepdims=False)
        ring = [(i, (i + shift) % groups) for i in range(groups)]
        received.append(lax.ppermute(mine, "dp", ring))

    rows, hiddens, grads, tails, gathered, backs = [], [], [], [], [], []
    for c in range(CHUNKS):
        if c == 1:
            send[c], received = lax.optimization_barrier((send[c], received))
        rows.append(exchange(send[c]))
        if c == 0:
            send_slices = place_slices(received, top_k, spread, parts)
        if CHUNKS == 1:
            rows[c], send_slices = lax.optimization_barrier((rows[c], send_slices))
        else:
            rows[c], backs[-1] = lax.optimization_barrier((rows[c], backs[-1]))
        hidden, grad, tail = expert_rows(rows[c], gate_weight, up_weight, down_weight)
        hiddens.append(hidden)
        grads.append(grad)
        tails.append(tail)
        if c < CHUNKS - 1:
            gathered.append(lax.all_gather(grad, "dp"))
        backs.append(back_rows(grad, tails, send_slices[c], gate_weight, up_weight, backs))
    down_partial = down_rows(hiddens, rows)
    back = exchange(backs[-1])

    gathered, back, below, above, grad_down_w = exchange_groups(
        grads[-1], down_partial, groups, gathered, back
    )
    terms = [(back, c, s, each) for c, each in enumerate(gathered) for s in range(groups)]
    for s in range(groups):
        terms.append((back, CHUNKS - 1, s, below[s]))
        if s:
            terms.append((back, CHUNKS - 1, s, above[groups - s]))
    grad_w = weight_rows(terms, model_width, groups)

    grad_tokens, scaled, done = 0.0, [], 0
    for c, part in enumerate(parts):
        at = slice(done, done + part)
        done = at.stop
        first = 2 * c * model_width
        grad_tokens += contract_rows(place[at], back[:, first : first + model_width])
        first = 2 * CHUNKS * model_width + c * LANES
        pair = back[:, first : first + 2].astype(jnp.float32)
        scaled.append(pair[:, 0] + pair[:, 1])
    grad_tokens = grad_tokens.astype(jnp.bfloat16)
    scaled = jnp.concatenate(scaled)[:, None]
    gate_b = gates.T.astype(jnp.bfloat16).astype(jnp.float32)
    grad_gates = []
    for k in range(top_k):
        hit = (expert_ids[:, k][None, :] == expert_at[:, None]) & (place > 0)
        grad_gates.append(jnp.sum(jnp.where(hit, scaled, 0.0), axis=0) / gate_b[k])
    grad_gates = jnp.stack(grad_gates).astype(jnp.bfloat16).T

    return (grad_tokens, grad_gates, *grad_w, grad_down_w[None])


def solution(mesh):
    placed = (
        P(("dp", "expert"), None),
        P(("dp", "expert"), None),
        P(("dp", "expert"), None),
        P(("dp", "expert"), None),
        P("expert", None, None),
        P("expert", None, None),
        P("expert", None, None),
    )
    return jax.shard_map(
        local,
        mesh=mesh,
        in_specs=placed,
        out_specs=(
            P(("dp", "expert"), None),
            P(("dp", "expert"), None),
            P("expert", "dp", None),
            P("expert", "dp", None),
            P("expert", "dp", None),
        ),
        check_vma=False,
    )
```

```python
import functools

import jax
import jax.numpy as jnp
import numpy as np
from jax import lax
from jax.experimental import pallas as pl
from jax.experimental.pallas import tpu as pltpu
from jax.sharding import PartitionSpec as P

LANES = 128
EXTRA = 16
CHUNKS = 1
VMEM = pltpu.CompilerParams(vmem_limit_bytes=62 * 1024 * 1024)
SOME = pltpu.CompilerParams(vmem_limit_bytes=56 * 1024 * 1024)
LITTLE = pltpu.CompilerParams(vmem_limit_bytes=16 * 1024 * 1024)


def contract_rows(left, right):
    return lax.dot_general(
        left, right, (((0,), (0,)), ((), ())), preferred_element_type=jnp.float32
    )


def contract_last(left, right):
    return lax.dot_general(
        left, right, (((1,), (1,)), ((), ())), preferred_element_type=jnp.float32
    )


def cost(flops=1024):
    return pl.CostEstimate(flops=flops, bytes_accessed=1024, transcendentals=0)


def chunk_ranks(capacity):
    edges = [capacity * c // CHUNKS for c in range(CHUNKS + 1)]
    return [np.arange(first, last) for first, last in zip(edges, edges[1:])]


def slot_tables(experts, capacity):
    ranks = chunk_ranks(capacity)
    rank_at = np.concatenate([np.tile(own, experts) for own in ranks])
    expert_at = np.concatenate([np.repeat(np.arange(experts), len(own)) for own in ranks])
    spread = (expert_at[:, None] == np.arange(LANES)[None, :]).astype(np.float32)
    spread[:, -1] = -rank_at
    return expert_at.astype(np.int32), jnp.asarray(spread, jnp.bfloat16)


def match_rows(id_rows):
    expert_of = lax.broadcasted_iota(jnp.int32, (LANES, id_rows[0].shape[1]), 0)
    return [each == expert_of for each in id_rows]


def chosen_slots(matches, spread):
    tok_count = matches[0].shape[1]
    named = functools.reduce(jnp.logical_or, matches)
    row = lax.broadcasted_iota(jnp.int32, (tok_count, tok_count), 0)
    col = lax.broadcasted_iota(jnp.int32, (tok_count, tok_count), 1)
    after = jnp.where(row < col, 1.0, 0.0).astype(jnp.bfloat16)
    earlier = jnp.dot(
        jnp.where(named, 1.0, 0.0).astype(jnp.bfloat16), after, preferred_element_type=jnp.float32
    )
    last = lax.broadcasted_iota(jnp.int32, named.shape, 0) == LANES - 1
    key = jnp.where(last, 1.0, jnp.where(named, earlier, -1.0)).astype(jnp.bfloat16)
    return jnp.dot(spread, key, preferred_element_type=jnp.float32) == 0.0


def route_kernel(ids_ref, gates_ref, spread_ref, x_ref, go_ref, place_ref, slices_ref, *send_refs):
    tok_count, model_width = x_ref.shape
    groups = slices_ref.shape[0]
    id_rows = [ids_ref[k : k + 1, :] for k in range(ids_ref.shape[0])]
    spread = spread_ref[...]
    matches = match_rows(id_rows)
    chosen = chosen_slots(matches, spread)
    gate_of = jnp.zeros(matches[0].shape, jnp.float32)
    for k, match in enumerate(matches):
        gate_of = jnp.where(match, gates_ref[k : k + 1, :], gate_of)
    gate_at = jnp.dot(spread, gate_of.astype(jnp.bfloat16), preferred_element_type=jnp.float32)
    place = jnp.where(chosen, 1.0, 0.0).astype(jnp.bfloat16)
    weigh = jnp.where(chosen, gate_at, 0.0).astype(jnp.bfloat16)
    place_ref[...] = place
    width = 512
    done = 0
    for send_ref in send_refs:
        rows = slice(done, done + send_ref.shape[0])
        done = rows.stop
        for at in range(0, model_width, width):
            cols = slice(at, at + width)
            right = slice(model_width + at, model_width + at + width)
            send_ref[:, cols] = jnp.dot(
                place[rows], x_ref[:, cols], preferred_element_type=jnp.float32
            ).astype(jnp.bfloat16)
            send_ref[:, right] = jnp.dot(
                weigh[rows], go_ref[:, cols], preferred_element_type=jnp.float32
            ).astype(jnp.bfloat16)
    share = model_width // groups
    line = lax.broadcasted_iota(jnp.int32, (EXTRA, tok_count), 0)
    tail = jnp.zeros((EXTRA, tok_count), jnp.float32)
    for k, each in enumerate(id_rows):
        tail = jnp.where(line == k, each.astype(jnp.float32), tail)
    for g in range(groups):
        slices_ref[g, :tok_count, :] = x_ref[:, g * share : (g + 1) * share]
        slices_ref[g, tok_count:, :] = jnp.zeros((EXTRA, share), jnp.bfloat16)
        slices_ref[g, tok_count:, :tok_count] = tail.astype(jnp.bfloat16)


def route(expert_ids, gates, tokens, grad_out, spread, parts, groups):
    tok_count, model_width = tokens.shape
    slots = spread.shape[0]
    out_shape = (
        jax.ShapeDtypeStruct((slots, tok_count), jnp.bfloat16),
        jax.ShapeDtypeStruct((groups, tok_count + EXTRA, model_width // groups), jnp.bfloat16),
        *[jax.ShapeDtypeStruct((part, 2 * model_width), jnp.bfloat16) for part in parts],
    )
    return pl.pallas_call(
        route_kernel,
        out_shape=out_shape,
        compiler_params=VMEM,
        cost_estimate=cost(),
    )(expert_ids.T, gates.T, spread, tokens, grad_out)


def slices_kernel(top_k, spread_ref, *refs):
    out_refs, refs = refs[-CHUNKS:], refs[:-CHUNKS]
    for s, x_ref in enumerate(refs):
        tok_count, width = x_ref.shape[0] - EXTRA, x_ref.shape[1]
        tail = x_ref[tok_count:, :tok_count].astype(jnp.float32).astype(jnp.int32)
        matches = match_rows([tail[k : k + 1, :] for k in range(top_k)])
        chosen = chosen_slots(matches, spread_ref[...])
        place = jnp.where(chosen, 1.0, 0.0).astype(jnp.bfloat16)
        done = 0
        for out_ref in out_refs:
            rows = slice(done, done + out_ref.shape[0])
            done = rows.stop
            out_ref[:, s * width : (s + 1) * width] = jnp.dot(
                place[rows],
                x_ref[:tok_count, :],
                preferred_element_type=jnp.float32,
            ).astype(jnp.bfloat16)


def place_slices(received, top_k, spread, parts):
    wide = len(received) * received[0].shape[1]
    return pl.pallas_call(
        functools.partial(slices_kernel, top_k),
        out_shape=[jax.ShapeDtypeStruct((part, wide), jnp.bfloat16) for part in parts],
        compiler_params=LITTLE,
        cost_estimate=cost(),
    )(spread, *received)


def down_kernel(chunks, *refs):
    out_ref = refs[-1]
    total = 0.0
    for hidden_ref, ge_ref in zip(refs[:chunks], refs[chunks:-1]):
        total += contract_rows(hidden_ref[...], ge_ref[...])
    out_ref[...] = total.astype(jnp.bfloat16)


def down_rows(hiddens, rows):
    hidden_width = hiddens[0].shape[1]
    model_width = rows[0].shape[1] // 2
    tile = 256
    return pl.pallas_call(
        functools.partial(down_kernel, len(rows)),
        grid=(hidden_width // tile,),
        in_specs=[pl.BlockSpec((each.shape[0], tile), lambda i: (0, i)) for each in hiddens]
        + [pl.BlockSpec((each.shape[0], model_width), lambda i: (0, 1)) for each in rows],
        out_specs=pl.BlockSpec((tile, model_width), lambda i: (i, 0)),
        out_shape=jax.ShapeDtypeStruct((hidden_width, model_width), jnp.bfloat16),
        compiler_params=VMEM,
        cost_estimate=cost(),
    )(*hiddens, *rows)


def weight_kernel(terms, _, *refs):
    for which, out_ref in enumerate(refs[-2:]):
        total = 0.0
        for t in range(terms):
            grads = refs[terms + t]
            grad = grads[0, which] if len(grads.shape) == 4 else grads[which]
            total += contract_rows(refs[t][...], grad)
        out_ref[0] = total


def weight_rows(terms, model_width, groups):
    hidden_width = terms[0][3].shape[-1]
    width = model_width // groups
    tile = 256

    def grads_spec(s, grads):
        if grads.ndim == 3:
            return pl.BlockSpec((*grads.shape[:2], tile), lambda i, z: (0, 0, i))
        return pl.BlockSpec(
            (1, *grads.shape[1:3], tile),
            lambda i, z: (lax.rem(z[0] + groups - s, groups), 0, 0, i),
        )

    whole = pl.BlockSpec((1, width, tile), lambda i, z: (0, 0, i))
    out_shape = jax.ShapeDtypeStruct((1, width, hidden_width), jnp.float32)
    return pl.pallas_call(
        functools.partial(weight_kernel, len(terms)),
        grid_spec=pltpu.PrefetchScalarGridSpec(
            num_scalar_prefetch=1,
            grid=(hidden_width // tile,),
            in_specs=[
                pl.BlockSpec((rows.shape[0], width), lambda i, z, at=(2 * c + 1) * groups + s: (0, at))
                for rows, c, s, _ in terms
            ]
            + [grads_spec(s, grads) for _, _, s, grads in terms],
            out_specs=(whole, whole),
        ),
        out_shape=(out_shape, out_shape),
        compiler_params=VMEM,
        cost_estimate=cost(),
    )(
        lax.axis_index("dp").astype(jnp.int32)[None],
        *[rows for rows, _, _, _ in terms],
        *[grads for _, _, _, grads in terms],
    )


def expert_kernel(rows_ref, gate_ref, up_ref, down_ref, hidden_ref, grads_ref, tail_ref, sum_ref):
    model_width = rows_ref.shape[1] // 2
    step = pl.program_id(0)
    rows_x = rows_ref[:, :model_width]
    tile = hidden_ref.shape[1]
    at = pl.ds(pl.multiple_of(step * tile, tile), tile)
    pre_gate = jnp.dot(rows_x, gate_ref[0, :, at], preferred_element_type=jnp.float32)
    pre_up = jnp.dot(rows_x, up_ref[0], preferred_element_type=jnp.float32)
    grad_hidden = contract_last(rows_ref[:, model_width:], down_ref[0])
    sigmoid_v = 1.0 / (1.0 + jnp.exp(-pre_gate))
    activated = pre_gate * sigmoid_v
    derivative = sigmoid_v * (1.0 + pre_gate * (1.0 - sigmoid_v))
    hidden = (activated * pre_up).astype(jnp.bfloat16)
    hidden_ref[...] = hidden
    grads_ref[0] = (grad_hidden * pre_up * derivative).astype(jnp.bfloat16)
    grads_ref[1] = (grad_hidden * activated).astype(jnp.bfloat16)
    gate_grad = jnp.sum(hidden.astype(jnp.float32) * grad_hidden, axis=1, keepdims=True)

    @pl.when(step == 0)
    def _():
        sum_ref[...] = jnp.zeros_like(sum_ref)

    sum_ref[...] += gate_grad

    @pl.when(step == pl.num_programs(0) - 1)
    def _():
        total = sum_ref[...]
        coarse = total.astype(jnp.bfloat16).astype(jnp.float32)
        lane = lax.broadcasted_iota(jnp.int32, total.shape, 1)
        tail = jnp.where(lane == 0, coarse, jnp.where(lane == 1, total - coarse, 0.0))
        tail_ref[...] = tail.astype(jnp.bfloat16)


def expert_rows(rows, gate_weight, up_weight, down_weight):
    count, wide = rows.shape
    _, model_width, hidden_width = gate_weight.shape
    tile = 256
    out_shape = (
        jax.ShapeDtypeStruct((count, hidden_width), jnp.bfloat16),
        jax.ShapeDtypeStruct((2, count, hidden_width), jnp.bfloat16),
        jax.ShapeDtypeStruct((count, LANES), jnp.bfloat16),
    )
    return pl.pallas_call(
        expert_kernel,
        grid=(hidden_width // tile,),
        in_specs=[
            pl.BlockSpec((count, wide), lambda i: (0, 0)),
            pl.BlockSpec(memory_space=pltpu.VMEM),
            pl.BlockSpec((1, model_width, tile), lambda i: (0, 0, i)),
            pl.BlockSpec((1, tile, model_width), lambda i: (0, i, 0)),
        ],
        out_specs=(
            pl.BlockSpec((count, tile), lambda i: (0, i)),
            pl.BlockSpec((2, count, tile), lambda i: (0, 0, i)),
            pl.BlockSpec((count, LANES), lambda i: (0, 0)),
        ),
        out_shape=out_shape,
        scratch_shapes=[pltpu.VMEM((count, LANES), jnp.float32)],
        compiler_params=SOME,
        cost_estimate=cost(),
    )(
        rows,
        pltpu.with_memory_space_constraint(gate_weight, pltpu.VMEM),
        up_weight,
        down_weight,
    )


def back_kernel(chunk, tiles, grads_ref, slices_ref, *refs):
    step = pl.program_id(0)
    tails, (gate_ref, up_ref), out_ref = refs[: chunk + 1], refs[chunk + 1 : chunk + 3], refs[-1]

    @pl.when(step < tiles)
    def _():
        row = contract_last(grads_ref[0], gate_ref[0]) + contract_last(grads_ref[1], up_ref[0])
        out_ref[...] = row.astype(jnp.bfloat16)

    @pl.when((step >= tiles) & (step < 2 * tiles))
    def _():
        out_ref[...] = slices_ref[...]

    @pl.when(step == 2 * tiles)
    def _():
        out_ref[...] = jnp.zeros_like(out_ref)
        for c, tail_ref in enumerate(tails):
            out_ref[:, c * LANES : (c + 1) * LANES] = tail_ref[...]


def back_rows(grads, tails, slices, gate_weight, up_weight, before):
    chunk = len(before)
    _, count, hidden_width = grads.shape
    model_width = gate_weight.shape[1]
    tile = 512
    tiles = model_width // tile
    last = chunk == CHUNKS - 1
    weight = pl.BlockSpec((1, tile, hidden_width), lambda i: (0, jnp.minimum(i, tiles - 1), 0))
    return pl.pallas_call(
        functools.partial(back_kernel, chunk, tiles),
        grid=(2 * tiles + last,),
        in_specs=[
            pl.BlockSpec((2, count, hidden_width), lambda i: (0, 0, 0)),
            pl.BlockSpec((count, tile), lambda i: (0, jnp.clip(i - tiles, 0, tiles - 1))),
            *[pl.BlockSpec((count, LANES), lambda i: (0, 0)) for _ in tails],
            weight,
            weight,
            *[pl.BlockSpec(memory_space=pl.ANY) for _ in before[-1:]],
        ],
        out_specs=pl.BlockSpec(
            (count, tile), lambda i: (0, jnp.where(i < 2 * tiles, 2 * tiles * chunk + i, 2 * tiles * CHUNKS))
        ),
        out_shape=jax.ShapeDtypeStruct((count, 2 * CHUNKS * model_width + tile), jnp.bfloat16),
        input_output_aliases={4 + len(tails): 0} if before else {},
        compiler_params=VMEM,
        cost_estimate=cost(),
    )(grads, slices, *tails, gate_weight, up_weight, *before[-1:])


def exchange_groups(grads, partial, groups, early, back):
    z = lax.axis_index("dp")
    depth = partial.shape[0] // groups

    def block(index):
        index = jnp.clip(index, 0, groups - 1)
        return lax.dynamic_slice_in_dim(partial, index * depth, depth, 0)

    def total(sent, index):
        return (sent.astype(jnp.float32) + block(index).astype(jnp.float32)).astype(jnp.bfloat16)

    below, above = [grads], [grads]
    rising = falling = None
    for step in range(1, groups + 1):
        sums = step - 1
        pair = None
        if sums == 1:
            pair = (partial[-depth:], partial[:depth])
        elif sums > 1:
            pair = (total(rising, z + groups - sums), total(falling, z - groups + sums))
        if step < groups:
            low, high = below[-1], above[-1]
            if pair:
                tied = (below[-1], above[-1], pair, early)
                below[-1], above[-1], pair, early = lax.optimization_barrier(tied)
            lifts = [(i, i + 1) for i in range(step - 1, groups - 1)]
            drops = [(i + 1, i) for i in range(groups - step)]
            below.append(lax.ppermute(low, "dp", lifts))
            above.append(lax.ppermute(high, "dp", drops))
        else:
            pair, back = lax.optimization_barrier((pair, back))
        if pair:
            rising = lax.ppermute(pair[0], "dp", [(i, i + 1) for i in range(sums)])
            falling = lax.ppermute(pair[1], "dp", [(i, i - 1) for i in range(groups - sums, groups)])
    summed = block(z).astype(jnp.float32) + rising.astype(jnp.float32) + falling.astype(jnp.float32)
    return early, back, below, above, summed


def local(tokens, grad_out, expert_ids, gates, gate_weight, up_weight, down_weight):
    experts = lax.axis_size("expert")
    groups = lax.axis_size("dp")
    tok_count, top_k = expert_ids.shape
    model_width = tokens.shape[1]
    capacity = 3 * tok_count * top_k // (2 * experts)
    parts = [experts * len(own) for own in chunk_ranks(capacity)]
    expert_at, spread = slot_tables(experts, capacity)
    z = lax.axis_index("dp")

    def exchange(rows):
        return lax.all_to_all(
            rows.reshape(experts, -1, rows.shape[1]),
            "expert",
            split_axis=0,
            concat_axis=0,
            tiled=True,
        ).reshape(rows.shape)

    place, slices, *send = route(expert_ids, gates, tokens, grad_out, spread, parts, groups)

    received = [lax.dynamic_index_in_dim(slices, z, 0, keepdims=False)]
    for shift in range(1, groups):
        mine = lax.dynamic_index_in_dim(slices, lax.rem(z + shift, groups), 0, keepdims=False)
        ring = [(i, (i + shift) % groups) for i in range(groups)]
        received.append(lax.ppermute(mine, "dp", ring))

    rows, hiddens, grads, tails, gathered, backs = [], [], [], [], [], []
    for c in range(CHUNKS):
        if c == 1:
            send[c], received = lax.optimization_barrier((send[c], received))
        rows.append(exchange(send[c]))
        if c == 0:
            send_slices = place_slices(received, top_k, spread, parts)
        if CHUNKS == 1:
            rows[c], send_slices = lax.optimization_barrier((rows[c], send_slices))
        else:
            rows[c], backs[-1] = lax.optimization_barrier((rows[c], backs[-1]))
        hidden, grad, tail = expert_rows(rows[c], gate_weight, up_weight, down_weight)
        hiddens.append(hidden)
        grads.append(grad)
        tails.append(tail)
        if c < CHUNKS - 1:
            gathered.append(lax.all_gather(grad, "dp"))
        backs.append(back_rows(grad, tails, send_slices[c], gate_weight, up_weight, backs))
    down_partial = down_rows(hiddens, rows)
    back = exchange(backs[-1])

    gathered, back, below, above, grad_down_w = exchange_groups(
        grads[-1], down_partial, groups, gathered, back
    )
    terms = [(back, c, s, each) for c, each in enumerate(gathered) for s in range(groups)]
    for s in range(groups):
        terms.append((back, CHUNKS - 1, s, below[s]))
        if s:
            terms.append((back, CHUNKS - 1, s, above[groups - s]))
    grad_w = weight_rows(terms, model_width, groups)

    grad_tokens, scaled, done = 0.0, [], 0
    for c, part in enumerate(parts):
        at = slice(done, done + part)
        done = at.stop
        first = 2 * c * model_width
        grad_tokens += contract_rows(place[at], back[:, first : first + model_width])
        first = 2 * CHUNKS * model_width + c * LANES
        pair = back[:, first : first + 2].astype(jnp.float32)
        scaled.append(pair[:, 0] + pair[:, 1])
    grad_tokens = grad_tokens.astype(jnp.bfloat16)
    scaled = jnp.concatenate(scaled)[:, None]
    gate_b = gates.T.astype(jnp.bfloat16).astype(jnp.float32)
    grad_gates = []
    for k in range(top_k):
        hit = (expert_ids[:, k][None, :] == expert_at[:, None]) & (place > 0)
        grad_gates.append(jnp.sum(jnp.where(hit, scaled, 0.0), axis=0) / gate_b[k])
    grad_gates = jnp.stack(grad_gates).astype(jnp.bfloat16).T

    return (grad_tokens, grad_gates, *grad_w, grad_down_w[None])


def solution(mesh):
    placed = (
        P(("dp", "expert"), None),
        P(("dp", "expert"), None),
        P(("dp", "expert"), None),
        P(("dp", "expert"), None),
        P("expert", None, None),
        P("expert", None, None),
        P("expert", None, None),
    )
    return jax.shard_map(
        local,
        mesh=mesh,
        in_specs=placed,
        out_specs=(
            P(("dp", "expert"), None),
            P(("dp", "expert"), None),
            P("expert", "dp", None),
            P("expert", "dp", None),
            P("expert", "dp", None),
        ),
        check_vma=False,
    )
```

```python
import functools

import jax
import jax.numpy as jnp
import numpy as np
from jax import lax
from jax.experimental import pallas as pl
from jax.experimental.pallas import tpu as pltpu
from jax.sharding import PartitionSpec as P

LANES = 128
EXTRA = 16
CHUNKS = 1
VMEM = pltpu.CompilerParams(vmem_limit_bytes=62 * 1024 * 1024)
SOME = pltpu.CompilerParams(vmem_limit_bytes=56 * 1024 * 1024)
LITTLE = pltpu.CompilerParams(vmem_limit_bytes=16 * 1024 * 1024)


def contract_rows(left, right):
    return lax.dot_general(
        left, right, (((0,), (0,)), ((), ())), preferred_element_type=jnp.float32
    )


def contract_last(left, right):
    return lax.dot_general(
        left, right, (((1,), (1,)), ((), ())), preferred_element_type=jnp.float32
    )


def cost(flops=1024):
    return pl.CostEstimate(flops=flops, bytes_accessed=1024, transcendentals=0)


def chunk_ranks(capacity):
    edges = [capacity * c // CHUNKS for c in range(CHUNKS + 1)]
    return [np.arange(first, last) for first, last in zip(edges, edges[1:])]


def slot_tables(experts, capacity):
    ranks = chunk_ranks(capacity)
    rank_at = np.concatenate([np.tile(own, experts) for own in ranks])
    expert_at = np.concatenate([np.repeat(np.arange(experts), len(own)) for own in ranks])
    spread = (expert_at[:, None] == np.arange(LANES)[None, :]).astype(np.float32)
    spread[:, -1] = -rank_at
    return expert_at.astype(np.int32), jnp.asarray(spread, jnp.bfloat16)


def match_rows(id_rows):
    expert_of = lax.broadcasted_iota(jnp.int32, (LANES, id_rows[0].shape[1]), 0)
    return [each == expert_of for each in id_rows]


def chosen_slots(matches, spread):
    tok_count = matches[0].shape[1]
    named = functools.reduce(jnp.logical_or, matches)
    row = lax.broadcasted_iota(jnp.int32, (tok_count, tok_count), 0)
    col = lax.broadcasted_iota(jnp.int32, (tok_count, tok_count), 1)
    after = jnp.where(row < col, 1.0, 0.0).astype(jnp.bfloat16)
    earlier = jnp.dot(
        jnp.where(named, 1.0, 0.0).astype(jnp.bfloat16), after, preferred_element_type=jnp.float32
    )
    last = lax.broadcasted_iota(jnp.int32, named.shape, 0) == LANES - 1
    key = jnp.where(last, 1.0, jnp.where(named, earlier, -1.0)).astype(jnp.bfloat16)
    return jnp.dot(spread, key, preferred_element_type=jnp.float32) == 0.0


def route_kernel(ids_ref, gates_ref, spread_ref, x_ref, go_ref, place_ref, slices_ref, *send_refs):
    tok_count, model_width = x_ref.shape
    groups = slices_ref.shape[0]
    id_rows = [ids_ref[k : k + 1, :] for k in range(ids_ref.shape[0])]
    spread = spread_ref[...]
    matches = match_rows(id_rows)
    chosen = chosen_slots(matches, spread)
    gate_of = jnp.zeros(matches[0].shape, jnp.float32)
    for k, match in enumerate(matches):
        gate_of = jnp.where(match, gates_ref[k : k + 1, :], gate_of)
    gate_at = jnp.dot(spread, gate_of.astype(jnp.bfloat16), preferred_element_type=jnp.float32)
    place = jnp.where(chosen, 1.0, 0.0).astype(jnp.bfloat16)
    weigh = jnp.where(chosen, gate_at, 0.0).astype(jnp.bfloat16)
    place_ref[...] = place
    width = 512
    done = 0
    for send_ref in send_refs:
        rows = slice(done, done + send_ref.shape[0])
        done = rows.stop
        for at in range(0, model_width, width):
            cols = slice(at, at + width)
            right = slice(model_width + at, model_width + at + width)
            send_ref[:, cols] = jnp.dot(
                place[rows], x_ref[:, cols], preferred_element_type=jnp.float32
            ).astype(jnp.bfloat16)
            send_ref[:, right] = jnp.dot(
                weigh[rows], go_ref[:, cols], preferred_element_type=jnp.float32
            ).astype(jnp.bfloat16)
    share = model_width // groups
    line = lax.broadcasted_iota(jnp.int32, (EXTRA, tok_count), 0)
    tail = jnp.zeros((EXTRA, tok_count), jnp.float32)
    for k, each in enumerate(id_rows):
        tail = jnp.where(line == k, each.astype(jnp.float32), tail)
    for g in range(groups):
        slices_ref[g, :tok_count, :] = x_ref[:, g * share : (g + 1) * share]
        slices_ref[g, tok_count:, :] = jnp.zeros((EXTRA, share), jnp.bfloat16)
        slices_ref[g, tok_count:, :tok_count] = tail.astype(jnp.bfloat16)


def route(expert_ids, gates, tokens, grad_out, spread, parts, groups):
    tok_count, model_width = tokens.shape
    slots = spread.shape[0]
    out_shape = (
        jax.ShapeDtypeStruct((slots, tok_count), jnp.bfloat16),
        jax.ShapeDtypeStruct((groups, tok_count + EXTRA, model_width // groups), jnp.bfloat16),
        *[jax.ShapeDtypeStruct((part, 2 * model_width), jnp.bfloat16) for part in parts],
    )
    return pl.pallas_call(
        route_kernel,
        out_shape=out_shape,
        compiler_params=VMEM,
        cost_estimate=cost(),
    )(expert_ids.T, gates.T, spread, tokens, grad_out)


def slices_kernel(top_k, spread_ref, *refs):
    out_refs, refs = refs[-CHUNKS:], refs[:-CHUNKS]
    for s, x_ref in enumerate(refs):
        tok_count, width = x_ref.shape[0] - EXTRA, x_ref.shape[1]
        tail = x_ref[tok_count:, :tok_count].astype(jnp.float32).astype(jnp.int32)
        matches = match_rows([tail[k : k + 1, :] for k in range(top_k)])
        chosen = chosen_slots(matches, spread_ref[...])
        place = jnp.where(chosen, 1.0, 0.0).astype(jnp.bfloat16)
        done = 0
        for out_ref in out_refs:
            rows = slice(done, done + out_ref.shape[0])
            done = rows.stop
            out_ref[:, s * width : (s + 1) * width] = jnp.dot(
                place[rows],
                x_ref[:tok_count, :],
                preferred_element_type=jnp.float32,
            ).astype(jnp.bfloat16)


def place_slices(received, top_k, spread, parts):
    wide = len(received) * received[0].shape[1]
    return pl.pallas_call(
        functools.partial(slices_kernel, top_k),
        out_shape=[jax.ShapeDtypeStruct((part, wide), jnp.bfloat16) for part in parts],
        compiler_params=LITTLE,
        cost_estimate=cost(),
    )(spread, *received)


def down_kernel(chunks, *refs):
    out_ref = refs[-1]
    total = 0.0
    for hidden_ref, ge_ref in zip(refs[:chunks], refs[chunks:-1]):
        total += contract_rows(hidden_ref[...], ge_ref[...])
    out_ref[...] = total.astype(jnp.bfloat16)


def down_rows(hiddens, rows):
    hidden_width = hiddens[0].shape[1]
    model_width = rows[0].shape[1] // 2
    tile = 256
    return pl.pallas_call(
        functools.partial(down_kernel, len(rows)),
        grid=(hidden_width // tile,),
        in_specs=[pl.BlockSpec((each.shape[0], tile), lambda i: (0, i)) for each in hiddens]
        + [pl.BlockSpec((each.shape[0], model_width), lambda i: (0, 1)) for each in rows],
        out_specs=pl.BlockSpec((tile, model_width), lambda i: (i, 0)),
        out_shape=jax.ShapeDtypeStruct((hidden_width, model_width), jnp.bfloat16),
        compiler_params=VMEM,
        cost_estimate=cost(),
    )(*hiddens, *rows)


def weight_kernel(terms, _, *refs):
    for which, out_ref in enumerate(refs[-2:]):
        total = 0.0
        for t in range(terms):
            grads = refs[terms + t]
            grad = grads[0, which] if len(grads.shape) == 4 else grads[which]
            total += contract_rows(refs[t][...], grad)
        out_ref[0] = total


def weight_rows(terms, model_width, groups):
    hidden_width = terms[0][3].shape[-1]
    width = model_width // groups
    tile = 256

    def rows_spec(rows, first, s):
        def place(i, z):
            return 0, first + (jnp.where(z[0] == 0, 1, groups - 1) if s is None else s)

        return pl.BlockSpec((rows.shape[0], width), place)

    def grads_spec(s, grads):
        if grads.ndim == 3:
            return pl.BlockSpec((*grads.shape[:2], tile), lambda i, z: (0, 0, i))
        return pl.BlockSpec(
            (1, *grads.shape[1:3], tile),
            lambda i, z: (lax.rem(z[0] + groups - s, groups), 0, 0, i),
        )

    whole = pl.BlockSpec((1, width, tile), lambda i, z: (0, 0, i))
    out_shape = jax.ShapeDtypeStruct((1, width, hidden_width), jnp.float32)
    return pl.pallas_call(
        functools.partial(weight_kernel, len(terms)),
        grid_spec=pltpu.PrefetchScalarGridSpec(
            num_scalar_prefetch=1,
            grid=(hidden_width // tile,),
            in_specs=[rows_spec(rows, (2 * c + 1) * groups, s) for rows, c, s, _ in terms]
            + [grads_spec(s, grads) for _, _, s, grads in terms],
            out_specs=(whole, whole),
        ),
        out_shape=(out_shape, out_shape),
        compiler_params=VMEM,
        cost_estimate=cost(),
    )(
        lax.axis_index("dp").astype(jnp.int32)[None],
        *[rows for rows, _, _, _ in terms],
        *[grads for _, _, _, grads in terms],
    )


def expert_kernel(rows_ref, gate_ref, up_ref, down_ref, hidden_ref, grads_ref, tail_ref, sum_ref):
    model_width = rows_ref.shape[1] // 2
    step = pl.program_id(0)
    rows_x = rows_ref[:, :model_width]
    tile = hidden_ref.shape[1]
    at = pl.ds(pl.multiple_of(step * tile, tile), tile)
    pre_gate = jnp.dot(rows_x, gate_ref[0, :, at], preferred_element_type=jnp.float32)
    pre_up = jnp.dot(rows_x, up_ref[0], preferred_element_type=jnp.float32)
    grad_hidden = contract_last(rows_ref[:, model_width:], down_ref[0])
    sigmoid_v = 1.0 / (1.0 + jnp.exp(-pre_gate))
    activated = pre_gate * sigmoid_v
    derivative = sigmoid_v * (1.0 + pre_gate * (1.0 - sigmoid_v))
    hidden = (activated * pre_up).astype(jnp.bfloat16)
    hidden_ref[...] = hidden
    grads_ref[0] = (grad_hidden * pre_up * derivative).astype(jnp.bfloat16)
    grads_ref[1] = (grad_hidden * activated).astype(jnp.bfloat16)
    gate_grad = jnp.sum(hidden.astype(jnp.float32) * grad_hidden, axis=1, keepdims=True)

    @pl.when(step == 0)
    def _():
        sum_ref[...] = jnp.zeros_like(sum_ref)

    sum_ref[...] += gate_grad

    @pl.when(step == pl.num_programs(0) - 1)
    def _():
        total = sum_ref[...]
        coarse = total.astype(jnp.bfloat16).astype(jnp.float32)
        lane = lax.broadcasted_iota(jnp.int32, total.shape, 1)
        tail = jnp.where(lane == 0, coarse, jnp.where(lane == 1, total - coarse, 0.0))
        tail_ref[...] = tail.astype(jnp.bfloat16)


def expert_rows(rows, gate_weight, up_weight, down_weight):
    count, wide = rows.shape
    _, model_width, hidden_width = gate_weight.shape
    tile = 256
    out_shape = (
        jax.ShapeDtypeStruct((count, hidden_width), jnp.bfloat16),
        jax.ShapeDtypeStruct((2, count, hidden_width), jnp.bfloat16),
        jax.ShapeDtypeStruct((count, LANES), jnp.bfloat16),
    )
    return pl.pallas_call(
        expert_kernel,
        grid=(hidden_width // tile,),
        in_specs=[
            pl.BlockSpec((count, wide), lambda i: (0, 0)),
            pl.BlockSpec(memory_space=pltpu.VMEM),
            pl.BlockSpec((1, model_width, tile), lambda i: (0, 0, i)),
            pl.BlockSpec((1, tile, model_width), lambda i: (0, i, 0)),
        ],
        out_specs=(
            pl.BlockSpec((count, tile), lambda i: (0, i)),
            pl.BlockSpec((2, count, tile), lambda i: (0, 0, i)),
            pl.BlockSpec((count, LANES), lambda i: (0, 0)),
        ),
        out_shape=out_shape,
        scratch_shapes=[pltpu.VMEM((count, LANES), jnp.float32)],
        compiler_params=SOME,
        cost_estimate=cost(),
    )(
        rows,
        pltpu.with_memory_space_constraint(gate_weight, pltpu.VMEM),
        up_weight,
        down_weight,
    )


def back_kernel(chunk, tiles, grads_ref, slices_ref, *refs):
    step = pl.program_id(0)
    tails, (gate_ref, up_ref), out_ref = refs[: chunk + 1], refs[chunk + 1 : chunk + 3], refs[-1]

    @pl.when(step < tiles)
    def _():
        row = contract_last(grads_ref[0], gate_ref[0]) + contract_last(grads_ref[1], up_ref[0])
        out_ref[...] = row.astype(jnp.bfloat16)

    @pl.when((step >= tiles) & (step < 2 * tiles))
    def _():
        out_ref[...] = slices_ref[...]

    @pl.when(step == 2 * tiles)
    def _():
        out_ref[...] = jnp.zeros_like(out_ref)
        for c, tail_ref in enumerate(tails):
            out_ref[:, c * LANES : (c + 1) * LANES] = tail_ref[...]


def back_rows(grads, tails, slices, gate_weight, up_weight, before):
    chunk = len(before)
    _, count, hidden_width = grads.shape
    model_width = gate_weight.shape[1]
    tile = 512
    tiles = model_width // tile
    last = chunk == CHUNKS - 1
    weight = pl.BlockSpec((1, tile, hidden_width), lambda i: (0, jnp.minimum(i, tiles - 1), 0))
    return pl.pallas_call(
        functools.partial(back_kernel, chunk, tiles),
        grid=(2 * tiles + last,),
        in_specs=[
            pl.BlockSpec((2, count, hidden_width), lambda i: (0, 0, 0)),
            pl.BlockSpec((count, tile), lambda i: (0, jnp.clip(i - tiles, 0, tiles - 1))),
            *[pl.BlockSpec((count, LANES), lambda i: (0, 0)) for _ in tails],
            weight,
            weight,
            *[pl.BlockSpec(memory_space=pl.ANY) for _ in before[-1:]],
        ],
        out_specs=pl.BlockSpec(
            (count, tile), lambda i: (0, jnp.where(i < 2 * tiles, 2 * tiles * chunk + i, 2 * tiles * CHUNKS))
        ),
        out_shape=jax.ShapeDtypeStruct((count, 2 * CHUNKS * model_width + tile), jnp.bfloat16),
        input_output_aliases={4 + len(tails): 0} if before else {},
        compiler_params=VMEM,
        cost_estimate=cost(),
    )(grads, slices, *tails, gate_weight, up_weight, *before[-1:])


def exchange_groups(grads, partial, groups, early, back):
    z = lax.axis_index("dp")
    depth = partial.shape[0] // groups

    def block(index):
        index = jnp.clip(index, 0, groups - 1)
        return lax.dynamic_slice_in_dim(partial, index * depth, depth, 0)

    def total(sent, index):
        return (sent.astype(jnp.float32) + block(index).astype(jnp.float32)).astype(jnp.bfloat16)

    upper = z >= groups // 2
    apart = groups > 3
    below, above = [grads], [grads]
    rising = falling = both = None
    for step in range(1, groups + 1):
        sums = step - 1
        pair = None
        if sums == 1 and apart:
            start = jnp.where(upper, 0, (groups - 1) * depth)
            pair = (lax.dynamic_slice_in_dim(partial, start, depth, 0),)
        elif sums == 1:
            pair = (partial[-depth:], partial[:depth])
        elif sums > 1:
            pair = (total(rising, z + groups - sums), total(falling, z - groups + sums))
        if step < groups:
            low, high = below[-1], above[-1]
            if pair:
                tied = (below[-1], above[-1], pair, early)
                below[-1], above[-1], pair, early = lax.optimization_barrier(tied)
            lifts = [(i, i + 1) for i in range(step - 1, groups - 1)]
            drops = [(i + 1, i) for i in range(groups - step)]
            if step == groups - 1 and apart:
                both = lax.ppermute(jnp.where(upper, low, high), "dp", lifts + drops)
            else:
                below.append(lax.ppermute(low, "dp", lifts))
                above.append(lax.ppermute(high, "dp", drops))
        else:
            pair, back = lax.optimization_barrier((pair, back))
        if pair:
            lifts = [(i, i + 1) for i in range(sums)]
            drops = [(i, i - 1) for i in range(groups - sums, groups)]
            if len(pair) == 1:
                sent = lax.ppermute(pair[0], "dp", lifts + drops)
                rising = jnp.where(upper, 0, sent)
                falling = jnp.where(upper, sent, 0)
            else:
                rising = lax.ppermute(pair[0], "dp", lifts)
                falling = lax.ppermute(pair[1], "dp", drops)
    summed = block(z).astype(jnp.float32) + rising.astype(jnp.float32) + falling.astype(jnp.float32)
    return early, back, below, above, both, summed


def local(tokens, grad_out, expert_ids, gates, gate_weight, up_weight, down_weight):
    experts = lax.axis_size("expert")
    groups = lax.axis_size("dp")
    tok_count, top_k = expert_ids.shape
    model_width = tokens.shape[1]
    capacity = 3 * tok_count * top_k // (2 * experts)
    parts = [experts * len(own) for own in chunk_ranks(capacity)]
    expert_at, spread = slot_tables(experts, capacity)
    z = lax.axis_index("dp")

    def exchange(rows):
        return lax.all_to_all(
            rows.reshape(experts, -1, rows.shape[1]),
            "expert",
            split_axis=0,
            concat_axis=0,
            tiled=True,
        ).reshape(rows.shape)

    place, slices, *send = route(expert_ids, gates, tokens, grad_out, spread, parts, groups)

    received = [lax.dynamic_index_in_dim(slices, z, 0, keepdims=False)]
    for shift in range(1, groups):
        mine = lax.dynamic_index_in_dim(slices, lax.rem(z + shift, groups), 0, keepdims=False)
        ring = [(i, (i + shift) % groups) for i in range(groups)]
        received.append(lax.ppermute(mine, "dp", ring))

    rows, hiddens, grads, tails, gathered, backs = [], [], [], [], [], []
    for c in range(CHUNKS):
        if c == 1:
            send[c], received = lax.optimization_barrier((send[c], received))
        rows.append(exchange(send[c]))
        if c == 0:
            send_slices = place_slices(received, top_k, spread, parts)
        if CHUNKS == 1:
            rows[c], send_slices = lax.optimization_barrier((rows[c], send_slices))
        else:
            rows[c], backs[-1] = lax.optimization_barrier((rows[c], backs[-1]))
        hidden, grad, tail = expert_rows(rows[c], gate_weight, up_weight, down_weight)
        hiddens.append(hidden)
        grads.append(grad)
        tails.append(tail)
        if c < CHUNKS - 1:
            gathered.append(lax.all_gather(grad, "dp"))
        backs.append(back_rows(grad, tails, send_slices[c], gate_weight, up_weight, backs))
    down_partial = down_rows(hiddens, rows)
    back = exchange(backs[-1])

    gathered, back, below, above, both, grad_down_w = exchange_groups(
        grads[-1], down_partial, groups, gathered, back
    )
    terms = [(back, c, s, each) for c, each in enumerate(gathered) for s in range(groups)]
    for s in range(len(below)):
        terms.append((back, CHUNKS - 1, s, below[s]))
        if s:
            terms.append((back, CHUNKS - 1, groups - s, above[s]))
    if both is not None:
        terms.append((back, CHUNKS - 1, None, both))
    grad_w = weight_rows(terms, model_width, groups)

    grad_tokens, scaled, done = 0.0, [], 0
    for c, part in enumerate(parts):
        at = slice(done, done + part)
        done = at.stop
        first = 2 * c * model_width
        grad_tokens += contract_rows(place[at], back[:, first : first + model_width])
        first = 2 * CHUNKS * model_width + c * LANES
        pair = back[:, first : first + 2].astype(jnp.float32)
        scaled.append(pair[:, 0] + pair[:, 1])
    grad_tokens = grad_tokens.astype(jnp.bfloat16)
    scaled = jnp.concatenate(scaled)[:, None]
    gate_b = gates.T.astype(jnp.bfloat16).astype(jnp.float32)
    grad_gates = []
    for k in range(top_k):
        hit = (expert_ids[:, k][None, :] == expert_at[:, None]) & (place > 0)
        grad_gates.append(jnp.sum(jnp.where(hit, scaled, 0.0), axis=0) / gate_b[k])
    grad_gates = jnp.stack(grad_gates).astype(jnp.bfloat16).T

    return (grad_tokens, grad_gates, *grad_w, grad_down_w[None])


def solution(mesh):
    placed = (
        P(("dp", "expert"), None),
        P(("dp", "expert"), None),
        P(("dp", "expert"), None),
        P(("dp", "expert"), None),
        P("expert", None, None),
        P("expert", None, None),
        P("expert", None, None),
    )
    return jax.shard_map(
        local,
        mesh=mesh,
        in_specs=placed,
        out_specs=(
            P(("dp", "expert"), None),
            P(("dp", "expert"), None),
            P("expert", "dp", None),
            P("expert", "dp", None),
            P("expert", "dp", None),
        ),
        check_vma=False,
    )
```

```python
import functools

import jax
import jax.numpy as jnp
import numpy as np
from jax import lax
from jax.experimental import pallas as pl
from jax.experimental.pallas import tpu as pltpu
from jax.sharding import PartitionSpec as P

LANES = 128
EXTRA = 16
CHUNKS = 1
VMEM = pltpu.CompilerParams(vmem_limit_bytes=62 * 1024 * 1024)
SOME = pltpu.CompilerParams(vmem_limit_bytes=56 * 1024 * 1024)
LITTLE = pltpu.CompilerParams(vmem_limit_bytes=16 * 1024 * 1024)


def contract_rows(left, right):
    return lax.dot_general(
        left, right, (((0,), (0,)), ((), ())), preferred_element_type=jnp.float32
    )


def contract_last(left, right):
    return lax.dot_general(
        left, right, (((1,), (1,)), ((), ())), preferred_element_type=jnp.float32
    )


def cost(flops=1024):
    return pl.CostEstimate(flops=flops, bytes_accessed=1024, transcendentals=0)


def chunk_ranks(capacity):
    edges = [capacity * c // CHUNKS for c in range(CHUNKS + 1)]
    return [np.arange(first, last) for first, last in zip(edges, edges[1:])]


def slot_tables(experts, capacity):
    ranks = chunk_ranks(capacity)
    rank_at = np.concatenate([np.tile(own, experts) for own in ranks])
    expert_at = np.concatenate([np.repeat(np.arange(experts), len(own)) for own in ranks])
    spread = (expert_at[:, None] == np.arange(LANES)[None, :]).astype(np.float32)
    spread[:, -1] = -rank_at
    return expert_at.astype(np.int32), jnp.asarray(spread, jnp.bfloat16)


def match_rows(id_rows):
    expert_of = lax.broadcasted_iota(jnp.int32, (LANES, id_rows[0].shape[1]), 0)
    return [each == expert_of for each in id_rows]


def chosen_slots(matches, spread):
    tok_count = matches[0].shape[1]
    named = functools.reduce(jnp.logical_or, matches)
    row = lax.broadcasted_iota(jnp.int32, (tok_count, tok_count), 0)
    col = lax.broadcasted_iota(jnp.int32, (tok_count, tok_count), 1)
    after = jnp.where(row < col, 1.0, 0.0).astype(jnp.bfloat16)
    earlier = jnp.dot(
        jnp.where(named, 1.0, 0.0).astype(jnp.bfloat16), after, preferred_element_type=jnp.float32
    )
    last = lax.broadcasted_iota(jnp.int32, named.shape, 0) == LANES - 1
    key = jnp.where(last, 1.0, jnp.where(named, earlier, -1.0)).astype(jnp.bfloat16)
    return jnp.dot(spread, key, preferred_element_type=jnp.float32) == 0.0


def route_kernel(ids_ref, gates_ref, spread_ref, x_ref, go_ref, place_ref, slices_ref, send_hbm, sent, sems):
    tok_count, model_width = x_ref.shape
    groups = slices_ref.shape[0]
    id_rows = [ids_ref[k : k + 1, :] for k in range(ids_ref.shape[0])]
    spread = spread_ref[...]
    matches = match_rows(id_rows)
    chosen = chosen_slots(matches, spread)
    gate_of = jnp.zeros(matches[0].shape, jnp.float32)
    for k, match in enumerate(matches):
        gate_of = jnp.where(match, gates_ref[k : k + 1, :], gate_of)
    gate_at = jnp.dot(spread, gate_of.astype(jnp.bfloat16), preferred_element_type=jnp.float32)
    place = jnp.where(chosen, 1.0, 0.0).astype(jnp.bfloat16)
    weigh = jnp.where(chosen, gate_at, 0.0).astype(jnp.bfloat16)
    place_ref[...] = place
    count = sems.shape[0]
    depth = sent.shape[0] // count
    leaving = []
    for r in range(count):
        rows = slice(r * depth, (r + 1) * depth)
        x_rows = jnp.dot(place[rows], x_ref[...], preferred_element_type=jnp.float32)
        sent[rows, :model_width] = x_rows.astype(jnp.bfloat16)
        go_rows = jnp.dot(weigh[rows], go_ref[...], preferred_element_type=jnp.float32)
        sent[rows, model_width:] = go_rows.astype(jnp.bfloat16)
        block = pl.ds(r * depth, depth)
        copy = pltpu.make_async_copy(sent.at[block], send_hbm.at[block], sems.at[r])
        copy.start()
        leaving.append(copy)
    share = model_width // groups
    line = lax.broadcasted_iota(jnp.int32, (EXTRA, tok_count), 0)
    tail = jnp.zeros((EXTRA, tok_count), jnp.float32)
    for k, each in enumerate(id_rows):
        tail = jnp.where(line == k, each.astype(jnp.float32), tail)
    for g in range(groups):
        slices_ref[g, :tok_count, :] = x_ref[:, g * share : (g + 1) * share]
        slices_ref[g, tok_count:, :] = jnp.zeros((EXTRA, share), jnp.bfloat16)
        slices_ref[g, tok_count:, :tok_count] = tail.astype(jnp.bfloat16)
    for copy in leaving:
        copy.wait()


def route(expert_ids, gates, tokens, grad_out, spread, groups):
    tok_count, model_width = tokens.shape
    slots = spread.shape[0]
    out_shape = (
        jax.ShapeDtypeStruct((slots, tok_count), jnp.bfloat16),
        jax.ShapeDtypeStruct((groups, tok_count + EXTRA, model_width // groups), jnp.bfloat16),
        jax.ShapeDtypeStruct((slots, 2 * model_width), jnp.bfloat16),
    )
    return pl.pallas_call(
        route_kernel,
        out_specs=(
            pl.BlockSpec(memory_space=pltpu.VMEM),
            pl.BlockSpec(memory_space=pltpu.VMEM),
            pl.BlockSpec(memory_space=pl.ANY),
        ),
        out_shape=out_shape,
        scratch_shapes=[
            pltpu.VMEM((slots, 2 * model_width), jnp.bfloat16),
            pltpu.SemaphoreType.DMA((4,)),
        ],
        compiler_params=VMEM,
        cost_estimate=cost(),
    )(expert_ids.T, gates.T, spread, tokens, grad_out)


def slices_kernel(top_k, spread_ref, *refs):
    out_refs, refs = refs[-CHUNKS:], refs[:-CHUNKS]
    for s, x_ref in enumerate(refs):
        tok_count, width = x_ref.shape[0] - EXTRA, x_ref.shape[1]
        tail = x_ref[tok_count:, :tok_count].astype(jnp.float32).astype(jnp.int32)
        matches = match_rows([tail[k : k + 1, :] for k in range(top_k)])
        chosen = chosen_slots(matches, spread_ref[...])
        place = jnp.where(chosen, 1.0, 0.0).astype(jnp.bfloat16)
        done = 0
        for out_ref in out_refs:
            rows = slice(done, done + out_ref.shape[0])
            done = rows.stop
            out_ref[:, s * width : (s + 1) * width] = jnp.dot(
                place[rows],
                x_ref[:tok_count, :],
                preferred_element_type=jnp.float32,
            ).astype(jnp.bfloat16)


def place_slices(received, top_k, spread, parts):
    wide = len(received) * received[0].shape[1]
    return pl.pallas_call(
        functools.partial(slices_kernel, top_k),
        out_shape=[jax.ShapeDtypeStruct((part, wide), jnp.bfloat16) for part in parts],
        compiler_params=LITTLE,
        cost_estimate=cost(),
    )(spread, *received)


def down_kernel(chunks, *refs):
    out_ref = refs[-1]
    total = 0.0
    for hidden_ref, ge_ref in zip(refs[:chunks], refs[chunks:-1]):
        total += contract_rows(hidden_ref[...], ge_ref[...])
    out_ref[...] = total.astype(jnp.bfloat16)


def down_rows(hiddens, rows):
    hidden_width = hiddens[0].shape[1]
    model_width = rows[0].shape[1] // 2
    tile = 256
    return pl.pallas_call(
        functools.partial(down_kernel, len(rows)),
        grid=(hidden_width // tile,),
        in_specs=[pl.BlockSpec((each.shape[0], tile), lambda i: (0, i)) for each in hiddens]
        + [pl.BlockSpec((each.shape[0], model_width), lambda i: (0, 1)) for each in rows],
        out_specs=pl.BlockSpec((tile, model_width), lambda i: (i, 0)),
        out_shape=jax.ShapeDtypeStruct((hidden_width, model_width), jnp.bfloat16),
        compiler_params=VMEM,
        cost_estimate=cost(),
    )(*hiddens, *rows)


def weight_kernel(terms, _, *refs):
    for which, out_ref in enumerate(refs[-2:]):
        total = 0.0
        for t in range(terms):
            grads = refs[terms + t]
            grad = grads[0, which] if len(grads.shape) == 4 else grads[which]
            total += contract_rows(refs[t][...], grad)
        out_ref[0] = total


def weight_rows(terms, model_width, groups):
    hidden_width = terms[0][3].shape[-1]
    width = model_width // groups
    tile = 256

    def rows_spec(rows, first, s):
        def place(i, z):
            return 0, first + (jnp.where(z[0] == 0, 1, groups - 1) if s is None else s)

        return pl.BlockSpec((rows.shape[0], width), place)

    def grads_spec(s, grads):
        if grads.ndim == 3:
            return pl.BlockSpec((*grads.shape[:2], tile), lambda i, z: (0, 0, i))
        return pl.BlockSpec(
            (1, *grads.shape[1:3], tile),
            lambda i, z: (lax.rem(z[0] + groups - s, groups), 0, 0, i),
        )

    whole = pl.BlockSpec((1, width, tile), lambda i, z: (0, 0, i))
    out_shape = jax.ShapeDtypeStruct((1, width, hidden_width), jnp.float32)
    return pl.pallas_call(
        functools.partial(weight_kernel, len(terms)),
        grid_spec=pltpu.PrefetchScalarGridSpec(
            num_scalar_prefetch=1,
            grid=(hidden_width // tile,),
            in_specs=[rows_spec(rows, (2 * c + 1) * groups, s) for rows, c, s, _ in terms]
            + [grads_spec(s, grads) for _, _, s, grads in terms],
            out_specs=(whole, whole),
        ),
        out_shape=(out_shape, out_shape),
        compiler_params=VMEM,
        cost_estimate=cost(),
    )(
        lax.axis_index("dp").astype(jnp.int32)[None],
        *[rows for rows, _, _, _ in terms],
        *[grads for _, _, _, grads in terms],
    )


def expert_kernel(rows_ref, gate_ref, up_ref, down_ref, hidden_ref, grads_ref, tail_ref, sum_ref):
    model_width = rows_ref.shape[1] // 2
    step = pl.program_id(0)
    rows_x = rows_ref[:, :model_width]
    tile = hidden_ref.shape[1]
    at = pl.ds(pl.multiple_of(step * tile, tile), tile)
    pre_gate = jnp.dot(rows_x, gate_ref[0, :, at], preferred_element_type=jnp.float32)
    pre_up = jnp.dot(rows_x, up_ref[0], preferred_element_type=jnp.float32)
    grad_hidden = contract_last(rows_ref[:, model_width:], down_ref[0])
    sigmoid_v = 1.0 / (1.0 + jnp.exp(-pre_gate))
    activated = pre_gate * sigmoid_v
    derivative = sigmoid_v * (1.0 + pre_gate * (1.0 - sigmoid_v))
    hidden = (activated * pre_up).astype(jnp.bfloat16)
    hidden_ref[...] = hidden
    grads_ref[0] = (grad_hidden * pre_up * derivative).astype(jnp.bfloat16)
    grads_ref[1] = (grad_hidden * activated).astype(jnp.bfloat16)
    gate_grad = jnp.sum(hidden.astype(jnp.float32) * grad_hidden, axis=1, keepdims=True)

    @pl.when(step == 0)
    def _():
        sum_ref[...] = jnp.zeros_like(sum_ref)

    sum_ref[...] += gate_grad

    @pl.when(step == pl.num_programs(0) - 1)
    def _():
        total = sum_ref[...]
        coarse = total.astype(jnp.bfloat16).astype(jnp.float32)
        lane = lax.broadcasted_iota(jnp.int32, total.shape, 1)
        tail = jnp.where(lane == 0, coarse, jnp.where(lane == 1, total - coarse, 0.0))
        tail_ref[...] = tail.astype(jnp.bfloat16)


def expert_rows(rows, gate_weight, up_weight, down_weight):
    count, wide = rows.shape
    _, model_width, hidden_width = gate_weight.shape
    tile = 256
    out_shape = (
        jax.ShapeDtypeStruct((count, hidden_width), jnp.bfloat16),
        jax.ShapeDtypeStruct((2, count, hidden_width), jnp.bfloat16),
        jax.ShapeDtypeStruct((count, LANES), jnp.bfloat16),
    )
    return pl.pallas_call(
        expert_kernel,
        grid=(hidden_width // tile,),
        in_specs=[
            pl.BlockSpec((count, wide), lambda i: (0, 0)),
            pl.BlockSpec(memory_space=pltpu.VMEM),
            pl.BlockSpec((1, model_width, tile), lambda i: (0, 0, i)),
            pl.BlockSpec((1, tile, model_width), lambda i: (0, i, 0)),
        ],
        out_specs=(
            pl.BlockSpec((count, tile), lambda i: (0, i)),
            pl.BlockSpec((2, count, tile), lambda i: (0, 0, i)),
            pl.BlockSpec((count, LANES), lambda i: (0, 0)),
        ),
        out_shape=out_shape,
        scratch_shapes=[pltpu.VMEM((count, LANES), jnp.float32)],
        compiler_params=SOME,
        cost_estimate=cost(),
    )(
        rows,
        pltpu.with_memory_space_constraint(gate_weight, pltpu.VMEM),
        up_weight,
        down_weight,
    )


def back_kernel(chunk, tiles, grads_ref, slices_ref, *refs):
    step = pl.program_id(0)
    tails, (gate_ref, up_ref), out_ref = refs[: chunk + 1], refs[chunk + 1 : chunk + 3], refs[-1]

    @pl.when(step < tiles)
    def _():
        row = contract_last(grads_ref[0], gate_ref[0]) + contract_last(grads_ref[1], up_ref[0])
        out_ref[...] = row.astype(jnp.bfloat16)

    @pl.when((step >= tiles) & (step < 2 * tiles))
    def _():
        out_ref[...] = slices_ref[...]

    @pl.when(step == 2 * tiles)
    def _():
        out_ref[...] = jnp.zeros_like(out_ref)
        for c, tail_ref in enumerate(tails):
            out_ref[:, c * LANES : (c + 1) * LANES] = tail_ref[...]


def back_rows(grads, tails, slices, gate_weight, up_weight, before):
    chunk = len(before)
    _, count, hidden_width = grads.shape
    model_width = gate_weight.shape[1]
    tile = 512
    tiles = model_width // tile
    last = chunk == CHUNKS - 1
    weight = pl.BlockSpec((1, tile, hidden_width), lambda i: (0, jnp.minimum(i, tiles - 1), 0))
    return pl.pallas_call(
        functools.partial(back_kernel, chunk, tiles),
        grid=(2 * tiles + last,),
        in_specs=[
            pl.BlockSpec((2, count, hidden_width), lambda i: (0, 0, 0)),
            pl.BlockSpec((count, tile), lambda i: (0, jnp.clip(i - tiles, 0, tiles - 1))),
            *[pl.BlockSpec((count, LANES), lambda i: (0, 0)) for _ in tails],
            weight,
            weight,
            *[pl.BlockSpec(memory_space=pl.ANY) for _ in before[-1:]],
        ],
        out_specs=pl.BlockSpec(
            (count, tile), lambda i: (0, jnp.where(i < 2 * tiles, 2 * tiles * chunk + i, 2 * tiles * CHUNKS))
        ),
        out_shape=jax.ShapeDtypeStruct((count, 2 * CHUNKS * model_width + tile), jnp.bfloat16),
        input_output_aliases={4 + len(tails): 0} if before else {},
        compiler_params=VMEM,
        cost_estimate=cost(),
    )(grads, slices, *tails, gate_weight, up_weight, *before[-1:])


def exchange_groups(grads, partial, groups, early, back):
    z = lax.axis_index("dp")
    depth = partial.shape[0] // groups

    def block(index):
        index = jnp.clip(index, 0, groups - 1)
        return lax.dynamic_slice_in_dim(partial, index * depth, depth, 0)

    def total(sent, index):
        return (sent.astype(jnp.float32) + block(index).astype(jnp.float32)).astype(jnp.bfloat16)

    upper = z >= groups // 2
    apart = groups > 3
    below, above = [grads], [grads]
    rising = falling = both = None
    for step in range(1, groups + 1):
        sums = step - 1
        pair = None
        if sums == 1 and apart:
            start = jnp.where(upper, 0, (groups - 1) * depth)
            pair = (lax.dynamic_slice_in_dim(partial, start, depth, 0),)
        elif sums == 1:
            pair = (partial[-depth:], partial[:depth])
        elif sums > 1:
            pair = (total(rising, z + groups - sums), total(falling, z - groups + sums))
        if step < groups:
            low, high = below[-1], above[-1]
            if pair:
                tied = (below[-1], above[-1], pair, early)
                below[-1], above[-1], pair, early = lax.optimization_barrier(tied)
            lifts = [(i, i + 1) for i in range(step - 1, groups - 1)]
            drops = [(i + 1, i) for i in range(groups - step)]
            if step == groups - 1 and apart:
                both = lax.ppermute(jnp.where(upper, low, high), "dp", lifts + drops)
            else:
                below.append(lax.ppermute(low, "dp", lifts))
                above.append(lax.ppermute(high, "dp", drops))
        else:
            pair, back = lax.optimization_barrier((pair, back))
        if pair:
            lifts = [(i, i + 1) for i in range(sums)]
            drops = [(i, i - 1) for i in range(groups - sums, groups)]
            if len(pair) == 1:
                sent = lax.ppermute(pair[0], "dp", lifts + drops)
                rising = jnp.where(upper, 0, sent)
                falling = jnp.where(upper, sent, 0)
            else:
                rising = lax.ppermute(pair[0], "dp", lifts)
                falling = lax.ppermute(pair[1], "dp", drops)
    summed = block(z).astype(jnp.float32) + rising.astype(jnp.float32) + falling.astype(jnp.float32)
    return early, back, below, above, both, summed


def local(tokens, grad_out, expert_ids, gates, gate_weight, up_weight, down_weight):
    experts = lax.axis_size("expert")
    groups = lax.axis_size("dp")
    tok_count, top_k = expert_ids.shape
    model_width = tokens.shape[1]
    capacity = 3 * tok_count * top_k // (2 * experts)
    parts = [experts * len(own) for own in chunk_ranks(capacity)]
    expert_at, spread = slot_tables(experts, capacity)
    z = lax.axis_index("dp")

    def exchange(rows):
        return lax.all_to_all(
            rows.reshape(experts, -1, rows.shape[1]),
            "expert",
            split_axis=0,
            concat_axis=0,
            tiled=True,
        ).reshape(rows.shape)

    place, slices, *send = route(expert_ids, gates, tokens, grad_out, spread, groups)

    received = [lax.dynamic_index_in_dim(slices, z, 0, keepdims=False)]
    for shift in range(1, groups):
        mine = lax.dynamic_index_in_dim(slices, lax.rem(z + shift, groups), 0, keepdims=False)
        ring = [(i, (i + shift) % groups) for i in range(groups)]
        received.append(lax.ppermute(mine, "dp", ring))

    rows, hiddens, grads, tails, gathered, backs = [], [], [], [], [], []
    for c in range(CHUNKS):
        if c == 1:
            send[c], received = lax.optimization_barrier((send[c], received))
        rows.append(exchange(send[c]))
        if c == 0:
            send_slices = place_slices(received, top_k, spread, parts)
        if CHUNKS == 1:
            rows[c], send_slices = lax.optimization_barrier((rows[c], send_slices))
        else:
            rows[c], backs[-1] = lax.optimization_barrier((rows[c], backs[-1]))
        hidden, grad, tail = expert_rows(rows[c], gate_weight, up_weight, down_weight)
        hiddens.append(hidden)
        grads.append(grad)
        tails.append(tail)
        if c < CHUNKS - 1:
            gathered.append(lax.all_gather(grad, "dp"))
        backs.append(back_rows(grad, tails, send_slices[c], gate_weight, up_weight, backs))
    down_partial = down_rows(hiddens, rows)
    back = exchange(backs[-1])

    gathered, back, below, above, both, grad_down_w = exchange_groups(
        grads[-1], down_partial, groups, gathered, back
    )
    terms = [(back, c, s, each) for c, each in enumerate(gathered) for s in range(groups)]
    for s in range(len(below)):
        terms.append((back, CHUNKS - 1, s, below[s]))
        if s:
            terms.append((back, CHUNKS - 1, groups - s, above[s]))
    if both is not None:
        terms.append((back, CHUNKS - 1, None, both))
    grad_w = weight_rows(terms, model_width, groups)

    grad_tokens, scaled, done = 0.0, [], 0
    for c, part in enumerate(parts):
        at = slice(done, done + part)
        done = at.stop
        first = 2 * c * model_width
        grad_tokens += contract_rows(place[at], back[:, first : first + model_width])
        first = 2 * CHUNKS * model_width + c * LANES
        pair = back[:, first : first + 2].astype(jnp.float32)
        scaled.append(pair[:, 0] + pair[:, 1])
    grad_tokens = grad_tokens.astype(jnp.bfloat16)
    scaled = jnp.concatenate(scaled)[:, None]
    gate_b = gates.T.astype(jnp.bfloat16).astype(jnp.float32)
    grad_gates = []
    for k in range(top_k):
        hit = (expert_ids[:, k][None, :] == expert_at[:, None]) & (place > 0)
        grad_gates.append(jnp.sum(jnp.where(hit, scaled, 0.0), axis=0) / gate_b[k])
    grad_gates = jnp.stack(grad_gates).astype(jnp.bfloat16).T

    return (grad_tokens, grad_gates, *grad_w, grad_down_w[None])


def solution(mesh):
    placed = (
        P(("dp", "expert"), None),
        P(("dp", "expert"), None),
        P(("dp", "expert"), None),
        P(("dp", "expert"), None),
        P("expert", None, None),
        P("expert", None, None),
        P("expert", None, None),
    )
    return jax.shard_map(
        local,
        mesh=mesh,
        in_specs=placed,
        out_specs=(
            P(("dp", "expert"), None),
            P(("dp", "expert"), None),
            P("expert", "dp", None),
            P("expert", "dp", None),
            P("expert", "dp", None),
        ),
        check_vma=False,
    )
```

```python
import functools

import jax
import jax.numpy as jnp
import numpy as np
from jax import lax
from jax.experimental import pallas as pl
from jax.experimental.pallas import tpu as pltpu
from jax.sharding import PartitionSpec as P

LANES = 128
EXTRA = 16
CHUNKS = 1
VMEM = pltpu.CompilerParams(vmem_limit_bytes=62 * 1024 * 1024)
SOME = pltpu.CompilerParams(vmem_limit_bytes=56 * 1024 * 1024)
LITTLE = pltpu.CompilerParams(vmem_limit_bytes=16 * 1024 * 1024)


def contract_rows(left, right):
    return lax.dot_general(
        left, right, (((0,), (0,)), ((), ())), preferred_element_type=jnp.float32
    )


def contract_last(left, right):
    return lax.dot_general(
        left, right, (((1,), (1,)), ((), ())), preferred_element_type=jnp.float32
    )


def cost(flops=1024):
    return pl.CostEstimate(flops=flops, bytes_accessed=1024, transcendentals=0)


def chunk_ranks(capacity):
    edges = [capacity * c // CHUNKS for c in range(CHUNKS + 1)]
    return [np.arange(first, last) for first, last in zip(edges, edges[1:])]


def slot_tables(experts, capacity):
    ranks = chunk_ranks(capacity)
    rank_at = np.concatenate([np.tile(own, experts) for own in ranks])
    expert_at = np.concatenate([np.repeat(np.arange(experts), len(own)) for own in ranks])
    spread = (expert_at[:, None] == np.arange(LANES)[None, :]).astype(np.float32)
    spread[:, -1] = -rank_at
    return expert_at.astype(np.int32), jnp.asarray(spread, jnp.bfloat16)


def match_rows(id_rows):
    expert_of = lax.broadcasted_iota(jnp.int32, (LANES, id_rows[0].shape[1]), 0)
    return [each == expert_of for each in id_rows]


def chosen_slots(matches, spread):
    tok_count = matches[0].shape[1]
    named = functools.reduce(jnp.logical_or, matches)
    row = lax.broadcasted_iota(jnp.int32, (tok_count, tok_count), 0)
    col = lax.broadcasted_iota(jnp.int32, (tok_count, tok_count), 1)
    after = jnp.where(row < col, 1.0, 0.0).astype(jnp.bfloat16)
    earlier = jnp.dot(
        jnp.where(named, 1.0, 0.0).astype(jnp.bfloat16), after, preferred_element_type=jnp.float32
    )
    last = lax.broadcasted_iota(jnp.int32, named.shape, 0) == LANES - 1
    key = jnp.where(last, 1.0, jnp.where(named, earlier, -1.0)).astype(jnp.bfloat16)
    return jnp.dot(spread, key, preferred_element_type=jnp.float32) == 0.0


def route_kernel(ids_ref, gates_ref, spread_ref, x_ref, go_ref, place_ref, slices_ref, send_hbm, sent, sems):
    tok_count, model_width = x_ref.shape
    groups = slices_ref.shape[0]
    id_rows = [ids_ref[k : k + 1, :] for k in range(ids_ref.shape[0])]
    spread = spread_ref[...]
    matches = match_rows(id_rows)
    chosen = chosen_slots(matches, spread)
    gate_of = jnp.zeros(matches[0].shape, jnp.float32)
    for k, match in enumerate(matches):
        gate_of = jnp.where(match, gates_ref[k : k + 1, :], gate_of)
    gate_at = jnp.dot(spread, gate_of.astype(jnp.bfloat16), preferred_element_type=jnp.float32)
    place = jnp.where(chosen, 1.0, 0.0).astype(jnp.bfloat16)
    weigh = jnp.where(chosen, gate_at, 0.0).astype(jnp.bfloat16)
    place_ref[...] = place
    count = sems.shape[0]
    depth = sent.shape[0] // count
    leaving = []
    for r in range(count):
        rows = slice(r * depth, (r + 1) * depth)
        x_rows = jnp.dot(place[rows], x_ref[...], preferred_element_type=jnp.float32)
        sent[rows, :model_width] = x_rows.astype(jnp.bfloat16)
        go_rows = jnp.dot(weigh[rows], go_ref[...], preferred_element_type=jnp.float32)
        sent[rows, model_width:] = go_rows.astype(jnp.bfloat16)
        block = pl.ds(r * depth, depth)
        copy = pltpu.make_async_copy(sent.at[block], send_hbm.at[block], sems.at[r])
        copy.start()
        leaving.append(copy)
    share = model_width // groups
    line = lax.broadcasted_iota(jnp.int32, (EXTRA, tok_count), 0)
    tail = jnp.zeros((EXTRA, tok_count), jnp.float32)
    for k, each in enumerate(id_rows):
        tail = jnp.where(line == k, each.astype(jnp.float32), tail)
    for g in range(groups):
        slices_ref[g, :tok_count, :] = x_ref[:, g * share : (g + 1) * share]
        slices_ref[g, tok_count:, :] = jnp.zeros((EXTRA, share), jnp.bfloat16)
        slices_ref[g, tok_count:, :tok_count] = tail.astype(jnp.bfloat16)
    for copy in leaving:
        copy.wait()


def route(expert_ids, gates, tokens, grad_out, spread, groups):
    tok_count, model_width = tokens.shape
    slots = spread.shape[0]
    out_shape = (
        jax.ShapeDtypeStruct((slots, tok_count), jnp.bfloat16),
        jax.ShapeDtypeStruct((groups, tok_count + EXTRA, model_width // groups), jnp.bfloat16),
        jax.ShapeDtypeStruct((slots, 2 * model_width), jnp.bfloat16),
    )
    return pl.pallas_call(
        route_kernel,
        out_specs=(
            pl.BlockSpec(memory_space=pltpu.VMEM),
            pl.BlockSpec(memory_space=pltpu.VMEM),
            pl.BlockSpec(memory_space=pl.ANY),
        ),
        out_shape=out_shape,
        scratch_shapes=[
            pltpu.VMEM((slots, 2 * model_width), jnp.bfloat16),
            pltpu.SemaphoreType.DMA((4,)),
        ],
        compiler_params=VMEM,
        cost_estimate=cost(),
    )(expert_ids.T, gates.T, spread, tokens, grad_out)


def slices_kernel(top_k, spread_ref, *refs):
    out_refs, refs = refs[-CHUNKS:], refs[:-CHUNKS]
    for s, x_ref in enumerate(refs):
        tok_count, width = x_ref.shape[0] - EXTRA, x_ref.shape[1]
        tail = x_ref[tok_count:, :tok_count].astype(jnp.float32).astype(jnp.int32)
        matches = match_rows([tail[k : k + 1, :] for k in range(top_k)])
        chosen = chosen_slots(matches, spread_ref[...])
        place = jnp.where(chosen, 1.0, 0.0).astype(jnp.bfloat16)
        done = 0
        for out_ref in out_refs:
            rows = slice(done, done + out_ref.shape[0])
            done = rows.stop
            out_ref[:, s * width : (s + 1) * width] = jnp.dot(
                place[rows],
                x_ref[:tok_count, :],
                preferred_element_type=jnp.float32,
            ).astype(jnp.bfloat16)


def place_slices(received, top_k, spread, parts):
    wide = len(received) * received[0].shape[1]
    return pl.pallas_call(
        functools.partial(slices_kernel, top_k),
        out_shape=[jax.ShapeDtypeStruct((part, wide), jnp.bfloat16) for part in parts],
        compiler_params=LITTLE,
        cost_estimate=cost(),
    )(spread, *received)


def down_kernel(chunks, *refs):
    out_ref = refs[-1]
    total = 0.0
    for hidden_ref, ge_ref in zip(refs[:chunks], refs[chunks:-1]):
        total += contract_rows(hidden_ref[...], ge_ref[...])
    out_ref[...] = total.astype(jnp.bfloat16)


def down_rows(hiddens, rows):
    hidden_width = hiddens[0].shape[1]
    model_width = rows[0].shape[1] // 2
    tile = 256
    return pl.pallas_call(
        functools.partial(down_kernel, len(rows)),
        grid=(hidden_width // tile,),
        in_specs=[pl.BlockSpec((each.shape[0], tile), lambda i: (0, i)) for each in hiddens]
        + [pl.BlockSpec((each.shape[0], model_width), lambda i: (0, 1)) for each in rows],
        out_specs=pl.BlockSpec((tile, model_width), lambda i: (i, 0)),
        out_shape=jax.ShapeDtypeStruct((hidden_width, model_width), jnp.bfloat16),
        compiler_params=VMEM,
        cost_estimate=cost(),
    )(*hiddens, *rows)


def weight_kernel(terms, _, *refs):
    for which, out_ref in enumerate(refs[-2:]):
        total = 0.0
        for t in range(terms):
            grads = refs[terms + t]
            grad = grads[0, which] if len(grads.shape) == 4 else grads[which]
            total += contract_rows(refs[t][...], grad)
        out_ref[0] = total


def weight_rows(terms, model_width, groups):
    hidden_width = terms[0][3].shape[-1]
    width = model_width // groups
    tile = 256

    def rows_spec(rows, first, s):
        def place(i, z):
            return 0, first + (jnp.where(z[0] == 0, 1, groups - 1) if s is None else s)

        return pl.BlockSpec((rows.shape[0], width), place)

    def grads_spec(s, grads):
        if grads.ndim == 3:
            return pl.BlockSpec((*grads.shape[:2], tile), lambda i, z: (0, 0, i))
        return pl.BlockSpec(
            (1, *grads.shape[1:3], tile),
            lambda i, z: (lax.rem(z[0] + groups - s, groups), 0, 0, i),
        )

    whole = pl.BlockSpec((1, width, tile), lambda i, z: (0, 0, i))
    out_shape = jax.ShapeDtypeStruct((1, width, hidden_width), jnp.float32)
    return pl.pallas_call(
        functools.partial(weight_kernel, len(terms)),
        grid_spec=pltpu.PrefetchScalarGridSpec(
            num_scalar_prefetch=1,
            grid=(hidden_width // tile,),
            in_specs=[rows_spec(rows, (2 * c + 1) * groups, s) for rows, c, s, _ in terms]
            + [grads_spec(s, grads) for _, _, s, grads in terms],
            out_specs=(whole, whole),
        ),
        out_shape=(out_shape, out_shape),
        compiler_params=VMEM,
        cost_estimate=cost(),
    )(
        lax.axis_index("dp").astype(jnp.int32)[None],
        *[rows for rows, _, _, _ in terms],
        *[grads for _, _, _, grads in terms],
    )


def expert_kernel(rows_ref, gate_ref, up_ref, down_ref, hidden_ref, grads_ref, tail_ref, sum_ref):
    model_width = rows_ref.shape[1] // 2
    step = pl.program_id(0)
    rows_x = rows_ref[:, :model_width]
    tile = hidden_ref.shape[1]
    at = pl.ds(pl.multiple_of(step * tile, tile), tile)
    pre_gate = jnp.dot(rows_x, gate_ref[0, :, at], preferred_element_type=jnp.float32)
    pre_up = jnp.dot(rows_x, up_ref[0], preferred_element_type=jnp.float32)
    grad_hidden = contract_last(rows_ref[:, model_width:], down_ref[0])
    sigmoid_v = 1.0 / (1.0 + jnp.exp(-pre_gate))
    activated = pre_gate * sigmoid_v
    derivative = sigmoid_v * (1.0 + pre_gate * (1.0 - sigmoid_v))
    hidden = (activated * pre_up).astype(jnp.bfloat16)
    hidden_ref[...] = hidden
    grads_ref[0] = (grad_hidden * pre_up * derivative).astype(jnp.bfloat16)
    grads_ref[1] = (grad_hidden * activated).astype(jnp.bfloat16)
    gate_grad = jnp.sum(hidden.astype(jnp.float32) * grad_hidden, axis=1, keepdims=True)

    @pl.when(step == 0)
    def _():
        sum_ref[...] = jnp.zeros_like(sum_ref)

    sum_ref[...] += gate_grad

    @pl.when(step == pl.num_programs(0) - 1)
    def _():
        total = sum_ref[...]
        coarse = total.astype(jnp.bfloat16).astype(jnp.float32)
        lane = lax.broadcasted_iota(jnp.int32, total.shape, 1)
        tail = jnp.where(lane == 0, coarse, jnp.where(lane == 1, total - coarse, 0.0))
        tail_ref[...] = tail.astype(jnp.bfloat16)


def expert_rows(rows, gate_weight, up_weight, down_weight):
    count, wide = rows.shape
    _, model_width, hidden_width = gate_weight.shape
    tile = 256
    out_shape = (
        jax.ShapeDtypeStruct((count, hidden_width), jnp.bfloat16),
        jax.ShapeDtypeStruct((2, count, hidden_width), jnp.bfloat16),
        jax.ShapeDtypeStruct((count, LANES), jnp.bfloat16),
    )
    return pl.pallas_call(
        expert_kernel,
        grid=(hidden_width // tile,),
        in_specs=[
            pl.BlockSpec((count, wide), lambda i: (0, 0)),
            pl.BlockSpec(memory_space=pltpu.VMEM),
            pl.BlockSpec((1, model_width, tile), lambda i: (0, 0, i)),
            pl.BlockSpec((1, tile, model_width), lambda i: (0, i, 0)),
        ],
        out_specs=(
            pl.BlockSpec((count, tile), lambda i: (0, i)),
            pl.BlockSpec((2, count, tile), lambda i: (0, 0, i)),
            pl.BlockSpec((count, LANES), lambda i: (0, 0)),
        ),
        out_shape=out_shape,
        scratch_shapes=[pltpu.VMEM((count, LANES), jnp.float32)],
        compiler_params=SOME,
        cost_estimate=cost(),
    )(
        rows,
        pltpu.with_memory_space_constraint(gate_weight, pltpu.VMEM),
        up_weight,
        down_weight,
    )


def back_kernel(chunk, tiles, grads_ref, slices_ref, *refs):
    step = pl.program_id(0)
    tails, (gate_ref, up_ref), out_ref = refs[: chunk + 1], refs[chunk + 1 : chunk + 3], refs[-1]

    @pl.when(step < tiles)
    def _():
        row = contract_last(grads_ref[0], gate_ref[0]) + contract_last(grads_ref[1], up_ref[0])
        out_ref[...] = row.astype(jnp.bfloat16)

    @pl.when((step >= tiles) & (step < 2 * tiles))
    def _():
        out_ref[...] = slices_ref[...]

    @pl.when(step == 2 * tiles)
    def _():
        out_ref[...] = jnp.zeros_like(out_ref)
        for c, tail_ref in enumerate(tails):
            out_ref[:, c * LANES : (c + 1) * LANES] = tail_ref[...]


def back_rows(grads, tails, slices, gate_weight, up_weight, before):
    chunk = len(before)
    _, count, hidden_width = grads.shape
    model_width = gate_weight.shape[1]
    tile = 512
    tiles = model_width // tile
    last = chunk == CHUNKS - 1
    weight = pl.BlockSpec((1, tile, hidden_width), lambda i: (0, jnp.minimum(i, tiles - 1), 0))
    return pl.pallas_call(
        functools.partial(back_kernel, chunk, tiles),
        grid=(2 * tiles + last,),
        in_specs=[
            pl.BlockSpec((2, count, hidden_width), lambda i: (0, 0, 0)),
            pl.BlockSpec((count, tile), lambda i: (0, jnp.clip(i - tiles, 0, tiles - 1))),
            *[pl.BlockSpec((count, LANES), lambda i: (0, 0)) for _ in tails],
            weight,
            weight,
            *[pl.BlockSpec(memory_space=pl.ANY) for _ in before[-1:]],
        ],
        out_specs=pl.BlockSpec(
            (count, tile), lambda i: (0, jnp.where(i < 2 * tiles, 2 * tiles * chunk + i, 2 * tiles * CHUNKS))
        ),
        out_shape=jax.ShapeDtypeStruct((count, 2 * CHUNKS * model_width + tile), jnp.bfloat16),
        input_output_aliases={4 + len(tails): 0} if before else {},
        compiler_params=VMEM,
        cost_estimate=cost(),
    )(grads, slices, *tails, gate_weight, up_weight, *before[-1:])


def last_kernel(_, own_ref, rising_ref, falling_ref, out_ref):
    total = rising_ref[...].astype(jnp.float32) + falling_ref[...].astype(jnp.float32)
    out_ref[0] = total + own_ref[...].astype(jnp.float32)


def last_sum(partial, rising, falling):
    depth, wide = rising.shape
    tile = 48
    tiles = depth // tile
    part = pl.BlockSpec((tile, wide), lambda i, z: (i, 0))
    return pl.pallas_call(
        last_kernel,
        grid_spec=pltpu.PrefetchScalarGridSpec(
            num_scalar_prefetch=1,
            grid=(tiles,),
            in_specs=[pl.BlockSpec((tile, wide), lambda i, z: (z[0] * tiles + i, 0)), part, part],
            out_specs=pl.BlockSpec((1, tile, wide), lambda i, z: (0, i, 0)),
        ),
        out_shape=jax.ShapeDtypeStruct((1, depth, wide), jnp.float32),
        compiler_params=VMEM,
        cost_estimate=cost(),
    )(lax.axis_index("dp").astype(jnp.int32)[None], partial, rising, falling)


def exchange_groups(grads, partial, groups, early, back):
    z = lax.axis_index("dp")
    depth = partial.shape[0] // groups

    def block(index):
        index = jnp.clip(index, 0, groups - 1)
        return lax.dynamic_slice_in_dim(partial, index * depth, depth, 0)

    def total(sent, index):
        return (sent.astype(jnp.float32) + block(index).astype(jnp.float32)).astype(jnp.bfloat16)

    upper = z >= groups // 2
    apart = groups > 3
    below, above = [grads], [grads]
    rising = falling = both = None
    for step in range(1, groups + 1):
        sums = step - 1
        pair = None
        if sums == 1 and apart:
            start = jnp.where(upper, 0, (groups - 1) * depth)
            pair = (lax.dynamic_slice_in_dim(partial, start, depth, 0),)
        elif sums == 1:
            pair = (partial[-depth:], partial[:depth])
        elif sums > 1:
            pair = (total(rising, z + groups - sums), total(falling, z - groups + sums))
        if step < groups:
            low, high = below[-1], above[-1]
            if pair:
                tied = (below[-1], above[-1], pair, early)
                below[-1], above[-1], pair, early = lax.optimization_barrier(tied)
            lifts = [(i, i + 1) for i in range(step - 1, groups - 1)]
            drops = [(i + 1, i) for i in range(groups - step)]
            if step == groups - 1 and apart:
                both = lax.ppermute(jnp.where(upper, low, high), "dp", lifts + drops)
            else:
                below.append(lax.ppermute(low, "dp", lifts))
                above.append(lax.ppermute(high, "dp", drops))
        else:
            pair, back = lax.optimization_barrier((pair, back))
        if pair:
            lifts = [(i, i + 1) for i in range(sums)]
            drops = [(i, i - 1) for i in range(groups - sums, groups)]
            if len(pair) == 1:
                sent = lax.ppermute(pair[0], "dp", lifts + drops)
                rising = jnp.where(upper, 0, sent)
                falling = jnp.where(upper, sent, 0)
            else:
                rising = lax.ppermute(pair[0], "dp", lifts)
                falling = lax.ppermute(pair[1], "dp", drops)
    summed = last_sum(partial, rising, falling)
    return early, back, below, above, both, summed


def local(tokens, grad_out, expert_ids, gates, gate_weight, up_weight, down_weight):
    experts = lax.axis_size("expert")
    groups = lax.axis_size("dp")
    tok_count, top_k = expert_ids.shape
    model_width = tokens.shape[1]
    capacity = 3 * tok_count * top_k // (2 * experts)
    parts = [experts * len(own) for own in chunk_ranks(capacity)]
    expert_at, spread = slot_tables(experts, capacity)
    z = lax.axis_index("dp")

    def exchange(rows):
        return lax.all_to_all(
            rows.reshape(experts, -1, rows.shape[1]),
            "expert",
            split_axis=0,
            concat_axis=0,
            tiled=True,
        ).reshape(rows.shape)

    place, slices, *send = route(expert_ids, gates, tokens, grad_out, spread, groups)

    received = [lax.dynamic_index_in_dim(slices, z, 0, keepdims=False)]
    for shift in range(1, groups):
        mine = lax.dynamic_index_in_dim(slices, lax.rem(z + shift, groups), 0, keepdims=False)
        ring = [(i, (i + shift) % groups) for i in range(groups)]
        received.append(lax.ppermute(mine, "dp", ring))

    rows, hiddens, grads, tails, gathered, backs = [], [], [], [], [], []
    for c in range(CHUNKS):
        if c == 1:
            send[c], received = lax.optimization_barrier((send[c], received))
        rows.append(exchange(send[c]))
        if c == 0:
            send_slices = place_slices(received, top_k, spread, parts)
        if CHUNKS == 1:
            rows[c], send_slices = lax.optimization_barrier((rows[c], send_slices))
        else:
            rows[c], backs[-1] = lax.optimization_barrier((rows[c], backs[-1]))
        hidden, grad, tail = expert_rows(rows[c], gate_weight, up_weight, down_weight)
        hiddens.append(hidden)
        grads.append(grad)
        tails.append(tail)
        if c < CHUNKS - 1:
            gathered.append(lax.all_gather(grad, "dp"))
        backs.append(back_rows(grad, tails, send_slices[c], gate_weight, up_weight, backs))
    down_partial = down_rows(hiddens, rows)
    back = exchange(backs[-1])

    gathered, back, below, above, both, grad_down_w = exchange_groups(
        grads[-1], down_partial, groups, gathered, back
    )
    terms = [(back, c, s, each) for c, each in enumerate(gathered) for s in range(groups)]
    for s in range(len(below)):
        terms.append((back, CHUNKS - 1, s, below[s]))
        if s:
            terms.append((back, CHUNKS - 1, groups - s, above[s]))
    if both is not None:
        terms.append((back, CHUNKS - 1, None, both))
    grad_w = weight_rows(terms, model_width, groups)

    grad_tokens, scaled, done = 0.0, [], 0
    for c, part in enumerate(parts):
        at = slice(done, done + part)
        done = at.stop
        first = 2 * c * model_width
        grad_tokens += contract_rows(place[at], back[:, first : first + model_width])
        first = 2 * CHUNKS * model_width + c * LANES
        pair = back[:, first : first + 2].astype(jnp.float32)
        scaled.append(pair[:, 0] + pair[:, 1])
    grad_tokens = grad_tokens.astype(jnp.bfloat16)
    scaled = jnp.concatenate(scaled)[:, None]
    gate_b = gates.T.astype(jnp.bfloat16).astype(jnp.float32)
    grad_gates = []
    for k in range(top_k):
        hit = (expert_ids[:, k][None, :] == expert_at[:, None]) & (place > 0)
        grad_gates.append(jnp.sum(jnp.where(hit, scaled, 0.0), axis=0) / gate_b[k])
    grad_gates = jnp.stack(grad_gates).astype(jnp.bfloat16).T

    return (grad_tokens, grad_gates, *grad_w, grad_down_w)


def solution(mesh):
    placed = (
        P(("dp", "expert"), None),
        P(("dp", "expert"), None),
        P(("dp", "expert"), None),
        P(("dp", "expert"), None),
        P("expert", None, None),
        P("expert", None, None),
        P("expert", None, None),
    )
    return jax.shard_map(
        local,
        mesh=mesh,
        in_specs=placed,
        out_specs=(
            P(("dp", "expert"), None),
            P(("dp", "expert"), None),
            P("expert", "dp", None),
            P("expert", "dp", None),
            P("expert", "dp", None),
        ),
        check_vma=False,
    )
```

```python
import functools

import jax
import jax.numpy as jnp
import numpy as np
from jax import lax
from jax.experimental import pallas as pl
from jax.experimental.pallas import tpu as pltpu
from jax.sharding import PartitionSpec as P

LANES = 128
EXTRA = 16
CHUNKS = 1
VMEM = pltpu.CompilerParams(vmem_limit_bytes=62 * 1024 * 1024)
SOME = pltpu.CompilerParams(vmem_limit_bytes=56 * 1024 * 1024)
LITTLE = pltpu.CompilerParams(vmem_limit_bytes=16 * 1024 * 1024)


def contract_rows(left, right):
    return lax.dot_general(
        left, right, (((0,), (0,)), ((), ())), preferred_element_type=jnp.float32
    )


def contract_last(left, right):
    return lax.dot_general(
        left, right, (((1,), (1,)), ((), ())), preferred_element_type=jnp.float32
    )


def cost(flops=1024):
    return pl.CostEstimate(flops=flops, bytes_accessed=1024, transcendentals=0)


def chunk_ranks(capacity):
    edges = [capacity * c // CHUNKS for c in range(CHUNKS + 1)]
    return [np.arange(first, last) for first, last in zip(edges, edges[1:])]


def slot_tables(experts, capacity):
    ranks = chunk_ranks(capacity)
    rank_at = np.concatenate([np.tile(own, experts) for own in ranks])
    expert_at = np.concatenate([np.repeat(np.arange(experts), len(own)) for own in ranks])
    spread = (expert_at[:, None] == np.arange(LANES)[None, :]).astype(np.float32)
    spread[:, -1] = -rank_at
    return expert_at.astype(np.int32), jnp.asarray(spread, jnp.bfloat16)


def match_rows(id_rows):
    expert_of = lax.broadcasted_iota(jnp.int32, (LANES, id_rows[0].shape[1]), 0)
    return [each == expert_of for each in id_rows]


def chosen_slots(matches, spread):
    tok_count = matches[0].shape[1]
    named = functools.reduce(jnp.logical_or, matches)
    row = lax.broadcasted_iota(jnp.int32, (tok_count, tok_count), 0)
    col = lax.broadcasted_iota(jnp.int32, (tok_count, tok_count), 1)
    after = jnp.where(row < col, 1.0, 0.0).astype(jnp.bfloat16)
    earlier = jnp.dot(
        jnp.where(named, 1.0, 0.0).astype(jnp.bfloat16), after, preferred_element_type=jnp.float32
    )
    last = lax.broadcasted_iota(jnp.int32, named.shape, 0) == LANES - 1
    key = jnp.where(last, 1.0, jnp.where(named, earlier, -1.0)).astype(jnp.bfloat16)
    return jnp.dot(spread, key, preferred_element_type=jnp.float32) == 0.0


def route_kernel(ids_ref, gates_ref, spread_ref, x_ref, go_ref, place_ref, slices_ref, send_hbm, sent, sems):
    tok_count, model_width = x_ref.shape
    groups = slices_ref.shape[0]
    id_rows = [ids_ref[k : k + 1, :] for k in range(ids_ref.shape[0])]
    spread = spread_ref[...]
    matches = match_rows(id_rows)
    chosen = chosen_slots(matches, spread)
    gate_of = jnp.zeros(matches[0].shape, jnp.float32)
    for k, match in enumerate(matches):
        gate_of = jnp.where(match, gates_ref[k : k + 1, :], gate_of)
    gate_at = jnp.dot(spread, gate_of.astype(jnp.bfloat16), preferred_element_type=jnp.float32)
    place = jnp.where(chosen, 1.0, 0.0).astype(jnp.bfloat16)
    weigh = jnp.where(chosen, gate_at, 0.0).astype(jnp.bfloat16)
    place_ref[...] = place
    count = sems.shape[0]
    depth = sent.shape[0] // count
    leaving = []
    for r in range(count):
        rows = slice(r * depth, (r + 1) * depth)
        x_rows = jnp.dot(place[rows], x_ref[...], preferred_element_type=jnp.float32)
        sent[rows, :model_width] = x_rows.astype(jnp.bfloat16)
        go_rows = jnp.dot(weigh[rows], go_ref[...], preferred_element_type=jnp.float32)
        sent[rows, model_width:] = go_rows.astype(jnp.bfloat16)
        block = pl.ds(r * depth, depth)
        copy = pltpu.make_async_copy(sent.at[block], send_hbm.at[block], sems.at[r])
        copy.start()
        leaving.append(copy)
    share = model_width // groups
    line = lax.broadcasted_iota(jnp.int32, (EXTRA, tok_count), 0)
    tail = jnp.zeros((EXTRA, tok_count), jnp.float32)
    for k, each in enumerate(id_rows):
        tail = jnp.where(line == k, each.astype(jnp.float32), tail)
    for g in range(groups):
        slices_ref[g, :tok_count, :] = x_ref[:, g * share : (g + 1) * share]
        slices_ref[g, tok_count:, :] = jnp.zeros((EXTRA, share), jnp.bfloat16)
        slices_ref[g, tok_count:, :tok_count] = tail.astype(jnp.bfloat16)
    for copy in leaving:
        copy.wait()


def route(expert_ids, gates, tokens, grad_out, spread, groups):
    tok_count, model_width = tokens.shape
    slots = spread.shape[0]
    out_shape = (
        jax.ShapeDtypeStruct((slots, tok_count), jnp.bfloat16),
        jax.ShapeDtypeStruct((groups, tok_count + EXTRA, model_width // groups), jnp.bfloat16),
        jax.ShapeDtypeStruct((slots, 2 * model_width), jnp.bfloat16),
    )
    return pl.pallas_call(
        route_kernel,
        out_specs=(
            pl.BlockSpec(memory_space=pltpu.VMEM),
            pl.BlockSpec(memory_space=pltpu.VMEM),
            pl.BlockSpec(memory_space=pl.ANY),
        ),
        out_shape=out_shape,
        scratch_shapes=[
            pltpu.VMEM((slots, 2 * model_width), jnp.bfloat16),
            pltpu.SemaphoreType.DMA((4,)),
        ],
        compiler_params=VMEM,
        cost_estimate=cost(),
    )(expert_ids.T, gates.T, spread, tokens, grad_out)


def slices_kernel(top_k, spread_ref, *refs):
    out_refs, refs = refs[-CHUNKS:], refs[:-CHUNKS]
    for s, x_ref in enumerate(refs):
        tok_count, width = x_ref.shape[0] - EXTRA, x_ref.shape[1]
        tail = x_ref[tok_count:, :tok_count].astype(jnp.float32).astype(jnp.int32)
        matches = match_rows([tail[k : k + 1, :] for k in range(top_k)])
        chosen = chosen_slots(matches, spread_ref[...])
        place = jnp.where(chosen, 1.0, 0.0).astype(jnp.bfloat16)
        done = 0
        for out_ref in out_refs:
            rows = slice(done, done + out_ref.shape[0])
            done = rows.stop
            out_ref[:, s * width : (s + 1) * width] = jnp.dot(
                place[rows],
                x_ref[:tok_count, :],
                preferred_element_type=jnp.float32,
            ).astype(jnp.bfloat16)


def place_slices(received, top_k, spread, parts):
    wide = len(received) * received[0].shape[1]
    return pl.pallas_call(
        functools.partial(slices_kernel, top_k),
        out_shape=[jax.ShapeDtypeStruct((part, wide), jnp.bfloat16) for part in parts],
        compiler_params=LITTLE,
        cost_estimate=cost(),
    )(spread, *received)


def down_kernel(chunks, *refs):
    out_ref = refs[-1]
    total = 0.0
    for hidden_ref, ge_ref in zip(refs[:chunks], refs[chunks:-1]):
        total += contract_rows(hidden_ref[...], ge_ref[...])
    out_ref[...] = total.astype(jnp.bfloat16)


def down_rows(hiddens, rows):
    hidden_width = hiddens[0].shape[1]
    model_width = rows[0].shape[1] // 2
    tile = 256
    return pl.pallas_call(
        functools.partial(down_kernel, len(rows)),
        grid=(hidden_width // tile,),
        in_specs=[pl.BlockSpec((each.shape[0], tile), lambda i: (0, i)) for each in hiddens]
        + [pl.BlockSpec((each.shape[0], model_width), lambda i: (0, 1)) for each in rows],
        out_specs=pl.BlockSpec((tile, model_width), lambda i: (i, 0)),
        out_shape=jax.ShapeDtypeStruct((hidden_width, model_width), jnp.bfloat16),
        compiler_params=VMEM,
        cost_estimate=cost(),
    )(*hiddens, *rows)


def weight_kernel(terms, _, *refs):
    for which, out_ref in enumerate(refs[-2:]):
        total = 0.0
        for t in range(terms):
            grads = refs[terms + t]
            grad = grads[0, which] if len(grads.shape) == 4 else grads[which]
            total += contract_rows(refs[t][...], grad)
        out_ref[0] = total


def weight_rows(terms, model_width, groups):
    hidden_width = terms[0][3].shape[-1]
    width = model_width // groups
    tile = 256

    def rows_spec(rows, first, s):
        def place(i, z):
            return 0, first + (jnp.where(z[0] == 0, 1, groups - 1) if s is None else s)

        return pl.BlockSpec((rows.shape[0], width), place)

    def grads_spec(s, grads):
        if grads.ndim == 3:
            return pl.BlockSpec((*grads.shape[:2], tile), lambda i, z: (0, 0, i))
        return pl.BlockSpec(
            (1, *grads.shape[1:3], tile),
            lambda i, z: (lax.rem(z[0] + groups - s, groups), 0, 0, i),
        )

    whole = pl.BlockSpec((1, width, tile), lambda i, z: (0, 0, i))
    out_shape = jax.ShapeDtypeStruct((1, width, hidden_width), jnp.float32)
    return pl.pallas_call(
        functools.partial(weight_kernel, len(terms)),
        grid_spec=pltpu.PrefetchScalarGridSpec(
            num_scalar_prefetch=1,
            grid=(hidden_width // tile,),
            in_specs=[rows_spec(rows, (2 * c + 1) * groups, s) for rows, c, s, _ in terms]
            + [grads_spec(s, grads) for _, _, s, grads in terms],
            out_specs=(whole, whole),
        ),
        out_shape=(out_shape, out_shape),
        compiler_params=VMEM,
        cost_estimate=cost(),
    )(
        lax.axis_index("dp").astype(jnp.int32)[None],
        *[rows for rows, _, _, _ in terms],
        *[grads for _, _, _, grads in terms],
    )


def expert_kernel(rows_ref, gate_ref, up_ref, down_ref, hidden_ref, grads_ref, tail_ref, sum_ref):
    model_width = rows_ref.shape[1] // 2
    step = pl.program_id(0)
    rows_x = rows_ref[:, :model_width]
    tile = hidden_ref.shape[1]
    at = pl.ds(pl.multiple_of(step * tile, tile), tile)
    pre_gate = jnp.dot(rows_x, gate_ref[0, :, at], preferred_element_type=jnp.float32)
    pre_up = jnp.dot(rows_x, up_ref[0], preferred_element_type=jnp.float32)
    grad_hidden = contract_last(rows_ref[:, model_width:], down_ref[0])
    sigmoid_v = 1.0 / (1.0 + jnp.exp(-pre_gate))
    activated = pre_gate * sigmoid_v
    derivative = sigmoid_v * (1.0 + pre_gate * (1.0 - sigmoid_v))
    hidden = (activated * pre_up).astype(jnp.bfloat16)
    hidden_ref[...] = hidden
    grads_ref[0] = (grad_hidden * pre_up * derivative).astype(jnp.bfloat16)
    grads_ref[1] = (grad_hidden * activated).astype(jnp.bfloat16)
    gate_grad = jnp.sum(hidden.astype(jnp.float32) * grad_hidden, axis=1, keepdims=True)

    @pl.when(step == 0)
    def _():
        sum_ref[...] = jnp.zeros_like(sum_ref)

    sum_ref[...] += gate_grad

    @pl.when(step == pl.num_programs(0) - 1)
    def _():
        total = sum_ref[...]
        coarse = total.astype(jnp.bfloat16).astype(jnp.float32)
        lane = lax.broadcasted_iota(jnp.int32, total.shape, 1)
        tail = jnp.where(lane == 0, coarse, jnp.where(lane == 1, total - coarse, 0.0))
        tail_ref[...] = tail.astype(jnp.bfloat16)


def expert_rows(rows, gate_weight, up_weight, down_weight):
    count, wide = rows.shape
    _, model_width, hidden_width = gate_weight.shape
    tile = 256
    out_shape = (
        jax.ShapeDtypeStruct((count, hidden_width), jnp.bfloat16),
        jax.ShapeDtypeStruct((2, count, hidden_width), jnp.bfloat16),
        jax.ShapeDtypeStruct((count, LANES), jnp.bfloat16),
    )
    return pl.pallas_call(
        expert_kernel,
        grid=(hidden_width // tile,),
        in_specs=[
            pl.BlockSpec((count, wide), lambda i: (0, 0)),
            pl.BlockSpec(memory_space=pltpu.VMEM),
            pl.BlockSpec((1, model_width, tile), lambda i: (0, 0, i)),
            pl.BlockSpec((1, tile, model_width), lambda i: (0, i, 0)),
        ],
        out_specs=(
            pl.BlockSpec((count, tile), lambda i: (0, i)),
            pl.BlockSpec((2, count, tile), lambda i: (0, 0, i)),
            pl.BlockSpec((count, LANES), lambda i: (0, 0)),
        ),
        out_shape=out_shape,
        scratch_shapes=[pltpu.VMEM((count, LANES), jnp.float32)],
        compiler_params=SOME,
        cost_estimate=cost(),
    )(
        rows,
        pltpu.with_memory_space_constraint(gate_weight, pltpu.VMEM),
        up_weight,
        down_weight,
    )


def back_kernel(chunk, tiles, grads_ref, slices_ref, *refs):
    step = pl.program_id(0)
    tails, (gate_ref, up_ref), out_ref = refs[: chunk + 1], refs[chunk + 1 : chunk + 3], refs[-1]

    @pl.when(step < tiles)
    def _():
        row = contract_last(grads_ref[0], gate_ref[0]) + contract_last(grads_ref[1], up_ref[0])
        out_ref[...] = row.astype(jnp.bfloat16)

    @pl.when((step >= tiles) & (step < 2 * tiles))
    def _():
        out_ref[...] = slices_ref[...]

    @pl.when(step == 2 * tiles)
    def _():
        out_ref[...] = jnp.zeros_like(out_ref)
        for c, tail_ref in enumerate(tails):
            out_ref[:, c * LANES : (c + 1) * LANES] = tail_ref[...]


def back_rows(grads, tails, slices, gate_weight, up_weight, before):
    chunk = len(before)
    _, count, hidden_width = grads.shape
    model_width = gate_weight.shape[1]
    tile = 512
    tiles = model_width // tile
    last = chunk == CHUNKS - 1
    weight = pl.BlockSpec((1, tile, hidden_width), lambda i: (0, jnp.minimum(i, tiles - 1), 0))
    return pl.pallas_call(
        functools.partial(back_kernel, chunk, tiles),
        grid=(2 * tiles + last,),
        in_specs=[
            pl.BlockSpec((2, count, hidden_width), lambda i: (0, 0, 0)),
            pl.BlockSpec((count, tile), lambda i: (0, jnp.clip(i - tiles, 0, tiles - 1))),
            *[pl.BlockSpec((count, LANES), lambda i: (0, 0)) for _ in tails],
            weight,
            weight,
            *[pl.BlockSpec(memory_space=pl.ANY) for _ in before[-1:]],
        ],
        out_specs=pl.BlockSpec(
            (count, tile), lambda i: (0, jnp.where(i < 2 * tiles, 2 * tiles * chunk + i, 2 * tiles * CHUNKS))
        ),
        out_shape=jax.ShapeDtypeStruct((count, 2 * CHUNKS * model_width + tile), jnp.bfloat16),
        input_output_aliases={4 + len(tails): 0} if before else {},
        compiler_params=VMEM,
        cost_estimate=cost(),
    )(grads, slices, *tails, gate_weight, up_weight, *before[-1:])


def exchange_groups(grads, partial, groups, early, back):
    z = lax.axis_index("dp")
    depth = partial.shape[0] // groups

    def block(index):
        index = jnp.clip(index, 0, groups - 1)
        return lax.dynamic_slice_in_dim(partial, index * depth, depth, 0)

    def total(sent, index):
        return (sent.astype(jnp.float32) + block(index).astype(jnp.float32)).astype(jnp.bfloat16)

    upper = z >= groups // 2
    apart = groups > 3
    below, above = [grads], [grads]
    rising = falling = both = None
    for step in range(1, groups + 1):
        sums = step - 1
        pair = None
        if sums == 1 and apart:
            start = jnp.where(upper, 0, (groups - 1) * depth)
            pair = (lax.dynamic_slice_in_dim(partial, start, depth, 0),)
        elif sums == 1:
            pair = (partial[-depth:], partial[:depth])
        elif sums > 1:
            pair = (total(rising, z + groups - sums), total(falling, z - groups + sums))
        if step < groups:
            low, high = below[-1], above[-1]
            if sums > 1:
                tied = (below[-1], above[-1], pair, early)
                below[-1], above[-1], pair, early = lax.optimization_barrier(tied)
            lifts = [(i, i + 1) for i in range(step - 1, groups - 1)]
            drops = [(i + 1, i) for i in range(groups - step)]
            if step == groups - 1 and apart:
                both = lax.ppermute(jnp.where(upper, low, high), "dp", lifts + drops)
            else:
                below.append(lax.ppermute(low, "dp", lifts))
                above.append(lax.ppermute(high, "dp", drops))
        else:
            pair, back = lax.optimization_barrier((pair, back))
        if pair:
            lifts = [(i, i + 1) for i in range(sums)]
            drops = [(i, i - 1) for i in range(groups - sums, groups)]
            if len(pair) == 1:
                sent = lax.ppermute(pair[0], "dp", lifts + drops)
                rising = jnp.where(upper, 0, sent)
                falling = jnp.where(upper, sent, 0)
            else:
                rising = lax.ppermute(pair[0], "dp", lifts)
                falling = lax.ppermute(pair[1], "dp", drops)
    summed = block(z).astype(jnp.float32) + rising.astype(jnp.float32) + falling.astype(jnp.float32)
    return early, back, below, above, both, summed


def local(tokens, grad_out, expert_ids, gates, gate_weight, up_weight, down_weight):
    experts = lax.axis_size("expert")
    groups = lax.axis_size("dp")
    tok_count, top_k = expert_ids.shape
    model_width = tokens.shape[1]
    capacity = 3 * tok_count * top_k // (2 * experts)
    parts = [experts * len(own) for own in chunk_ranks(capacity)]
    expert_at, spread = slot_tables(experts, capacity)
    z = lax.axis_index("dp")

    def exchange(rows):
        return lax.all_to_all(
            rows.reshape(experts, -1, rows.shape[1]),
            "expert",
            split_axis=0,
            concat_axis=0,
            tiled=True,
        ).reshape(rows.shape)

    place, slices, *send = route(expert_ids, gates, tokens, grad_out, spread, groups)

    received = [lax.dynamic_index_in_dim(slices, z, 0, keepdims=False)]
    for shift in range(1, groups):
        mine = lax.dynamic_index_in_dim(slices, lax.rem(z + shift, groups), 0, keepdims=False)
        ring = [(i, (i + shift) % groups) for i in range(groups)]
        received.append(lax.ppermute(mine, "dp", ring))

    rows, hiddens, grads, tails, gathered, backs = [], [], [], [], [], []
    for c in range(CHUNKS):
        if c == 1:
            send[c], received = lax.optimization_barrier((send[c], received))
        rows.append(exchange(send[c]))
        if c == 0:
            send_slices = place_slices(received, top_k, spread, parts)
        if CHUNKS == 1:
            rows[c], send_slices = lax.optimization_barrier((rows[c], send_slices))
        else:
            rows[c], backs[-1] = lax.optimization_barrier((rows[c], backs[-1]))
        hidden, grad, tail = expert_rows(rows[c], gate_weight, up_weight, down_weight)
        hiddens.append(hidden)
        grads.append(grad)
        tails.append(tail)
        if c < CHUNKS - 1:
            gathered.append(lax.all_gather(grad, "dp"))
        backs.append(back_rows(grad, tails, send_slices[c], gate_weight, up_weight, backs))
    down_partial = down_rows(hiddens, rows)
    back = exchange(backs[-1])

    gathered, back, below, above, both, grad_down_w = exchange_groups(
        grads[-1], down_partial, groups, gathered, back
    )
    terms = [(back, c, s, each) for c, each in enumerate(gathered) for s in range(groups)]
    for s in range(len(below)):
        terms.append((back, CHUNKS - 1, s, below[s]))
        if s:
            terms.append((back, CHUNKS - 1, groups - s, above[s]))
    if both is not None:
        terms.append((back, CHUNKS - 1, None, both))
    grad_w = weight_rows(terms, model_width, groups)

    grad_tokens, scaled, done = 0.0, [], 0
    for c, part in enumerate(parts):
        at = slice(done, done + part)
        done = at.stop
        first = 2 * c * model_width
        grad_tokens += contract_rows(place[at], back[:, first : first + model_width])
        first = 2 * CHUNKS * model_width + c * LANES
        pair = back[:, first : first + 2].astype(jnp.float32)
        scaled.append(pair[:, 0] + pair[:, 1])
    grad_tokens = grad_tokens.astype(jnp.bfloat16)
    scaled = jnp.concatenate(scaled)[:, None]
    gate_b = gates.T.astype(jnp.bfloat16).astype(jnp.float32)
    grad_gates = []
    for k in range(top_k):
        hit = (expert_ids[:, k][None, :] == expert_at[:, None]) & (place > 0)
        grad_gates.append(jnp.sum(jnp.where(hit, scaled, 0.0), axis=0) / gate_b[k])
    grad_gates = jnp.stack(grad_gates).astype(jnp.bfloat16).T

    return (grad_tokens, grad_gates, *grad_w, grad_down_w[None])


def solution(mesh):
    placed = (
        P(("dp", "expert"), None),
        P(("dp", "expert"), None),
        P(("dp", "expert"), None),
        P(("dp", "expert"), None),
        P("expert", None, None),
        P("expert", None, None),
        P("expert", None, None),
    )
    return jax.shard_map(
        local,
        mesh=mesh,
        in_specs=placed,
        out_specs=(
            P(("dp", "expert"), None),
            P(("dp", "expert"), None),
            P("expert", "dp", None),
            P("expert", "dp", None),
            P("expert", "dp", None),
        ),
        check_vma=False,
    )
```
